128 devices in a mesh: dp: 32 (over y, x_hi, z), seq: 4 (over x_lo, core).
Axes of the slice: x: 4 (x_hi: 2, x_lo: 2; x = x_hi * 2 + x_lo), y: 4, z: 4, core: 2. Of those that a mesh axis runs over, the one named last changes fastest.
Arguments:
- tokens: bfloat16 [32, 512, 512], P('dp', 'seq'), may hold values from -6 to 6
- cotangent: bfloat16 [32, 512, 512], P('dp', 'seq'), may hold values from -6 to 6
- segments: int32 [32, 512], P('dp', 'seq'), may hold values from 0 to 2, as said below
- w_attn: float32 [2, 512, 2048], P(None, ('dp', 'seq')), may hold values from -1.06066017 to 1.06066017
- w_mlp: float32 [2, 512, 4096], P(None, ('dp', 'seq')), may hold values from -0.26516504 to 0.26516504
- vectors: float32 [2, 12, 512], P(None, None, ('dp', 'seq')), may hold values from -1.2 to 1.5
- m_attn: float32 [2, 512, 2048], P(None, ('dp', 'seq')), may hold values from -16 to 16
- m_mlp: float32 [2, 512, 4096], P(None, ('dp', 'seq')), may hold values from -16 to 16
- m_vec: float32 [2, 12, 512], P(None, None, ('dp', 'seq')), may hold values from -16 to 16
- v_attn: float32 [2, 512, 2048], P(None, ('dp', 'seq')), may hold values from 0.049152 to 4.9152
- v_mlp: float32 [2, 512, 4096], P(None, ('dp', 'seq')), may hold values from 0.049152 to 4.9152
- v_vec: float32 [2, 12, 512], P(None, None, ('dp', 'seq')), may hold values from 0.049152 to 4.9152
Outputs:
- block_out: bfloat16 [32, 512, 512], P('dp', 'seq')
- input_grad: float32 [32, 512, 512], P('dp', 'seq')
- attn_first: float32 [2, 512, 2048], P(None, ('dp', 'seq'))
- attn_second: float32 [2, 512, 2048], P(None, ('dp', 'seq'))
- attn_new: float32 [2, 512, 2048], P(None, ('dp', 'seq'))
- mlp_first: float32 [2, 512, 4096], P(None, ('dp', 'seq'))
- mlp_second: float32 [2, 512, 4096], P(None, ('dp', 'seq'))
- mlp_new: float32 [2, 512, 4096], P(None, ('dp', 'seq'))
- vec_first: float32 [2, 12, 512], P(None, None, ('dp', 'seq'))
- vec_second: float32 [2, 12, 512], P(None, None, ('dp', 'seq'))
- vec_new: float32 [2, 12, 512], P(None, None, ('dp', 'seq'))
The draws below stay inside these ranges and needn't reach their ends.
Inputs may be any that keep to these rules, and one draw needn't show every extreme that they name: `segments`: each sequence holds exactly three documents numbered 0, 1, 2 in order of position; document 1 covers more than three quarters of the sequence.
All inputs are finite; a program needn't handle non-finite values.
Results may differ from the reference program's by a relative error of at most 0.04.
Values may be sent and summed in bfloat16 or wider, within the bound.
A program may use at most 192 MiB of HBM per device.

```python
import math
import jax
import jax.numpy as jnp
from jax import lax

D = 512
HEADS = 8
HD = 64
FF = 2048
LAYERS = 2
LEN = 512
STEP = 10
SEQS = 32
TOKENS = 16384
NVEC = 12


def spread_columns(base, limit, scale_low, scale_high):
    columns = lax.broadcasted_iota(jnp.int32, base.shape, base.ndim - 1)
    return base * jnp.where(columns < limit, scale_low, scale_high)


def draw_segments(key, part):
    key = jax.random.fold_in(key, 11)
    key_start, key_end = jax.random.split(key)
    edge = LEN // 8
    first_end = jax.random.randint(key_start, (SEQS, 1), 1, edge)
    last_start = jax.random.randint(key_end, (SEQS, 1), LEN - edge, LEN)
    position = lax.broadcasted_iota(jnp.int32, (SEQS, LEN), 1)
    return (position >= first_end).astype(jnp.int32) + (position >= last_start).astype(jnp.int32)


def draw_w_attn(key, part):
    key = jax.random.fold_in(key, 21)
    shape = (LAYERS, D, 4 * D)
    base = jnp.clip(jax.random.normal(key, shape, jnp.float32), -6.0, 6.0)
    return spread_columns(base, 3 * D, D ** (-0.5), 4.0 * D ** (-0.5))


def draw_w_mlp(key, part):
    key = jax.random.fold_in(key, 22)
    shape = (LAYERS, D, 2 * FF)
    base = jnp.clip(jax.random.normal(key, shape, jnp.float32), -6.0, 6.0)
    return spread_columns(base, FF, D ** (-0.5), FF ** (-0.5))


def draw_vectors(key, part):
    key = jax.random.fold_in(key, 23)
    key_bias, key_gain = jax.random.split(key)
    shape = (LAYERS, NVEC, D)
    biases = 0.2 * jnp.clip(jax.random.normal(key_bias, shape, jnp.float32), -6.0, 6.0)
    gains = 1.0 + jax.random.uniform(key_gain, shape, jnp.float32, -0.4, 0.4)
    row_index = lax.broadcasted_iota(jnp.int32, shape, 1)
    gain_rows = (row_index == 3) | (row_index == NVEC - 2)
    return jnp.where(gain_rows, gains, biases)


def block_scale(rng, dims, pieces, low, largest):
    level, own = 1.0, jax.random.fold_in(rng, 6)
    for axis_at, shards_of in pieces:
        steps = jnp.exp(jax.random.uniform(jax.random.fold_in(own, axis_at), (shards_of,), jnp.float32, low / len(pieces), largest / len(pieces)))
        level = level * jnp.repeat(steps, dims[axis_at] // shards_of).reshape([-1 if axis == axis_at else 1 for axis in range(len(dims))])
    return level


def centred(own_key, dims, scale, reach, cuts=(), held_as=jnp.bfloat16):
    entries = jax.random.normal(own_key, dims, jnp.float32) * scale
    if len(cuts) > 0:
        entries = block_scale(own_key, dims, cuts, -0.22, 0.18) * entries
    return jnp.clip(entries, min=-reach, max=reach).astype(held_as)


def setup_inputs(seed: int = 0) -> dict:
    splits = jax.random.split(jax.random.key(seed), 13)
    return {
        "tokens": centred(splits[0], (SEQS, LEN, D), 1.0, 6.0, ((0, 32), (1, 4))),
        "cotangent": centred(splits[1], (SEQS, LEN, D), 1.0, 6.0, ((0, 32), (1, 4))),
        "segments": draw_segments(jax.random.fold_in(splits[12], 71), 0),
        "w_attn": draw_w_attn(jax.random.fold_in(splits[12], 71), 0),
        "w_mlp": draw_w_mlp(jax.random.fold_in(splits[12], 71), 0),
        "vectors": draw_vectors(jax.random.fold_in(splits[12], 71), 0),
        "m_attn": centred(splits[6], (LAYERS, D, 4 * D), (0.02 * TOKENS ** 0.5), 16.0, ((1, 128),), jnp.float32),
        "m_mlp": centred(splits[7], (LAYERS, D, 2 * FF), (0.02 * TOKENS ** 0.5), 16.0, ((1, 128),), jnp.float32),
        "m_vec": centred(splits[8], (LAYERS, NVEC, D), (0.02 * TOKENS ** 0.5), 16.0, ((2, 128),), jnp.float32),
        "v_attn": jnp.clip(jnp.exp(math.log(4.9152) - 4.6051702 * jax.random.uniform(splits[9], (LAYERS, D, 4 * D), jnp.float32) ** block_scale(splits[9], (LAYERS, D, 4 * D), ((1, 128),), -0.2, 0.2)), 0.049152, 4.9152),
        "v_mlp": jnp.clip(jnp.exp(math.log(4.9152) - 4.6051702 * jax.random.uniform(splits[10], (LAYERS, D, 2 * FF), jnp.float32) ** block_scale(splits[10], (LAYERS, D, 2 * FF), ((1, 128),), -0.2, 0.2)), 0.049152, 4.9152),
        "v_vec": jnp.clip(jnp.exp(math.log(4.9152) - 4.6051702 * jax.random.uniform(splits[11], (LAYERS, NVEC, D), jnp.float32) ** block_scale(splits[11], (LAYERS, NVEC, D), ((2, 128),), -0.2, 0.2)), 0.049152, 4.9152),
    }


@jax.custom_vjp
def low(v):
    return lax.optimization_barrier(v.astype(jnp.bfloat16)).astype(jnp.float32)

@jax.custom_vjp
def low_back(v):
    return v

def low_keep(v):
    return (low(v), None)

def low_pass(kept, grad):
    return (grad,)

def back_keep(v):
    return (v, None)

def back_low(kept, grad):
    return (low(grad),)
low.defvjp(low_keep, low_pass)
low_back.defvjp(back_keep, back_low)
NORM_EPSILON = 1e-06
ADAM_EPSILON = 1e-06
BETA_FIRST = 0.9
BETA_SECOND = 0.999
LEARN_RATE = 0.03
VECTOR_RATE = 0.2
WEIGHT_DECAY = 0.01
MASKED_SCORE = -1e+30

def round_both(values):
    return low(low_back(values))

def layer_norm(summed, gain, shift):
    center = summed - lax.optimization_barrier(jnp.mean(summed, axis=-1, keepdims=True))
    spread = lax.optimization_barrier(jnp.mean(center * center, axis=-1, keepdims=True))
    return center * lax.rsqrt(spread + NORM_EPSILON) * gain + shift

def matmul(left, right):
    return jnp.einsum('gtd,de->gte', left, right, precision=lax.Precision.HIGHEST)

def encoder_layer(hidden_in, attn_layer, mlp_layer, vec_layer, same_doc):
    inner_rows = FF // D
    projected = matmul(low(hidden_in), attn_layer[:, :3 * D])
    queries = round_both(projected[..., :D] + vec_layer[0])
    keys = round_both(projected[..., D:2 * D])
    values = round_both(projected[..., 2 * D:] + vec_layer[1])
    split_shape = hidden_in.shape[:-1] + (HEADS, HD)
    raw = jnp.einsum('gqhd,gkhd->ghqk', queries.reshape(split_shape), keys.reshape(split_shape), precision=lax.Precision.HIGHEST) * HD ** (-0.5)
    scores = jnp.where(same_doc[:, None], low_back(raw), MASKED_SCORE)
    top_score = lax.optimization_barrier(jnp.max(scores, axis=-1, keepdims=True))
    exp_scores = jnp.exp(scores - top_score)
    attn_probs = exp_scores / lax.optimization_barrier(jnp.sum(exp_scores, axis=-1, keepdims=True))
    mixed = jnp.einsum('ghqk,gkhd->gqhd', low(attn_probs), values.reshape(split_shape), precision=lax.Precision.HIGHEST).reshape(hidden_in.shape)
    attn_out = low_back(matmul(round_both(mixed), attn_layer[:, 3 * D:])) + vec_layer[2]
    normed = layer_norm(hidden_in + attn_out, vec_layer[3], vec_layer[4])
    in_bias = vec_layer[5:5 + inner_rows].reshape(FF)
    pre_act = low_back(matmul(low(normed), mlp_layer[:, :FF]) + in_bias)
    activ = low(jax.nn.gelu(pre_act, approximate=False))
    back_out = low_back(jnp.einsum('gtf,df->gtd', activ, mlp_layer[:, FF:], precision=lax.Precision.HIGHEST)) + vec_layer[5 + inner_rows]
    return layer_norm(normed + back_out, vec_layer[6 + inner_rows], vec_layer[7 + inner_rows])

def adam_update(weight, grad, first, second, rate, decay):
    first_new = BETA_FIRST * first + (1.0 - BETA_FIRST) * grad
    second_new = BETA_SECOND * second + (1.0 - BETA_SECOND) * grad * grad
    first_fix = 1.0 - BETA_FIRST ** STEP
    second_fix = 1.0 - BETA_SECOND ** STEP
    weight_new = weight - rate * (first_new / first_fix / (jnp.sqrt(second_new / second_fix) + ADAM_EPSILON) + decay * weight)
    return (first_new, second_new, weight_new)

def reference(tokens, cotangent, segments, w_attn, w_mlp, vectors, m_attn, m_mlp, m_vec, v_attn, v_mlp, v_vec):
    low_attn = low(w_attn)
    low_mlp = low(w_mlp)
    low_vec = low(vectors)
    group = math.gcd(SEQS, 4)
    blocks_in = tokens.astype(jnp.float32).reshape(SEQS // group, group, LEN, D)
    blocks_ct = cotangent.astype(jnp.float32).reshape(SEQS // group, group, LEN, D)
    blocks_seg = segments.reshape(SEQS // group, group, LEN)

    def one_block(totals, inputs):
        block_in, block_ct, block_seg = inputs
        same_doc = block_seg[:, :, None] == block_seg[:, None, :]

        def forward(hidden_in, attn_all, mlp_all, vec_all):
            for layer_index in range(LAYERS):
                hidden_in = encoder_layer(hidden_in, attn_all[layer_index], mlp_all[layer_index], vec_all[layer_index], same_doc)
            return hidden_in
        result, pullback = jax.vjp(forward, block_in, low_attn, low_mlp, low_vec)
        grad_in, grad_attn, grad_mlp, grad_vec = pullback(block_ct)
        totals = (totals[0] + grad_attn, totals[1] + grad_mlp, totals[2] + grad_vec)
        return (totals, (result.astype(jnp.bfloat16), grad_in))
    start = (jnp.zeros(w_attn.shape, jnp.float32), jnp.zeros(w_mlp.shape, jnp.float32), jnp.zeros(vectors.shape, jnp.float32))
    totals, (outputs, grads_in) = lax.scan(one_block, start, (blocks_in, blocks_ct, blocks_seg))
    block_out = outputs.reshape(SEQS, LEN, D)
    input_grad = grads_in.reshape(SEQS, LEN, D)
    attn_first, attn_second, attn_new = adam_update(w_attn, totals[0], m_attn, v_attn, LEARN_RATE, WEIGHT_DECAY)
    mlp_first, mlp_second, mlp_new = adam_update(w_mlp, totals[1], m_mlp, v_mlp, LEARN_RATE, WEIGHT_DECAY)
    vec_first, vec_second, vec_new = adam_update(vectors, totals[2], m_vec, v_vec, VECTOR_RATE, 0.0)
    return (block_out, input_grad, attn_first, attn_second, attn_new, mlp_first, mlp_second, mlp_new, vec_first, vec_second, vec_new)
```

```python
import math

import jax
import jax.numpy as jnp
from jax import lax
from jax.experimental import pallas as pl
from jax.experimental.pallas import tpu as pltpu
from jax.sharding import PartitionSpec as P

STEP = 10
NORM_EPSILON = 1e-06
ADAM_EPSILON = 1e-06
BETA_FIRST = 0.9
BETA_SECOND = 0.999
LEARN_RATE = 0.03
VECTOR_RATE = 0.2
WEIGHT_DECAY = 0.01
MASKED_SCORE = -1e30
VMEM_BYTES = 62 * 2**20
MESH = pl.DeviceIdType.MESH
BF = jnp.bfloat16
F32 = jnp.float32
THIRDS = (((0, 128), (128, 256), (256, 512)), ((0, 384), (384, 768), (768, 1024)))
WIDTHS = (512, 1024)
ORDERS = (("x", "y", "z"), ("y", "z", "x"), ("z", "x", "y"))


class Place:
    def __init__(self):
        self.dp = lax.axis_index("dp")
        self.seq = lax.axis_index("seq")
        self.core = self.seq % 2
        self.at = {
            "x": ((self.dp // 4) % 2) * 2 + self.seq // 2,
            "y": self.dp // 8,
            "z": self.dp % 4,
        }

    def device(self, at, core):
        return {
            "dp": (at["y"] * 2 + at["x"] // 2) * 4 + at["z"],
            "seq": (at["x"] % 2) * 2 + core,
        }

    def along(self, axis, step):
        at = dict(self.at)
        at[axis] = (at[axis] + step) % 4
        return at[axis], self.device(at, self.core)

    def other_core(self):
        return self.device(self.at, 1 - self.core)

    def in_group(self, step):
        peer = (self.seq + step) % 4
        return peer, {"dp": self.dp, "seq": peer}


def region(buf, layer, at, core, columns):
    whole = slice(None)
    if "x" in at:
        x_hi, x_lo = at["x"] // 2, at["x"] % 2
    else:
        x_hi, x_lo = whole, whole
    cols = pl.ds(columns[0], columns[1] - columns[0])
    return buf.at[layer, x_lo, core, at.get("y", whole), x_hi, at.get("z", whole), whole, cols]


def greet(place):
    barrier = pltpu.get_barrier_semaphore()
    peers = [place.other_core()]
    for axis in ("x", "y", "z"):
        for step in (1, 2, 3):
            peers.append(place.along(axis, step)[1])
    far = {"dp": place.dp, "seq": (1 - place.seq // 2) * 2 + (1 - place.core)}
    peers.append(far)
    for peer in peers:
        pl.semaphore_signal(barrier, inc=1, device_id=peer, device_id_type=MESH)
    pl.semaphore_wait(barrier, len(peers))


def remote(src, dst, send, recv, device):
    return pltpu.make_async_remote_copy(
        src_ref=src, dst_ref=dst, send_sem=send, recv_sem=recv, device_id=device, device_id_type=MESH
    )


def share_vectors(place, vsum, vgot, v_send, v_recv):
    for rnd, axis in enumerate(("core", "x", "y", "z")):
        steps = (1,) if axis == "core" else (1, 2, 3)
        copies = []
        for step in steps:
            device = place.other_core() if axis == "core" else place.along(axis, step)[1]
            copy = remote(vsum, vgot.at[rnd, step - 1], v_send.at[rnd, step - 1], v_recv.at[rnd, step - 1], device)
            copy.start()
            copies.append(copy)
        for copy in copies:
            copy.wait()
        total = vsum[...]
        for step in steps:
            total = total + vgot[rnd, step - 1]
        vsum[...] = total


def dims_of(axes):
    out = ()
    if "x" in axes:
        out += (2,)
    if "y" in axes:
        out += (4,)
    if "x" in axes:
        out += (2,)
    if "z" in axes:
        out += (4,)
    return out


def each_block(dims, body):
    count = 1
    for size in dims:
        count *= size

    def one(i, carry):
        index = ()
        rest = i
        for size in reversed(dims):
            index = (rest % size,) + index
            rest = rest // size
        body(index)
        return carry

    if count == 1:
        body(tuple(0 for _ in dims))
    else:
        lax.fori_loop(0, count, one, 0)


NT = (((1,), (1,)), ((), ()))
NN = (((1,), (0,)), ((), ()))
TN = (((0,), (0,)), ((), ()))
CHUNKS = ((0, 0), (0, 1), (1, 0), (1, 1))
PIECES = (16, 1536)
SCALE = 0.125


def mm(left, right, dims=NN):
    return lax.dot_general(left, right, dims, preferred_element_type=F32)


def column_sum(values):
    return jnp.sum(values, axis=0, keepdims=True)


def normalize(summed):
    center = summed - jnp.mean(summed, axis=-1, keepdims=True)
    spread = jnp.mean(center * center, axis=-1, keepdims=True)
    inverse = lax.rsqrt(spread + NORM_EPSILON)
    return center * inverse, inverse


def normalize_back(grad, hat, inverse):
    mean = jnp.mean(grad, axis=-1, keepdims=True)
    along = jnp.mean(grad * hat, axis=-1, keepdims=True)
    return inverse * (grad - mean - hat * along)


class Gather:
    def __init__(self, place, bufs, send, recv, swap_send, swap_recv):
        self.place, self.bufs = place, bufs
        self.send, self.recv, self.swap_send, self.swap_recv = send, recv, swap_send, swap_recv

    def copies(self, l, arr, phase, coming):
        place = self.place
        out = []
        for j, order in enumerate(ORDERS):
            axis = order[phase]
            here = {a: place.at[a] for a in order[phase:]}
            for step in (1, 2, 3):
                _, device = place.along(axis, step)
                spot = dict(here)
                if coming:
                    spot[axis] = (place.at[axis] - step) % 4
                ref = region(self.bufs[arr], l, spot, place.core, THIRDS[arr][j])
                sems = (self.send.at[l, arr, phase, j, step - 1], self.recv.at[l, arr, phase, j, step - 1])
                out.append(remote(ref, ref, *sems, device))
        return out

    def start(self, l, arr, phase):
        for copy in self.copies(l, arr, phase, False):
            copy.start()

    def arrive(self, l, arr, phase):
        for copy in self.copies(l, arr, phase, True):
            copy.wait_recv()

    def swap(self, l, arr):
        mine = self.bufs[arr].at[l, :, self.place.core]
        return remote(mine, mine, self.swap_send.at[l, arr], self.swap_recv.at[l, arr], self.place.other_core())

    def swap_start(self, l, arr):
        self.arrive(l, arr, 2)
        self.swap(l, arr).start()

    def swap_arrive(self, l, arr):
        theirs = self.bufs[arr].at[l, :, 1 - self.place.core]
        remote(
            theirs, theirs, self.swap_send.at[l, arr], self.swap_recv.at[l, arr], self.place.other_core()
        ).wait_recv()

    def finish(self):
        for chunk in CHUNKS:
            for phase in range(3):
                for copy in self.copies(*chunk, phase, False):
                    copy.wait_send()
            self.swap(*chunk).wait_send()


class Scatter:
    def __init__(self, place, bufs, landed, slots, total, swap_send, swap_recv, send, recv):
        self.place, self.bufs, self.landed, self.slots, self.total = place, bufs, landed, slots, total
        self.swap_send, self.swap_recv, self.send, self.recv = swap_send, swap_recv, send, recv

    def slot(self, phase, arr, j):
        return self.slots[(phase * 2 + arr) * 3 + j]

    def swap(self, l, arr):
        return remote(
            self.bufs[arr].at[l, :, 1 - self.place.core],
            self.landed[arr].at[l],
            self.swap_send.at[l, arr],
            self.swap_recv.at[l, arr],
            self.place.other_core(),
        )

    def copies(self, l, arr, phase):
        place = self.place
        out = []
        for j, order in enumerate(ORDERS):
            rev = order[::-1]
            for step in (1, 2, 3):
                there = {a: place.at[a] for a in rev[:phase]}
                there[rev[phase]], device = place.along(rev[phase], step)
                src = region(self.bufs[arr], l, there, place.core, THIRDS[arr][j])
                dst = self.slot(phase, arr, j).at[l, step - 1]
                sems = (self.send.at[l, arr, phase, j, step - 1], self.recv.at[l, arr, phase, j, step - 1])
                out.append(remote(src, dst, *sems, device))
        return out

    def add_up(self, l, arr, phase):
        for j, order in enumerate(ORDERS):
            rev = order[::-1]
            here = {a: self.place.at[a] for a in rev[: phase + 1]}
            own = region(self.bufs[arr], l, here, self.place.core, THIRDS[arr][j])
            came = self.slot(phase, arr, j)

            def body(index, own=own, came=came, j=j):
                total = own[index].astype(F32)
                for k in range(3):
                    total = total + came[(l, k) + index].astype(F32)
                if phase < 2:
                    own[index] = total.astype(BF)
                else:
                    low, high = THIRDS[arr][j]
                    self.total[l, :, 512 * arr + low : 512 * arr + high] = total

            each_block(dims_of(rev[phase + 1 :]), body)

    def begin(self, l, arr):
        self.swap(l, arr).start()

    def step(self, l, arr, stage):
        if stage == 0:
            self.swap(l, arr).wait_recv()

            def body(index):
                own = self.bufs[arr].at[(l, index[0], self.place.core) + index[1:]]
                own[...] = (own[...].astype(F32) + self.landed[arr][(l,) + index].astype(F32)).astype(BF)

            each_block((2, 4, 2, 4), body)
        else:
            for copy in self.copies(l, arr, stage - 1):
                copy.wait_recv()
            self.add_up(l, arr, stage - 1)
        if stage < 3:
            for copy in self.copies(l, arr, stage):
                copy.start()

    def finish(self):
        for chunk in CHUNKS:
            self.swap(*chunk).wait_send()
            for phase in range(3):
                for copy in self.copies(*chunk, phase):
                    copy.wait_send()


def train_kernel(*refs):
    names = NAMES
    r = dict(zip(names, refs[: len(names)]))
    slots = refs[len(names) :]
    place = Place()
    seq = place.seq
    wa, wm, ga, gm, vec, vgrad = r["wa"], r["wm"], r["ga"], r["gm"], r["vec"], r["vgrad"]
    s0, r0, stage, kv = r["s0"], r["r0"], r["stage"], r["kv"]
    unsent = []

    for q in range(4):
        for l in range(2):
            s0[q, l, :, 0:512] = r["w_attn"][l, :, 512 * q : 512 * q + 512]
            s0[q, l, :, 512:1536] = r["w_mlp"][l, :, 1024 * q : 1024 * q + 1024]
    vec[...] = r["table"][...]
    r["docs"][seq] = r["seg_row"][...]
    greet(place)

    def to_group(src, dst, send, recv):
        out = []
        for step in (1, 2, 3):
            peer, device = place.in_group(step)
            copy = remote(src(peer, step), dst(step), send.at[step], recv.at[step], device)
            copy.start()
            out.append(copy)
            unsent.append(copy)
        return out

    pieces = to_group(lambda peer, step: s0.at[peer], lambda step: r0.at[seq], r["a2a_send"].at[0], r["a2a_recv"].at[0])
    docs = to_group(lambda peer, step: r["docs"].at[seq], lambda step: r["docs"].at[seq], r["doc_send"], r["doc_recv"])
    r0[seq] = s0[seq]
    for copy in pieces:
        copy.wait_recv()
    for src in range(4):
        for l in range(2):
            stage[l, 4 * src : 4 * src + 4, :] = r0[src, l]
    at = place.at
    for l, arr in CHUNKS:
        block = stage[l, :, 512 * arr : 512 * arr + WIDTHS[arr]].astype(BF)
        (wa, wm)[arr][l, at["x"] % 2, place.core, at["y"], at["x"] // 2, at["z"]] = block
    gather = Gather(place, (wa, wm), r["ag_send"], r["ag_recv"], r["sw_send"], r["sw_recv"])
    for phase in range(3):
        for chunk in CHUNKS:
            if phase > 0:
                gather.arrive(*chunk, phase - 1)
            gather.start(*chunk, phase)
    share_vectors(place, vec, r["vgot"].at[0], r["v_send"].at[0], r["v_recv"].at[0])
    for copy in docs:
        copy.wait_recv()
    seg_row = jnp.concatenate([r["docs"][i] for i in range(4)], axis=1)
    r["bias"][...] = jnp.where(r["seg_col"][...] == seg_row, 0.0, MASKED_SCORE)
    gather.swap_start(0, 0)
    gather.swap_arrive(0, 0)

    def weight(l, arr, q, low=0, high=None):
        return (wa, wm)[arr][l, q // 2, q % 2, :, :, :, :, low : WIDTHS[arr] if high is None else high].reshape(
            512, (WIDTHS[arr] if high is None else high) - low
        )

    def put_grad(l, arr, q, low, value):
        width = value.shape[1]
        (ga, gm)[arr][l, q // 2, q % 2, :, :, :, :, low : low + width] = value.astype(BF).reshape(4, 2, 4, 16, width)

    def row(l, k):
        return vec[12 * l + k : 12 * l + k + 1, :]

    def put_row(l, k, value):
        vgrad[12 * l + k : 12 * l + k + 1, :] = value

    lanes = lax.broadcasted_iota(jnp.int32, (1, 128), 1)
    first = (lanes < 64).astype(F32)
    second = 1.0 - first
    first_low, second_low = first.astype(BF), second.astype(BF)

    def both(pair):
        return jnp.concatenate([pair * first_low, pair * second_low], axis=0)

    def joined(stacked):
        return stacked[:128] * first + stacked[128:] * second

    def group_rows(ref, l, which, low):
        return ref[l, :, which, :, low : low + 128].reshape(512, 128)

    hidden = r["tokens"][...].astype(F32)
    for l in range(2):
        if l == 1:
            gather.swap_arrive(1, 0)
        low_in = hidden.astype(BF)
        r["x"][l] = low_in
        kv[l, seq, 0] = mm(low_in, weight(l, 0, 1)).astype(BF)
        kv[l, seq, 1] = (mm(low_in, weight(l, 0, 2)) + row(l, 1)).astype(BF)
        moved = to_group(
            lambda peer, step: kv.at[l, seq], lambda step: kv.at[l, seq], r["kv_send"].at[l], r["kv_recv"].at[l]
        )
        r["q"][l] = (mm(low_in, weight(l, 0, 0)) + row(l, 0)).astype(BF)
        if l == 0:
            gather.swap_start(0, 1)
        for copy in moved:
            copy.wait_recv()
        for pair in range(4):
            low = 128 * pair
            keys, values = group_rows(kv, l, 0, low), group_rows(kv, l, 1, low)
            scores = mm(both(r["q"][l, :, low : low + 128]), keys, NT) * SCALE
            bias = r["bias"][...]
            scores = scores + jnp.concatenate([bias, bias], axis=0)
            powers = jnp.exp(scores - jnp.max(scores, axis=-1, keepdims=True))
            probs = (powers * (1.0 / jnp.sum(powers, axis=-1, keepdims=True))).astype(BF)
            r["probs"][l, pair] = probs
            r["o"][l, :, low : low + 128] = joined(mm(probs, values)).astype(BF)
        if l == 0:
            gather.swap_arrive(0, 1)
            gather.swap_start(1, 0)
        else:
            gather.swap_arrive(1, 1)
        hat, inverse = normalize(hidden + mm(r["o"][l], weight(l, 0, 3)) + row(l, 2))
        r["hat1"][l] = hat
        r["inv1"][l] = inverse
        normed = hat * row(l, 3) + row(l, 4)
        low_normed = normed.astype(BF)
        r["n1"][l] = low_normed
        back = jnp.zeros((128, 512), F32)
        for i in range(4):
            low = 512 * (i % 2)
            pre = mm(low_normed, weight(l, 1, i // 2, low, low + 512)) + row(l, 5 + i)
            normal = 0.5 + 0.5 * lax.erf(pre * (0.5**0.5))
            act = (pre * normal).astype(BF)
            r["act"][l, :, 512 * i : 512 * i + 512] = act
            slope = normal + pre * (jnp.exp(pre * pre * -0.5) * (1.0 / (2.0 * math.pi) ** 0.5))
            r["slope"][l, :, 512 * i : 512 * i + 512] = slope.astype(BF)
            back = back + mm(act, weight(l, 1, 2 + i // 2, low, low + 512), NT)
            if l == 0 and i == 1:
                gather.swap_start(1, 1)
        hat, inverse = normalize(normed + back + row(l, 9))
        r["hat2"][l] = hat
        r["inv2"][l] = inverse
        hidden = hat * row(l, 10) + row(l, 11)
    r["block_out"][...] = hidden.astype(BF)

    scatter = Scatter(
        place, (ga, gm), (r["r0a"], r["r0m"]), slots, r["total"], r["gs_send"], r["gs_recv"], r["rs_send"], r["rs_recv"]
    )
    grad = r["cotangent"][...].astype(F32)
    for l in (1, 0):
        hat = r["hat2"][l]
        put_row(l, 10, column_sum(grad * hat))
        put_row(l, 11, column_sum(grad))
        grad_second = normalize_back(grad * row(l, 10), hat, r["inv2"][l])
        put_row(l, 9, column_sum(grad_second))
        low_second = grad_second.astype(BF)
        grad_normed = grad_second
        for i in range(4):
            low = 512 * (i % 2)
            span = slice(512 * i, 512 * i + 512)
            grad_act = mm(low_second, weight(l, 1, 2 + i // 2, low, low + 512))
            grad_pre = (grad_act * r["slope"][l, :, span].astype(F32)).astype(BF)
            put_row(l, 5 + i, column_sum(grad_pre.astype(F32)))
            put_grad(l, 1, 2 + i // 2, low, mm(low_second, r["act"][l, :, span], TN))
            put_grad(l, 1, i // 2, low, mm(r["n1"][l], grad_pre, TN))
            grad_normed = grad_normed + mm(grad_pre, weight(l, 1, i // 2, low, low + 512), NT)
            if l == 0 and i == 0:
                scatter.step(1, 1, 1)
                scatter.step(1, 0, 0)
            if l == 0 and i == 2:
                scatter.step(1, 1, 2)
                scatter.step(1, 0, 1)
        scatter.begin(l, 1)
        hat = r["hat1"][l]
        put_row(l, 3, column_sum(grad_normed * hat))
        put_row(l, 4, column_sum(grad_normed))
        grad_first = normalize_back(grad_normed * row(l, 3), hat, r["inv1"][l])
        put_row(l, 2, column_sum(grad_first))
        low_first = grad_first.astype(BF)
        put_grad(l, 0, 3, 0, mm(r["o"][l], low_first, TN))
        grad_mixed = mm(low_first, weight(l, 0, 3), NT).astype(BF)
        dkv_out, dkv_in = r["dkv_out"], r["dkv_in"]
        for pair in range(4):
            low = 128 * pair
            keys, values = group_rows(kv, l, 0, low), group_rows(kv, l, 1, low)
            grad_pair = both(grad_mixed[:, low : low + 128])
            probs = r["probs"][l, pair]
            grad_probs = mm(grad_pair, values, NT)
            dkv_out[l, :, 1, :, low : low + 128] = mm(probs, grad_pair, TN).astype(BF).reshape(4, 128, 128)
            wide = probs.astype(F32)
            row_dot = jnp.sum(grad_probs * wide, axis=-1, keepdims=True)
            grad_scores = (wide * (grad_probs - row_dot)).astype(BF)
            r["dq"][:, low : low + 128] = (joined(mm(grad_scores, keys)) * SCALE).astype(BF)
            grad_keys = mm(grad_scores, both(r["q"][l, :, low : low + 128]), TN) * SCALE
            dkv_out[l, :, 0, :, low : low + 128] = grad_keys.astype(BF).reshape(4, 128, 128)
        moved = to_group(
            lambda peer, step: dkv_out.at[l, peer],
            lambda step: dkv_in.at[l, step - 1],
            r["dkv_send"].at[l],
            r["dkv_recv"].at[l],
        )
        low_in = r["x"][l]
        grad_queries = r["dq"][...]
        put_row(l, 0, column_sum(grad_queries.astype(F32)))
        put_grad(l, 0, 0, 0, mm(low_in, grad_queries, TN))
        grad = grad_first + mm(grad_queries, weight(l, 0, 0), NT)
        if l == 0:
            scatter.step(1, 1, 3)
            scatter.step(1, 0, 2)
        scatter.step(l, 1, 0)
        for copy in moved:
            copy.wait_recv()
        for which in range(2):
            total = dkv_out[l, seq, which].astype(F32)
            for k in range(3):
                total = total + dkv_in[l, k, which].astype(F32)
            low_total = total.astype(BF)
            if which == 1:
                put_row(l, 1, column_sum(low_total.astype(F32)))
            put_grad(l, 0, 1 + which, 0, mm(low_in, low_total, TN))
            grad = grad + mm(low_total, weight(l, 0, 1 + which), NT)
        scatter.begin(l, 0)
    r["input_grad"][...] = grad
    scatter.step(1, 0, 3)
    scatter.step(0, 1, 1)
    scatter.step(0, 0, 0)
    share_vectors(place, vgrad, r["vgot"].at[1], r["v_send"].at[1], r["v_recv"].at[1])
    scatter.step(0, 1, 2)
    scatter.step(0, 0, 1)
    scatter.step(0, 1, 3)
    scatter.step(0, 0, 2)
    scatter.step(0, 0, 3)
    s4, fin, total = r["s4"], r["fin"], r["total"]
    for dst in range(4):
        for l in range(2):
            s4[dst, l] = total[l, 4 * dst : 4 * dst + 4, :]
    moved = to_group(lambda peer, step: s4.at[peer], lambda step: fin.at[seq], r["a2a_send"].at[1], r["a2a_recv"].at[1])
    fin[seq] = s4[seq]
    gather.finish()
    scatter.finish()
    for copy in moved:
        copy.wait_recv()
    for copy in unsent:
        copy.wait_send()


INPUTS = ("tokens", "cotangent", "seg_row", "seg_col", "w_attn", "w_mlp", "table")
OUTPUTS = {
    "block_out": ((128, 512), BF),
    "input_grad": ((128, 512), F32),
    "fin": ((4, 2, 4, 1536), F32),
    "vgrad": ((24, 512), F32),
}
DIMS = (2, 2, 2, 4, 2, 4, 16)
HALF = (2, 2, 4, 2, 4, 16)
SCRATCH = {
    "wa": (DIMS + (512,), BF),
    "wm": (DIMS + (1024,), BF),
    "ga": (DIMS + (512,), BF),
    "gm": (DIMS + (1024,), BF),
    "r0a": (HALF + (512,), BF),
    "r0m": (HALF + (1024,), BF),
    "vec": ((24, 512), F32),
    "s0": ((4, 2, 4, 1536), F32),
    "r0": ((4, 2, 4, 1536), F32),
    "s4": ((4, 2, 4, 1536), F32),
    "stage": ((2, 16, 1536), F32),
    "total": ((2, 16, 1536), F32),
    "vgot": ((2, 4, 3, 24, 512), F32),
    "docs": ((4, 1, 128), jnp.int32),
    "bias": ((128, 512), F32),
    "x": ((2, 128, 512), BF),
    "q": ((2, 128, 512), BF),
    "kv": ((2, 4, 2, 128, 512), BF),
    "probs": ((2, 4, 256, 512), BF),
    "o": ((2, 128, 512), BF),
    "hat1": ((2, 128, 512), F32),
    "inv1": ((2, 128, 1), F32),
    "n1": ((2, 128, 512), BF),
    "act": ((2, 128, 2048), BF),
    "slope": ((2, 128, 2048), BF),
    "hat2": ((2, 128, 512), F32),
    "inv2": ((2, 128, 1), F32),
    "dq": ((128, 512), BF),
    "dkv_out": ((2, 4, 2, 128, 512), BF),
    "dkv_in": ((2, 3, 2, 128, 512), BF),
}
SEMS = {
    "a2a": (2, 4),
    "doc": (4,),
    "ag": (2, 2, 3, 3, 3),
    "sw": (2, 2),
    "gs": (2, 2),
    "rs": (2, 2, 3, 3, 3),
    "kv": (2, 4),
    "dkv": (2, 4),
    "v": (2, 4, 3),
}
NAMES = INPUTS + tuple(OUTPUTS) + tuple(SCRATCH) + tuple(f"{n}_{d}" for n in SEMS for d in ("send", "recv"))


def train(*args):
    slots = []
    for phase in range(3):
        for arr in range(2):
            for j in range(3):
                low, high = THIRDS[arr][j]
                rest = dims_of(ORDERS[j][::-1][phase + 1 :])
                slots.append(pltpu.VMEM((2, 3) + rest + (16, high - low), BF))
    scratch = [pltpu.VMEM(*spec) for spec in SCRATCH.values()]
    for shape in SEMS.values():
        scratch += [pltpu.SemaphoreType.DMA(shape)] * 2
    return pl.pallas_call(
        train_kernel,
        out_shape=tuple(jax.ShapeDtypeStruct(*spec) for spec in OUTPUTS.values()),
        in_specs=[pl.BlockSpec(memory_space=pltpu.VMEM)] * len(INPUTS),
        out_specs=[pl.BlockSpec(memory_space=pltpu.VMEM)] * len(OUTPUTS),
        scratch_shapes=scratch + slots,
        compiler_params=pltpu.CompilerParams(
            collective_id=0, has_side_effects=True, vmem_limit_bytes=VMEM_BYTES
        ),
        name="train",
    )(*args)


def adam_update(weight, grad, first, second, rate, decay):
    first_new = BETA_FIRST * first + (1.0 - BETA_FIRST) * grad
    second_new = BETA_SECOND * second + (1.0 - BETA_SECOND) * grad * grad
    first_fix = 1.0 - BETA_FIRST**STEP
    second_fix = 1.0 - BETA_SECOND**STEP
    weight_new = weight - rate * (
        first_new / first_fix / (jnp.sqrt(second_new / second_fix) + ADAM_EPSILON) + decay * weight
    )
    return (first_new, second_new, weight_new)


def local(
    tokens, cotangent, segments, w_attn, w_mlp, vectors, m_attn, m_mlp, m_vec, v_attn, v_mlp, v_vec
):
    place = lax.axis_index("dp") * 4 + lax.axis_index("seq")
    table = lax.dynamic_update_slice(
        jnp.zeros((24, 512), F32),
        vectors.astype(BF).astype(F32).reshape(24, 4),
        (0, 4 * place),
    )
    block_out, input_grad, fin, vec_total = train(
        tokens[0], cotangent[0], segments, segments.reshape(128, 1), w_attn, w_mlp, table
    )
    grad_attn = fin[..., :512].transpose(1, 2, 0, 3).reshape(2, 4, 2048)
    grad_mlp = fin[..., 512:].transpose(1, 2, 0, 3).reshape(2, 4, 4096)
    grad_vec = lax.dynamic_slice(vec_total, (0, 4 * place), (24, 4)).reshape(2, 12, 4)
    return (
        block_out[None],
        input_grad[None],
        *adam_update(w_attn, grad_attn, m_attn, v_attn, LEARN_RATE, WEIGHT_DECAY),
        *adam_update(w_mlp, grad_mlp, m_mlp, v_mlp, LEARN_RATE, WEIGHT_DECAY),
        *adam_update(vectors, grad_vec, m_vec, v_vec, VECTOR_RATE, 0.0),
    )


def solution(mesh):
    in_specs = (
        P("dp", "seq", None),
        P("dp", "seq", None),
        P("dp", "seq"),
        P(None, ("dp", "seq"), None),
        P(None, ("dp", "seq"), None),
        P(None, None, ("dp", "seq")),
        P(None, ("dp", "seq"), None),
        P(None, ("dp", "seq"), None),
        P(None, None, ("dp", "seq")),
        P(None, ("dp", "seq"), None),
        P(None, ("dp", "seq"), None),
        P(None, None, ("dp", "seq")),
    )
    out_specs = (
        P("dp", "seq", None),
        P("dp", "seq", None),
        P(None, ("dp", "seq"), None),
        P(None, ("dp", "seq"), None),
        P(None, ("dp", "seq"), None),
        P(None, ("dp", "seq"), None),
        P(None, ("dp", "seq"), None),
        P(None, ("dp", "seq"), None),
        P(None, None, ("dp", "seq")),
        P(None, None, ("dp", "seq")),
        P(None, None, ("dp", "seq")),
    )
    return jax.shard_map(local, mesh=mesh, in_specs=in_specs, out_specs=out_specs, check_vma=False)
```

```python
import math

import jax
import jax.numpy as jnp
from jax import lax
from jax.experimental import pallas as pl
from jax.experimental.pallas import tpu as pltpu
from jax.sharding import PartitionSpec as P

STEP = 10
NORM_EPSILON = 1e-06
ADAM_EPSILON = 1e-06
BETA_FIRST = 0.9
BETA_SECOND = 0.999
LEARN_RATE = 0.03
VECTOR_RATE = 0.2
WEIGHT_DECAY = 0.01
MASKED_SCORE = -1e30
VMEM_BYTES = 62 * 2**20
MESH = pl.DeviceIdType.MESH
BF = jnp.bfloat16
F32 = jnp.float32
THIRDS = (((0, 128), (128, 256), (256, 512)), ((0, 384), (384, 768), (768, 1024)))
WIDTHS = (512, 1024)
ORDERS = (("x", "y", "z"), ("y", "z", "x"), ("z", "x", "y"))


class Place:
    def __init__(self):
        self.dp = lax.axis_index("dp")
        self.seq = lax.axis_index("seq")
        self.core = self.seq % 2
        self.at = {
            "x": ((self.dp // 4) % 2) * 2 + self.seq // 2,
            "y": self.dp // 8,
            "z": self.dp % 4,
        }

    def device(self, at, core):
        return {
            "dp": (at["y"] * 2 + at["x"] // 2) * 4 + at["z"],
            "seq": (at["x"] % 2) * 2 + core,
        }

    def along(self, axis, step):
        at = dict(self.at)
        at[axis] = (at[axis] + step) % 4
        return at[axis], self.device(at, self.core)

    def other_core(self):
        return self.device(self.at, 1 - self.core)

    def in_group(self, step):
        peer = (self.seq + step) % 4
        return peer, {"dp": self.dp, "seq": peer}


def region(buf, layer, at, core, columns):
    whole = slice(None)
    if "x" in at:
        x_hi, x_lo = at["x"] // 2, at["x"] % 2
    else:
        x_hi, x_lo = whole, whole
    cols = pl.ds(columns[0], columns[1] - columns[0])
    return buf.at[layer, x_lo, core, at.get("y", whole), x_hi, at.get("z", whole), whole, cols]


def greet(place):
    barrier = pltpu.get_barrier_semaphore()
    peers = [place.other_core()]
    for axis in ("x", "y", "z"):
        for step in (1, 2, 3):
            peers.append(place.along(axis, step)[1])
    far = {"dp": place.dp, "seq": (1 - place.seq // 2) * 2 + (1 - place.core)}
    peers.append(far)
    for peer in peers:
        pl.semaphore_signal(barrier, inc=1, device_id=peer, device_id_type=MESH)
    pl.semaphore_wait(barrier, len(peers))


def remote(src, dst, send, recv, device):
    return pltpu.make_async_remote_copy(
        src_ref=src, dst_ref=dst, send_sem=send, recv_sem=recv, device_id=device, device_id_type=MESH
    )


class Table:
    ROUNDS = (("core", (1,)), ("x", (1, 2, 3)), ("y", (1, 2, 3)), ("z", (1, 2, 3)))

    def __init__(self, place, total, came, send, recv):
        self.place, self.total, self.came, self.send, self.recv = place, total, came, send, recv
        self.going = None

    def start(self, number):
        axis, steps = self.ROUNDS[number]
        self.going = []
        for step in steps:
            device = self.place.other_core() if axis == "core" else self.place.along(axis, step)[1]
            copy = remote(
                self.total,
                self.came.at[number, step - 1],
                self.send.at[number, step - 1],
                self.recv.at[number, step - 1],
                device,
            )
            copy.start()
            self.going.append(copy)

    def finish(self, number):
        for copy in self.going:
            copy.wait()
        total = self.total[...]
        for step in self.ROUNDS[number][1]:
            total = total + self.came[number, step - 1]
        self.total[...] = total


def dims_of(axes):
    out = ()
    if "x" in axes:
        out += (2,)
    if "y" in axes:
        out += (4,)
    if "x" in axes:
        out += (2,)
    if "z" in axes:
        out += (4,)
    return out


def each_block(dims, body):
    count = 1
    for size in dims[:-1]:
        count *= size

    def one(i, carry):
        index = ()
        rest = i
        for size in reversed(dims[:-1]):
            index = (rest % size,) + index
            rest = rest // size
        body(index)
        return carry

    if count == 1:
        body(tuple(0 for _ in dims[:-1]))
    else:
        lax.fori_loop(0, count, one, 0)


NT = (((1,), (1,)), ((), ()))
NN = (((1,), (0,)), ((), ()))
TN = (((0,), (0,)), ((), ()))
CHUNKS = ((0, 0), (0, 1), (1, 0), (1, 1))
PIECES = (16, 1536)
SCALE = 0.125
QUARTERS = (0, 3, 1, 2)


def mm(left, right, dims=NN):
    return lax.dot_general(left, right, dims, preferred_element_type=F32)


def column_sum(values):
    return jnp.sum(values, axis=0, keepdims=True)


def normalize(summed):
    center = summed - jnp.mean(summed, axis=-1, keepdims=True)
    spread = jnp.mean(center * center, axis=-1, keepdims=True)
    inverse = lax.rsqrt(spread + NORM_EPSILON)
    return center * inverse, inverse


def normalize_back(grad, hat, inverse):
    mean = jnp.mean(grad, axis=-1, keepdims=True)
    along = jnp.mean(grad * hat, axis=-1, keepdims=True)
    return inverse * (grad - mean - hat * along)


class Gather:
    def __init__(self, place, bufs, send, recv, swap_send, swap_recv):
        self.place, self.bufs = place, bufs
        self.send, self.recv, self.swap_send, self.swap_recv = send, recv, swap_send, swap_recv

    def copies(self, l, arr, phase, coming):
        place = self.place
        out = []
        for j, order in enumerate(ORDERS):
            axis = order[phase]
            here = {a: place.at[a] for a in order[phase:]}
            for step in (1, 2, 3):
                _, device = place.along(axis, step)
                spot = dict(here)
                if coming:
                    spot[axis] = (place.at[axis] - step) % 4
                ref = region(self.bufs[arr], l, spot, place.core, THIRDS[arr][j])
                sems = (self.send.at[l, arr, phase, j, step - 1], self.recv.at[l, arr, phase, j, step - 1])
                out.append(remote(ref, ref, *sems, device))
        return out

    def start(self, l, arr, phase):
        for copy in self.copies(l, arr, phase, False):
            copy.start()
        if phase == 2:
            for j in range(3):
                self.swap(l, arr, j, 0).start()

    def arrive(self, l, arr, phase):
        for copy in self.copies(l, arr, phase, True):
            copy.wait_recv()

    def swap(self, l, arr, j, step, coming=False):
        place = self.place
        axis = ORDERS[j][2]
        core = 1 - place.core if coming else place.core
        ref = region(self.bufs[arr], l, {axis: (place.at[axis] - step) % 4}, core, THIRDS[arr][j])
        return remote(
            ref, ref, self.swap_send.at[l, arr, j, step], self.swap_recv.at[l, arr, j, step], place.other_core()
        )

    def swap_start(self, l, arr):
        copies = self.copies(l, arr, 2, True)
        for step in (1, 3, 2):
            for j in range(3):
                copies[3 * j + step - 1].wait_recv()
                self.swap(l, arr, j, step).start()

    def swap_arrive(self, l, arr):
        for j in range(3):
            for step in range(4):
                self.swap(l, arr, j, step, True).wait_recv()

    def finish(self):
        for chunk in CHUNKS:
            for phase in range(3):
                for copy in self.copies(*chunk, phase, False):
                    copy.wait_send()
            for j in range(3):
                for step in range(4):
                    self.swap(*chunk, j, step).wait_send()


class Scatter:
    def __init__(self, place, bufs, slots, total, send, recv):
        self.place, self.bufs, self.slots, self.total, self.send, self.recv = place, bufs, slots, total, send, recv

    def slot(self, phase, arr, j):
        return self.slots[(phase * 2 + arr) * 3 + j]

    def part(self, l, arr, at, j):
        whole = slice(None)
        x_hi, x_lo = (at["x"] // 2, at["x"] % 2) if "x" in at else (whole, whole)
        low, high = THIRDS[arr][j]
        return self.bufs[arr].at[
            l, x_lo, at.get("y", whole), x_hi, at.get("z", whole), whole, pl.ds(low, high - low)
        ]

    def copies(self, l, arr, phase):
        place = self.place
        out = []
        for j, order in enumerate(ORDERS):
            rev = order[::-1]
            for step in (1, 2, 3):
                there = {a: place.at[a] for a in rev[:phase]}
                there[rev[phase]], device = place.along(rev[phase], step)
                dst = self.slot(phase, arr, j).at[l, step - 1]
                sems = (self.send.at[l, arr, phase, j, step - 1], self.recv.at[l, arr, phase, j, step - 1])
                out.append(remote(self.part(l, arr, there, j), dst, *sems, device))
        return out

    def add_up(self, l, arr, phase):
        for j, order in enumerate(ORDERS):
            rev = order[::-1]
            own = self.part(l, arr, {a: self.place.at[a] for a in rev[: phase + 1]}, j)
            came = self.slot(phase, arr, j)
            if phase == 2:
                low, high = THIRDS[arr][j]
                total = own[...].astype(F32)
                for k in range(3):
                    total = total + came[l, k].astype(F32)
                self.total[l, :, 512 * arr + low : 512 * arr + high] = total
                continue

            def body(index, own=own, came=came):
                total = own[index].astype(F32)
                for k in range(3):
                    total = total + came[(l, k) + index].astype(F32)
                own[index] = total.astype(BF)

            each_block(dims_of(rev[phase + 1 :]), body)

    def step(self, l, arr, stage):
        if stage > 0:
            for copy in self.copies(l, arr, stage - 1):
                copy.wait_recv()
            self.add_up(l, arr, stage - 1)
        if stage < 3:
            for copy in self.copies(l, arr, stage):
                copy.start()

    def finish(self):
        for chunk in CHUNKS:
            for phase in range(3):
                for copy in self.copies(*chunk, phase):
                    copy.wait_send()


def train_kernel(*refs):
    r = dict(zip(NAMES, refs[: len(NAMES)]))
    slots = refs[len(NAMES) :]
    place = Place()
    seq, core, x_lo = place.seq, place.core, place.seq // 2
    peer = 1 - core
    near = place.other_core()
    across = {"dp": place.dp, "seq": (1 - x_lo) * 2 + core}
    wa, wm, ga, gm, vec, vgrad = r["wa"], r["wm"], r["ga"], r["gm"], r["vec"], r["vgrad"]
    s0, r0, stage, kv = r["s0"], r["r0"], r["stage"], r["kv"]
    unsent = []

    def send(src, dst, sem, index, device):
        copy = remote(src, dst, r[sem + "_send"].at[index], r[sem + "_recv"].at[index], device)
        copy.start()
        unsent.append(copy)
        return copy

    for s, q in enumerate(QUARTERS):
        for l in range(2):
            s0[s, l, :, 0:512] = r["w_attn"][l, :, 512 * q : 512 * q + 512]
            s0[s, l, :, 512:1536] = r["w_mlp"][l, :, 1024 * s : 1024 * s + 1024]
    vec[...] = r["table"][...]
    r["docs"][seq] = r["seg_row"][...]
    greet(place)

    pieces, docs = [], []
    for step in (1, 2, 3):
        member, device = place.in_group(step)
        pieces.append(send(s0.at[member], r0.at[seq], "a2a", (0, step), device))
    table = Table(place, vec, r["vgot"].at[0], r["v_send"].at[0], r["v_recv"].at[0])
    table.start(0)
    for step in (1, 2, 3):
        member, device = place.in_group(step)
        docs.append(send(r["docs"].at[seq], r["docs"].at[seq], "doc", step, device))
    r0[seq] = s0[seq]
    for copy in pieces:
        copy.wait_recv()
    for src in range(4):
        for l in range(2):
            stage[l, 4 * src : 4 * src + 4, :] = r0[src, l]
    at = place.at
    for l, arr in CHUNKS:
        block = stage[l, :, 512 * arr : 512 * arr + WIDTHS[arr]].astype(BF)
        (wa, wm)[arr][l, at["x"] % 2, core, at["y"], at["x"] // 2, at["z"]] = block
    gather = Gather(place, (wa, wm), r["ag_send"], r["ag_recv"], r["sw_send"], r["sw_recv"])
    table.finish(0)
    table.start(1)
    for chunk in CHUNKS:
        gather.start(*chunk, 0)
    table.finish(1)
    table.start(2)
    for chunk in CHUNKS[:2]:
        gather.arrive(*chunk, 0)
        gather.start(*chunk, 1)
    table.finish(2)
    table.start(3)
    for chunk in CHUNKS[:2]:
        gather.arrive(*chunk, 1)
        gather.start(*chunk, 2)
    for copy in docs:
        copy.wait_recv()
    seg_row = jnp.concatenate([r["docs"][i] for i in range(4)], axis=1)
    r["bias"][...] = jnp.where(r["seg_col"][...] == seg_row, 0.0, MASKED_SCORE)
    for chunk in CHUNKS[2:]:
        gather.arrive(*chunk, 0)
    table.finish(3)
    gather.swap_start(0, 0)
    gather.swap_arrive(0, 0)

    def weight(l, arr, s, low=0, high=None):
        high = WIDTHS[arr] if high is None else high
        return (wa, wm)[arr][l, s // 2, s % 2, :, :, :, :, low:high].reshape(512, high - low)

    def attn_weight(l, q):
        return weight(l, 0, QUARTERS.index(q))

    def put_grad(l, arr, plane, left, right, parts):
        width = WIDTHS[arr] // parts
        for i in range(parts):
            value = mm(left, right(width * i, width * i + width), TN)
            (ga, gm)[arr][l, plane, :, :, :, :, width * i : width * i + width] = value.astype(BF).reshape(
                4, 2, 4, 16, width
            )

    def row(l, k):
        return vec[12 * l + k : 12 * l + k + 1, :]

    def put_row(l, k, value):
        vgrad[12 * l + k : 12 * l + k + 1, :] = value

    lanes = lax.broadcasted_iota(jnp.int32, (1, 128), 1)
    first = (lanes < 64).astype(F32)
    second = 1.0 - first
    first_low, second_low = first.astype(BF), second.astype(BF)

    def both(pair):
        return jnp.concatenate([pair * first_low, pair * second_low], axis=0)

    def joined(stacked):
        return stacked[:128] * first + stacked[128:] * second

    def group_rows(l, which, low):
        return kv[l, :, which, :, low : low + 128].reshape(512, 128)

    def put_keys(l, which, value):
        kv[l, seq, which] = value.astype(BF)
        mine = kv.at[l, seq, which]
        far = send(mine, mine, "kv", (l, which, 0), across)
        return far, send(mine, mine, "kv", (l, which, 1), near)

    def pass_on(l, which, far):
        far.wait_recv()
        came = kv.at[l, (1 - x_lo) * 2 + core, which]
        return send(came, came, "kv", (l, which, 2), near)

    pairs = r["pairs"]
    hidden = r["tokens"][...].astype(F32)
    for l in range(2):
        if l == 1:
            gather.swap_arrive(1, 0)
        low_in = hidden.astype(BF)
        pairs[l, 0, core] = low_in
        send(pairs.at[l, 0, core], pairs.at[l, 0, core], "act", (l, 0), near)
        keys_way = put_keys(l, 0, mm(low_in, attn_weight(l, 1)))
        values_way = put_keys(l, 1, mm(low_in, attn_weight(l, 2)) + row(l, 1))
        r["q"][l] = (mm(low_in, attn_weight(l, 0)) + row(l, 0)).astype(BF)
        if l == 0:
            for chunk in CHUNKS[2:]:
                gather.start(*chunk, 1)
            gather.swap_start(0, 1)
        on_keys = pass_on(l, 0, keys_way[0])
        on_values = pass_on(l, 1, values_way[0])
        if l == 0:
            for chunk in CHUNKS[2:]:
                gather.arrive(*chunk, 1)
                gather.start(*chunk, 2)
        for copy in (keys_way[1], values_way[1], on_keys, on_values):
            copy.wait_recv()
        for pair in range(4):
            low = 128 * pair
            scores = mm(both(r["q"][l, :, low : low + 128]), group_rows(l, 0, low), NT) * SCALE
            bias = r["bias"][...]
            scores = scores + jnp.concatenate([bias, bias], axis=0)
            powers = jnp.exp(scores - jnp.max(scores, axis=-1, keepdims=True))
            probs = (powers * (1.0 / jnp.sum(powers, axis=-1, keepdims=True))).astype(BF)
            r["probs"][l, pair] = probs
            pairs[l, 1, core, :, low : low + 128] = joined(mm(probs, group_rows(l, 1, low))).astype(BF)
        send(pairs.at[l, 1, core], pairs.at[l, 1, core], "act", (l, 1), near)
        if l == 0:
            gather.swap_arrive(0, 1)
        hat, inverse = normalize(hidden + mm(pairs[l, 1, core], attn_weight(l, 3)) + row(l, 2))
        r["hat1"][l] = hat
        r["inv1"][l] = inverse
        normed = hat * row(l, 3) + row(l, 4)
        low_normed = normed.astype(BF)
        pairs[l, 2, core] = low_normed
        send(pairs.at[l, 2, core], pairs.at[l, 2, core], "act", (l, 2), near)
        back = jnp.zeros((128, 512), F32)
        if l == 1:
            gather.swap_start(1, 1)
            gather.swap_arrive(1, 1)
        for i in range(4):
            half, low = i // 2, 512 * (i % 2)
            pre = mm(low_normed, weight(l, 1, half, low, low + 512)) + row(l, 5 + i)
            normal = 0.5 + 0.5 * lax.erf(pre * (0.5**0.5))
            act = (pre * normal).astype(BF)
            r["act"][l, half, core, :, low : low + 512] = act
            slope = normal + pre * (jnp.exp(pre * pre * -0.5) * (1.0 / (2.0 * math.pi) ** 0.5))
            r["slope"][l, :, 512 * i : 512 * i + 512] = slope.astype(BF)
            back = back + mm(act, weight(l, 1, 2 + half, low, low + 512), NT)
        mine = r["act"].at[l, peer, core]
        send(mine, mine, "act", (l, 3), near)
        if l == 0:
            gather.swap_start(1, 0)
        hat, inverse = normalize(normed + back + row(l, 9))
        r["hat2"][l] = hat
        r["inv2"][l] = inverse
        hidden = hat * row(l, 10) + row(l, 11)
    r["block_out"][...] = hidden.astype(BF)

    scatter = Scatter(place, (ga, gm), slots, r["total"], r["rs_send"], r["rs_recv"])
    dkv, dkv_near, dkv_far, late, early = r["dkv"], r["dkv_near"], r["dkv_far"], r["late"], r["early"]

    def halves(part):
        return pl.ds(256 * part, 256)

    def give_near(l, part):
        return send(
            dkv.at[l, :, peer, :, :, halves(part)], dkv_near.at[l, :, :, :, halves(part)], "dkv", (l, part, 0), near
        )

    def give_far(l, part, copy):
        copy.wait_recv()
        span = slice(256 * part, 256 * part + 256)
        mine = dkv[l, 1 - x_lo, core, :, :, span].astype(F32) + dkv_near[l, 1 - x_lo, :, :, span].astype(F32)
        dkv[l, 1 - x_lo, core, :, :, span] = mine.astype(BF)
        return send(
            dkv.at[l, 1 - x_lo, core, :, :, halves(part)], dkv_far.at[l, :, :, halves(part)], "dkv", (l, part, 1), across
        )

    def act_arrive(l, which):
        if which == 3:
            ref = r["act"].at[l, core, peer]
        else:
            ref = pairs.at[l, which, peer]
        remote(ref, ref, r["act_send"].at[l, which], r["act_recv"].at[l, which], near).wait_recv()

    def two(ref, *index):
        return ref[index].reshape(256, -1)

    grad = r["cotangent"][...].astype(F32)
    for l in (1, 0):
        hat = r["hat2"][l]
        put_row(l, 10, column_sum(grad * hat))
        put_row(l, 11, column_sum(grad))
        grad_second = normalize_back(grad * row(l, 10), hat, r["inv2"][l])
        put_row(l, 9, column_sum(grad_second))
        low_second = grad_second.astype(BF)
        pairs[l, 3, core] = low_second
        got_second = send(pairs.at[l, 3, core], pairs.at[l, 3, core], "back", (l, 0), near)
        grad_normed = grad_second
        for i in range(4):
            half, low = i // 2, 512 * (i % 2)
            grad_act = mm(low_second, weight(l, 1, 2 + half, low, low + 512))
            grad_pre = (grad_act * r["slope"][l, :, 512 * i : 512 * i + 512].astype(F32)).astype(BF)
            put_row(l, 5 + i, column_sum(grad_pre.astype(F32)))
            r["du"][l, half, core, :, low : low + 512] = grad_pre
            grad_normed = grad_normed + mm(grad_pre, weight(l, 1, half, low, low + 512), NT)
        mine = r["du"].at[l, peer, core]
        send(mine, mine, "back", (l, 1), near)
        if l == 0:
            scatter.step(1, 1, 1)
        hat = r["hat1"][l]
        put_row(l, 3, column_sum(grad_normed * hat))
        put_row(l, 4, column_sum(grad_normed))
        grad_first = normalize_back(grad_normed * row(l, 3), hat, r["inv1"][l])
        put_row(l, 2, column_sum(grad_first))
        low_first = grad_first.astype(BF)
        early[l, 1, core] = low_first
        grad_mixed = mm(low_first, attn_weight(l, 3), NT).astype(BF)
        near_ways, far_ways = [], []
        for pair in range(4):
            low = 128 * pair
            keys, values = group_rows(l, 0, low), group_rows(l, 1, low)
            grad_pair = both(grad_mixed[:, low : low + 128])
            probs = r["probs"][l, pair]
            grad_probs = mm(grad_pair, values, NT)
            dkv[l, :, :, 1, :, low : low + 128] = mm(probs, grad_pair, TN).astype(BF).reshape(2, 2, 128, 128)
            wide = probs.astype(F32)
            row_dot = jnp.sum(grad_probs * wide, axis=-1, keepdims=True)
            grad_scores = (wide * (grad_probs - row_dot)).astype(BF)
            early[l, 0, core, :, low : low + 128] = (joined(mm(grad_scores, keys)) * SCALE).astype(BF)
            grad_keys = mm(grad_scores, both(r["q"][l, :, low : low + 128]), TN) * SCALE
            dkv[l, :, :, 0, :, low : low + 128] = grad_keys.astype(BF).reshape(2, 2, 128, 128)
            if pair % 2 == 1:
                near_ways.append(give_near(l, pair // 2))
            if pair == 2:
                far_ways.append(give_far(l, 0, near_ways[0]))
        mine = early.at[l, peer, core]
        send(mine, mine, "back", (l, 2), near)
        grad_queries = early[l, 0, core]
        put_row(l, 0, column_sum(grad_queries.astype(F32)))
        grad = grad_first + mm(grad_queries, attn_weight(l, 0), NT)
        far_ways.append(give_far(l, 1, near_ways[1]))
        if l == 0:
            scatter.step(1, 0, 1)
        got_second.wait_recv()
        act_arrive(l, 2)
        act_arrive(l, 3)
        theirs = r["du"].at[l, core, peer]
        remote(theirs, theirs, r["back_send"].at[l, 1], r["back_recv"].at[l, 1], near).wait_recv()
        put_grad(l, 1, 0, two(pairs, l, 2), lambda low, high: r["du"][l, core, :, :, low:high].reshape(256, -1), 2)
        put_grad(l, 1, 1, two(pairs, l, 3), lambda low, high: r["act"][l, core, :, :, low:high].reshape(256, -1), 2)
        scatter.step(l, 1, 0)
        act_arrive(l, 0)
        act_arrive(l, 1)
        theirs = early.at[l, core, peer]
        remote(theirs, theirs, r["back_send"].at[l, 2], r["back_recv"].at[l, 2], near).wait_recv()
        put_grad(l, 0, 0, two(pairs, l, core), lambda low, high: two(early, l, core), 1)
        if l == 0:
            scatter.step(1, 1, 2)
            scatter.step(1, 0, 2)
        for copy in far_ways:
            copy.wait_recv()
        for which in range(2):
            total = dkv[l, x_lo, core, which].astype(F32) + dkv_near[l, x_lo, which].astype(F32)
            late[l, which, core] = (total + dkv_far[l, which].astype(F32)).astype(BF)
        mine = late.at[l, peer, core]
        send(mine, mine, "back", (l, 3), near)
        put_row(l, 1, column_sum(late[l, 1, core].astype(F32)))
        if l == 0:
            table = Table(place, vgrad, r["vgot"].at[1], r["v_send"].at[1], r["v_recv"].at[1])
            table.start(0)
        grad = grad + mm(late[l, 0, core], attn_weight(l, 1), NT) + mm(late[l, 1, core], attn_weight(l, 2), NT)
        theirs = late.at[l, core, peer]
        remote(theirs, theirs, r["back_send"].at[l, 3], r["back_recv"].at[l, 3], near).wait_recv()
        put_grad(l, 0, 1, two(pairs, l, 0), lambda low, high: two(late, l, core), 1)
        if l == 0:
            table.finish(0)
            table.start(1)
        scatter.step(l, 0, 0)
    r["input_grad"][...] = grad
    scatter.step(1, 1, 3)
    scatter.step(1, 0, 3)
    table.finish(1)
    table.start(2)
    scatter.step(0, 1, 1)
    scatter.step(0, 0, 1)
    table.finish(2)
    table.start(3)
    scatter.step(0, 1, 2)
    scatter.step(0, 0, 2)
    table.finish(3)
    scatter.step(0, 1, 3)
    scatter.step(0, 0, 3)
    s4, fin, total = r["s4"], r["fin"], r["total"]
    for dst in range(4):
        for l in range(2):
            s4[dst, l] = total[l, 4 * dst : 4 * dst + 4, :]
    moved = []
    for step in (1, 2, 3):
        member, device = place.in_group(step)
        moved.append(send(s4.at[member], fin.at[seq], "a2a", (1, step), device))
    fin[seq] = s4[seq]
    gather.finish()
    scatter.finish()
    for copy in moved:
        copy.wait_recv()
    for copy in unsent:
        copy.wait_send()


INPUTS = ("tokens", "cotangent", "seg_row", "seg_col", "w_attn", "w_mlp", "table")
OUTPUTS = {
    "block_out": ((128, 512), BF),
    "input_grad": ((128, 512), F32),
    "fin": ((4, 2, 4, 1536), F32),
    "vgrad": ((24, 512), F32),
}
DIMS = (2, 2, 2, 4, 2, 4, 16)
HALF = (2, 2, 4, 2, 4, 16)
SCRATCH = {
    "wa": (DIMS + (512,), BF),
    "wm": (DIMS + (1024,), BF),
    "ga": (HALF + (512,), BF),
    "gm": (HALF + (1024,), BF),
    "vec": ((24, 512), F32),
    "s0": ((4, 2, 4, 1536), F32),
    "r0": ((4, 2, 4, 1536), F32),
    "s4": ((4, 2, 4, 1536), F32),
    "stage": ((2, 16, 1536), F32),
    "total": ((2, 16, 1536), F32),
    "vgot": ((2, 4, 3, 24, 512), F32),
    "docs": ((4, 1, 128), jnp.int32),
    "bias": ((128, 512), F32),
    "q": ((2, 128, 512), BF),
    "kv": ((2, 4, 2, 128, 512), BF),
    "probs": ((2, 4, 256, 512), BF),
    "pairs": ((2, 4, 2, 128, 512), BF),
    "act": ((2, 2, 2, 128, 1024), BF),
    "du": ((2, 2, 2, 128, 1024), BF),
    "early": ((2, 2, 2, 128, 512), BF),
    "late": ((2, 2, 2, 128, 512), BF),
    "hat1": ((2, 128, 512), F32),
    "inv1": ((2, 128, 1), F32),
    "slope": ((2, 128, 2048), BF),
    "hat2": ((2, 128, 512), F32),
    "inv2": ((2, 128, 1), F32),
    "dkv": ((2, 2, 2, 2, 128, 512), BF),
    "dkv_near": ((2, 2, 2, 128, 512), BF),
    "dkv_far": ((2, 2, 128, 512), BF),
}
SEMS = {
    "a2a": (2, 4),
    "doc": (4,),
    "ag": (2, 2, 3, 3, 3),
    "sw": (2, 2, 3, 4),
    "rs": (2, 2, 3, 3, 3),
    "kv": (2, 2, 3),
    "dkv": (2, 2, 2),
    "act": (2, 4),
    "back": (2, 4),
    "v": (2, 4, 3),
}
NAMES = INPUTS + tuple(OUTPUTS) + tuple(SCRATCH) + tuple(f"{n}_{d}" for n in SEMS for d in ("send", "recv"))


def train(*args):
    slots = []
    for phase in range(3):
        for arr in range(2):
            for j in range(3):
                low, high = THIRDS[arr][j]
                rest = dims_of(ORDERS[j][::-1][phase + 1 :])
                slots.append(pltpu.VMEM((2, 3) + rest + (16, high - low), BF))
    scratch = [pltpu.VMEM(*spec) for spec in SCRATCH.values()]
    for shape in SEMS.values():
        scratch += [pltpu.SemaphoreType.DMA(shape)] * 2
    return pl.pallas_call(
        train_kernel,
        out_shape=tuple(jax.ShapeDtypeStruct(*spec) for spec in OUTPUTS.values()),
        in_specs=[pl.BlockSpec(memory_space=pltpu.VMEM)] * len(INPUTS),
        out_specs=[pl.BlockSpec(memory_space=pltpu.VMEM)] * len(OUTPUTS),
        scratch_shapes=scratch + slots,
        compiler_params=pltpu.CompilerParams(
            collective_id=0, has_side_effects=True, vmem_limit_bytes=VMEM_BYTES
        ),
        name="train",
    )(*args)


def adam_update(weight, grad, first, second, rate, decay):
    first_new = BETA_FIRST * first + (1.0 - BETA_FIRST) * grad
    second_new = BETA_SECOND * second + (1.0 - BETA_SECOND) * grad * grad
    first_fix = 1.0 - BETA_FIRST**STEP
    second_fix = 1.0 - BETA_SECOND**STEP
    weight_new = weight - rate * (
        first_new / first_fix / (jnp.sqrt(second_new / second_fix) + ADAM_EPSILON) + decay * weight
    )
    return (first_new, second_new, weight_new)


def local(
    tokens, cotangent, segments, w_attn, w_mlp, vectors, m_attn, m_mlp, m_vec, v_attn, v_mlp, v_vec
):
    place = lax.axis_index("dp") * 4 + lax.axis_index("seq")
    table = lax.dynamic_update_slice(
        jnp.zeros((24, 512), F32),
        vectors.astype(BF).astype(F32).reshape(24, 4),
        (0, 4 * place),
    )
    block_out, input_grad, fin, vec_total = train(
        tokens[0], cotangent[0], segments, segments.reshape(128, 1), w_attn, w_mlp, table
    )
    grad_attn = jnp.concatenate([fin[QUARTERS.index(q), ..., :512] for q in range(4)], axis=-1)
    grad_mlp = fin[..., 512:].transpose(1, 2, 0, 3).reshape(2, 4, 4096)
    grad_vec = lax.dynamic_slice(vec_total, (0, 4 * place), (24, 4)).reshape(2, 12, 4)
    return (
        block_out[None],
        input_grad[None],
        *adam_update(w_attn, grad_attn, m_attn, v_attn, LEARN_RATE, WEIGHT_DECAY),
        *adam_update(w_mlp, grad_mlp, m_mlp, v_mlp, LEARN_RATE, WEIGHT_DECAY),
        *adam_update(vectors, grad_vec, m_vec, v_vec, VECTOR_RATE, 0.0),
    )


def solution(mesh):
    in_specs = (
        P("dp", "seq", None),
        P("dp", "seq", None),
        P("dp", "seq"),
        P(None, ("dp", "seq"), None),
        P(None, ("dp", "seq"), None),
        P(None, None, ("dp", "seq")),
        P(None, ("dp", "seq"), None),
        P(None, ("dp", "seq"), None),
        P(None, None, ("dp", "seq")),
        P(None, ("dp", "seq"), None),
        P(None, ("dp", "seq"), None),
        P(None, None, ("dp", "seq")),
    )
    out_specs = (
        P("dp", "seq", None),
        P("dp", "seq", None),
        P(None, ("dp", "seq"), None),
        P(None, ("dp", "seq"), None),
        P(None, ("dp", "seq"), None),
        P(None, ("dp", "seq"), None),
        P(None, ("dp", "seq"), None),
        P(None, ("dp", "seq"), None),
        P(None, None, ("dp", "seq")),
        P(None, None, ("dp", "seq")),
        P(None, None, ("dp", "seq")),
    )
    return jax.shard_map(local, mesh=mesh, in_specs=in_specs, out_specs=out_specs, check_vma=False)
```

```python
import math

import jax
import jax.numpy as jnp
from jax import lax
from jax.experimental import pallas as pl
from jax.experimental.pallas import tpu as pltpu
from jax.sharding import PartitionSpec as P

STEP = 10
NORM_EPSILON = 1e-06
ADAM_EPSILON = 1e-06
BETA_FIRST = 0.9
BETA_SECOND = 0.999
LEARN_RATE = 0.03
VECTOR_RATE = 0.2
WEIGHT_DECAY = 0.01
MASKED_SCORE = -1e30
VMEM_BYTES = 62 * 2**20
MESH = pl.DeviceIdType.MESH
BF = jnp.bfloat16
F32 = jnp.float32
THIRDS = (((0, 128), (128, 256), (256, 512)), ((0, 384), (384, 768), (768, 1024)))
WIDTHS = (512, 1024)
ORDERS = (("x", "y", "z"), ("y", "z", "x"), ("z", "x", "y"))


class Place:
    def __init__(self):
        self.dp = lax.axis_index("dp")
        self.seq = lax.axis_index("seq")
        self.core = self.seq % 2
        self.at = {
            "x": ((self.dp // 4) % 2) * 2 + self.seq // 2,
            "y": self.dp // 8,
            "z": self.dp % 4,
        }

    def device(self, at, core):
        return {
            "dp": (at["y"] * 2 + at["x"] // 2) * 4 + at["z"],
            "seq": (at["x"] % 2) * 2 + core,
        }

    def along(self, axis, step):
        at = dict(self.at)
        at[axis] = (at[axis] + step) % 4
        return at[axis], self.device(at, self.core)

    def other_core(self):
        return self.device(self.at, 1 - self.core)

    def in_group(self, step):
        peer = (self.seq + step) % 4
        return peer, {"dp": self.dp, "seq": peer}


def region(buf, layer, at, core, columns):
    whole = slice(None)
    if "x" in at:
        x_hi, x_lo = at["x"] // 2, at["x"] % 2
    else:
        x_hi, x_lo = whole, whole
    cols = pl.ds(columns[0], columns[1] - columns[0])
    return buf.at[layer, x_lo, core, at.get("y", whole), x_hi, at.get("z", whole), whole, cols]


def greet(place):
    barrier = pltpu.get_barrier_semaphore()
    peers = [place.other_core()]
    for axis in ("x", "y", "z"):
        for step in (1, 2, 3):
            peers.append(place.along(axis, step)[1])
    far = {"dp": place.dp, "seq": (1 - place.seq // 2) * 2 + (1 - place.core)}
    peers.append(far)
    for peer in peers:
        pl.semaphore_signal(barrier, inc=1, device_id=peer, device_id_type=MESH)
    pl.semaphore_wait(barrier, len(peers))


def remote(src, dst, send, recv, device):
    return pltpu.make_async_remote_copy(
        src_ref=src, dst_ref=dst, send_sem=send, recv_sem=recv, device_id=device, device_id_type=MESH
    )


class Table:
    ROUNDS = {"core": (0, (1,)), "x": (1, (1, 2, 3)), "y": (2, (1, 2, 3)), "z": (3, (1, 2, 3))}

    def __init__(self, place, blocks, came, send, recv):
        self.place, self.blocks, self.came, self.send, self.recv = place, blocks, came, send, recv
        self.going, self.mode, self.axis = None, None, None

    def start(self, axis, mode="add"):
        number, steps = self.ROUNDS[axis]
        own = self.blocks.at[self.place.at["y"]]
        self.going, self.mode, self.axis = [], mode, axis
        for step in steps:
            if axis == "core":
                device = self.place.other_core()
            else:
                pos, device = self.place.along(axis, step)
            src = self.blocks.at[pos] if mode == "collect" else own
            dst = own if mode == "spread" else self.came.at[number, step - 1]
            copy = remote(src, dst, self.send.at[number, step - 1], self.recv.at[number, step - 1], device)
            copy.start()
            self.going.append(copy)

    def finish(self):
        number, steps = self.ROUNDS[self.axis]
        for copy in self.going:
            copy.wait()
        if self.mode != "spread":
            total = self.blocks[self.place.at["y"]]
            for step in steps:
                total = total + self.came[number, step - 1]
            self.blocks[self.place.at["y"]] = total


def dims_of(axes):
    out = ()
    if "x" in axes:
        out += (2,)
    if "y" in axes:
        out += (4,)
    if "x" in axes:
        out += (2,)
    if "z" in axes:
        out += (4,)
    return out


def each_block(dims, body):
    count = 1
    for size in dims[:-1]:
        count *= size

    def one(i, carry):
        index = ()
        rest = i
        for size in reversed(dims[:-1]):
            index = (rest % size,) + index
            rest = rest // size
        body(index)
        return carry

    if count == 1:
        body(tuple(0 for _ in dims[:-1]))
    else:
        lax.fori_loop(0, count, one, 0)


NT = (((1,), (1,)), ((), ()))
NN = (((1,), (0,)), ((), ()))
TN = (((0,), (0,)), ((), ()))
CHUNKS = ((0, 0), (0, 1), (1, 0), (1, 1))
PIECES = (16, 1536)
SCALE = 0.125
QUARTERS = (0, 3, 1, 2)


def mm(left, right, dims=NN):
    return lax.dot_general(left, right, dims, preferred_element_type=F32)


def column_sum(values):
    return jnp.sum(values, axis=0, keepdims=True)


def normalize(summed):
    center = summed - jnp.mean(summed, axis=-1, keepdims=True)
    spread = jnp.mean(center * center, axis=-1, keepdims=True)
    inverse = lax.rsqrt(spread + NORM_EPSILON)
    return center * inverse, inverse


def normalize_back(grad, hat, inverse):
    mean = jnp.mean(grad, axis=-1, keepdims=True)
    along = jnp.mean(grad * hat, axis=-1, keepdims=True)
    return inverse * (grad - mean - hat * along)


class Gather:
    def __init__(self, place, bufs, send, recv, swap_send, swap_recv):
        self.place, self.bufs = place, bufs
        self.send, self.recv, self.swap_send, self.swap_recv = send, recv, swap_send, swap_recv

    def copies(self, l, arr, phase, coming):
        place = self.place
        out = []
        for j, order in enumerate(ORDERS):
            axis = order[phase]
            here = {a: place.at[a] for a in order[phase:]}
            for step in (1, 2, 3):
                _, device = place.along(axis, step)
                spot = dict(here)
                if coming:
                    spot[axis] = (place.at[axis] - step) % 4
                ref = region(self.bufs[arr], l, spot, place.core, THIRDS[arr][j])
                sems = (self.send.at[l, arr, phase, j, step - 1], self.recv.at[l, arr, phase, j, step - 1])
                out.append(remote(ref, ref, *sems, device))
        return out

    def start(self, l, arr, phase):
        for copy in self.copies(l, arr, phase, False):
            copy.start()
        if phase == 2:
            for j in range(3):
                self.swap(l, arr, j, 0).start()

    def arrive(self, l, arr, phase):
        for copy in self.copies(l, arr, phase, True):
            copy.wait_recv()

    def swap(self, l, arr, j, step, coming=False):
        place = self.place
        axis = ORDERS[j][2]
        core = 1 - place.core if coming else place.core
        ref = region(self.bufs[arr], l, {axis: (place.at[axis] - step) % 4}, core, THIRDS[arr][j])
        return remote(
            ref, ref, self.swap_send.at[l, arr, j, step], self.swap_recv.at[l, arr, j, step], place.other_core()
        )

    def swap_start(self, l, arr):
        copies = self.copies(l, arr, 2, True)
        for step in (1, 3, 2):
            for j in range(3):
                copies[3 * j + step - 1].wait_recv()
                self.swap(l, arr, j, step).start()

    def swap_arrive(self, l, arr):
        for j in range(3):
            for step in range(4):
                self.swap(l, arr, j, step, True).wait_recv()

    def finish(self):
        for chunk in CHUNKS:
            for phase in range(3):
                for copy in self.copies(*chunk, phase, False):
                    copy.wait_send()
            for j in range(3):
                for step in range(4):
                    self.swap(*chunk, j, step).wait_send()


class Scatter:
    def __init__(self, place, bufs, slots, total, send, recv):
        self.place, self.bufs, self.slots, self.total, self.send, self.recv = place, bufs, slots, total, send, recv

    def slot(self, phase, arr, j):
        return self.slots[(phase * 2 + arr) * 3 + j]

    def part(self, l, arr, at, j):
        whole = slice(None)
        x_hi, x_lo = (at["x"] // 2, at["x"] % 2) if "x" in at else (whole, whole)
        low, high = THIRDS[arr][j]
        return self.bufs[arr].at[
            l, x_lo, at.get("y", whole), x_hi, at.get("z", whole), whole, pl.ds(low, high - low)
        ]

    def copies(self, l, arr, phase):
        place = self.place
        out = []
        for j, order in enumerate(ORDERS):
            rev = order[::-1]
            for step in (1, 2, 3):
                there = {a: place.at[a] for a in rev[:phase]}
                there[rev[phase]], device = place.along(rev[phase], step)
                dst = self.slot(phase, arr, j).at[l, step - 1]
                sems = (self.send.at[l, arr, phase, j, step - 1], self.recv.at[l, arr, phase, j, step - 1])
                out.append(remote(self.part(l, arr, there, j), dst, *sems, device))
        return out

    def add_up(self, l, arr, phase):
        for j, order in enumerate(ORDERS):
            rev = order[::-1]
            own = self.part(l, arr, {a: self.place.at[a] for a in rev[: phase + 1]}, j)
            came = self.slot(phase, arr, j)
            if phase == 2:
                low, high = THIRDS[arr][j]
                total = own[...].astype(F32)
                for k in range(3):
                    total = total + came[l, k].astype(F32)
                self.total[l, :, 512 * arr + low : 512 * arr + high] = total
                continue

            def body(index, own=own, came=came):
                total = own[index].astype(F32)
                for k in range(3):
                    total = total + came[(l, k) + index].astype(F32)
                own[index] = total.astype(BF)

            each_block(dims_of(rev[phase + 1 :]), body)

    def step(self, l, arr, stage):
        if stage > 0:
            for copy in self.copies(l, arr, stage - 1):
                copy.wait_recv()
            self.add_up(l, arr, stage - 1)
        if stage < 3:
            for copy in self.copies(l, arr, stage):
                copy.start()

    def finish(self):
        for chunk in CHUNKS:
            for phase in range(3):
                for copy in self.copies(*chunk, phase):
                    copy.wait_send()


def train_kernel(*refs):
    r = dict(zip(NAMES, refs[: len(NAMES)]))
    slots = refs[len(NAMES) :]
    place = Place()
    seq, core, x_lo = place.seq, place.core, place.seq // 2
    peer = 1 - core
    near = place.other_core()
    across = {"dp": place.dp, "seq": (1 - x_lo) * 2 + core}
    wa, wm, ga, gm, vec, vgrad = r["wa"], r["wm"], r["ga"], r["gm"], r["vec"], r["vgrad"]
    s0, r0, stage, kv = r["s0"], r["r0"], r["stage"], r["kv"]
    unsent = []

    def send(src, dst, sem, index, device):
        copy = remote(src, dst, r[sem + "_send"].at[index], r[sem + "_recv"].at[index], device)
        copy.start()
        unsent.append(copy)
        return copy

    t0 = r["t0"]
    for s, q in enumerate(QUARTERS):
        for l in range(2):
            t0[s, 8 * l : 8 * l + 4, 0:512] = r["w_attn"][l, :, 512 * q : 512 * q + 512]
            t0[s, 8 * l : 8 * l + 4, 512:768] = r["w_mlp"][l, :, 1024 * s : 1024 * s + 256]
            t0[s, 8 * l + 4 : 8 * l + 8, :] = r["w_mlp"][l, :, 1024 * s + 256 : 1024 * s + 1024]
    s0[...] = t0[...].astype(BF)
    tab = r["tab"]
    number = place.dp * 4 + seq
    tab[place.at["y"]] = jnp.zeros((24, 128), F32)
    for l in range(2):
        tab[place.at["y"], 12 * l : 12 * l + 12, 0:4] = r["vectors"][l].astype(BF).astype(F32)
    tab[place.at["y"]] = pltpu.roll(tab[place.at["y"]], 4 * (number % 32), 1)
    r["docs"][seq] = r["segments"][...]
    xall = r["xall"]
    xall[0, x_lo, core] = r["tokens"][...]
    greet(place)

    pieces, docs = [], []
    for step in (1, 2, 3):
        member, device = place.in_group(step)
        pieces.append(send(s0.at[member], r0.at[seq], "a2a", (2, step), device))
    table = Table(place, tab, r["vgot"].at[0], r["v_send"].at[0], r["v_recv"].at[0])
    table.start("core")
    for step in (1, 2, 3):
        member, device = place.in_group(step)
        docs.append(send(r["docs"].at[seq], r["docs"].at[seq], "doc", step, device))
    r0[seq] = s0[seq]
    for copy in pieces:
        copy.wait_recv()
    for src in range(4):
        t0[src] = r0[src].astype(F32)
        for l in range(2):
            stage[l, 4 * src : 4 * src + 4, 0:768] = t0[src, 8 * l : 8 * l + 4, :]
            stage[l, 4 * src : 4 * src + 4, 768:1536] = t0[src, 8 * l + 4 : 8 * l + 8, :]
    at = place.at
    for l, arr in CHUNKS:
        block = stage[l, :, 512 * arr : 512 * arr + WIDTHS[arr]].astype(BF)
        (wa, wm)[arr][l, at["x"] % 2, core, at["y"], at["x"] // 2, at["z"]] = block
    gather = Gather(place, (wa, wm), r["ag_send"], r["ag_recv"], r["sw_send"], r["sw_recv"])
    table.finish()
    table.start("x")
    for chunk in CHUNKS:
        gather.start(*chunk, 0)

    def share(l):
        mine = xall.at[l, x_lo, core]
        near_way = send(mine, mine, "x", (l, 0), near)
        return near_way, send(mine, mine, "x", (l, 1), across)

    def pass_on(l, far_way):
        far_way.wait_recv()
        came = xall.at[l, 1 - x_lo, core]
        return send(came, came, "x", (l, 2), near)

    first_near, first_far = share(0)
    table.finish()
    table.start("z")
    for chunk in CHUNKS:
        gather.arrive(*chunk, 0)
        gather.start(*chunk, 1)
    table.finish()
    table.start("y", "spread")
    for chunk in CHUNKS[:2]:
        gather.arrive(*chunk, 1)
        gather.start(*chunk, 2)
    first_on = pass_on(0, first_far)
    for copy in docs:
        copy.wait_recv()
    own_docs = jnp.broadcast_to(r["docs"][seq].astype(F32), (128, 128)).T
    for i in range(4):
        r["bias"][:, 128 * i : 128 * i + 128] = jnp.where(own_docs == r["docs"][i].astype(F32), 0.0, MASKED_SCORE)
    table.finish()
    for y in range(4):
        vec[:, 128 * y : 128 * y + 128] = tab[y]
    gather.swap_start(0, 0)
    for chunk in CHUNKS[2:]:
        gather.arrive(*chunk, 1)
        gather.start(*chunk, 2)
    first_near.wait_recv()
    first_on.wait_recv()
    gather.swap_arrive(0, 0)

    def weight(l, arr, s, low=0, high=None):
        high = WIDTHS[arr] if high is None else high
        return (wa, wm)[arr][l, s // 2, s % 2, :, :, :, :, low:high].reshape(512, high - low)

    def attn_weight(l, q):
        return weight(l, 0, QUARTERS.index(q))

    def put_grad(l, arr, plane, left, right, parts):
        width = WIDTHS[arr] // parts
        for i in range(parts):
            value = mm(left, right(width * i, width * i + width), TN)
            (ga, gm)[arr][l, plane, :, :, :, :, width * i : width * i + width] = value.astype(BF).reshape(
                4, 2, 4, 16, width
            )

    def row(l, k):
        return vec[12 * l + k : 12 * l + k + 1, :]

    def put_row(l, k, value):
        vgrad[12 * l + k : 12 * l + k + 1, :] = value

    lanes = lax.broadcasted_iota(jnp.int32, (1, 128), 1)
    first = (lanes < 64).astype(F32)
    second = 1.0 - first
    first_low, second_low = first.astype(BF), second.astype(BF)

    def both(pair):
        return jnp.concatenate([pair * first_low, pair * second_low], axis=0)

    def joined(stacked):
        return stacked[:128] * first + stacked[128:] * second

    def group_rows(l, which, low):
        return kv[l, which, :, :, low : low + 128].reshape(512, 128)

    def chip_keys(l, chip):
        rows = xall[l, chip].reshape(256, 512)
        kv[l, 0, chip] = mm(rows, attn_weight(l, 1)).astype(BF)
        kv[l, 1, chip] = (mm(rows, attn_weight(l, 2)) + row(l, 1)).astype(BF)

    pairs = r["pairs"]
    hidden = r["tokens"][...].astype(F32)
    for l in range(2):
        low_in = hidden.astype(BF)
        if l == 1:
            xall[1, x_lo, core] = low_in
            near_way, far_way = share(1)
            gather.swap_arrive(1, 0)
        r["q"][l] = (mm(low_in, attn_weight(l, 0)) + row(l, 0)).astype(BF)
        if l == 1:
            near_way.wait_recv()
        chip_keys(l, x_lo)
        if l == 1:
            on_way = pass_on(1, far_way)
            gather.swap_start(1, 1)
            on_way.wait_recv()
        chip_keys(l, 1 - x_lo)
        pairs[l, 0] = xall[l, x_lo]
        for pair in range(4):
            low = 128 * pair
            scores = mm(both(r["q"][l, :, low : low + 128]), group_rows(l, 0, low), NT) * SCALE
            bias = r["bias"][...]
            scores = scores + jnp.concatenate([bias, bias], axis=0)
            powers = jnp.exp(scores - jnp.max(scores, axis=-1, keepdims=True))
            probs = (powers * (1.0 / jnp.sum(powers, axis=-1, keepdims=True))).astype(BF)
            r["probs"][l, pair] = probs
            pairs[l, 1, core, :, low : low + 128] = joined(mm(probs, group_rows(l, 1, low))).astype(BF)
            if l == 0 and pair == 1:
                gather.swap_start(0, 1)
        send(pairs.at[l, 1, core], pairs.at[l, 1, core], "act", (l, 1), near)
        if l == 0:
            gather.swap_arrive(0, 1)
        hat, inverse = normalize(hidden + mm(pairs[l, 1, core], attn_weight(l, 3)) + row(l, 2))
        r["hat1"][l] = hat
        r["inv1"][l] = inverse
        normed = hat * row(l, 3) + row(l, 4)
        low_normed = normed.astype(BF)
        pairs[l, 2, core] = low_normed
        send(pairs.at[l, 2, core], pairs.at[l, 2, core], "act", (l, 2), near)
        back = jnp.zeros((128, 512), F32)
        if l == 1:
            gather.swap_arrive(1, 1)
        for i in range(4):
            half, low = i // 2, 512 * (i % 2)
            pre = mm(low_normed, weight(l, 1, half, low, low + 512)) + row(l, 5 + i)
            normal = 0.5 + 0.5 * lax.erf(pre * (0.5**0.5))
            act = (pre * normal).astype(BF)
            r["act"][l, half, core, :, low : low + 512] = act
            slope = normal + pre * (jnp.exp(pre * pre * -0.5) * (1.0 / (2.0 * math.pi) ** 0.5))
            r["slope"][l, :, 512 * i : 512 * i + 512] = slope.astype(BF)
            back = back + mm(act, weight(l, 1, 2 + half, low, low + 512), NT)
        mine = r["act"].at[l, peer, core]
        send(mine, mine, "act", (l, 3), near)
        if l == 0:
            gather.swap_start(1, 0)
        hat, inverse = normalize(normed + back + row(l, 9))
        r["hat2"][l] = hat
        r["inv2"][l] = inverse
        hidden = hat * row(l, 10) + row(l, 11)
    r["block_out"][...] = hidden.astype(BF)

    scatter = Scatter(place, (ga, gm), slots, r["total"], r["rs_send"], r["rs_recv"])
    dx, dx_near, dx_far, late, early = r["dx"], r["dx_near"], r["dx_far"], r["late"], r["early"]

    def grad_rows(l, chip):
        keys, values = late[l, 0, core, chip].reshape(256, 512), late[l, 1, core, chip].reshape(256, 512)
        part = mm(keys, attn_weight(l, 1), NT) + mm(values, attn_weight(l, 2), NT)
        dx[l, chip] = part.astype(BF).reshape(2, 128, 512)
        return send(dx.at[l, chip, peer], dx_near.at[l, chip], "dx", (l, (chip + x_lo) % 2), near)

    def give_far(l, copy):
        copy.wait_recv()
        mine = dx[l, 1 - x_lo, core].astype(F32) + dx_near[l, 1 - x_lo].astype(F32)
        dx[l, 1 - x_lo, core] = mine.astype(BF)
        return send(dx.at[l, 1 - x_lo, core], dx_far.at[l], "dx", (l, 2), across)

    def act_arrive(l, which):
        if which == 3:
            ref = r["act"].at[l, core, peer]
        else:
            ref = pairs.at[l, which, peer]
        remote(ref, ref, r["act_send"].at[l, which], r["act_recv"].at[l, which], near).wait_recv()

    def two(ref, *index):
        return ref[index].reshape(256, -1)

    def mlp_grads(l, got_second):
        got_second.wait_recv()
        act_arrive(l, 2)
        act_arrive(l, 3)
        theirs = r["du"].at[l, core, peer]
        remote(theirs, theirs, r["back_send"].at[l, 1], r["back_recv"].at[l, 1], near).wait_recv()
        put_grad(l, 1, 0, two(pairs, l, 2), lambda low, high: r["du"][l, core, :, :, low:high].reshape(256, -1), 2)
        put_grad(l, 1, 1, two(pairs, l, 3), lambda low, high: r["act"][l, core, :, :, low:high].reshape(256, -1), 2)
        scatter.step(l, 1, 0)

    s4, fin, total = r["s4"], r["fin"], r["total"]
    moved = []

    def hand_out(l):
        for dst in range(4):
            s4[dst, l] = total[l, 4 * dst : 4 * dst + 4, :]
        for step in (1, 2, 3):
            member, device = place.in_group(step)
            moved.append(send(s4.at[member, l], fin.at[seq, l], "a2a", (l, step), device))
        fin[seq, l] = s4[seq, l]

    grad = r["cotangent"][...].astype(F32)
    for l in (1, 0):
        hat = r["hat2"][l]
        put_row(l, 10, column_sum(grad * hat))
        put_row(l, 11, column_sum(grad))
        grad_second = normalize_back(grad * row(l, 10), hat, r["inv2"][l])
        put_row(l, 9, column_sum(grad_second))
        low_second = grad_second.astype(BF)
        pairs[l, 3, core] = low_second
        got_second = send(pairs.at[l, 3, core], pairs.at[l, 3, core], "back", (l, 0), near)
        grad_normed = grad_second
        for i in range(4):
            half, low = i // 2, 512 * (i % 2)
            grad_act = mm(low_second, weight(l, 1, 2 + half, low, low + 512))
            grad_pre = (grad_act * r["slope"][l, :, 512 * i : 512 * i + 512].astype(F32)).astype(BF)
            put_row(l, 5 + i, column_sum(grad_pre.astype(F32)))
            r["du"][l, half, core, :, low : low + 512] = grad_pre
            grad_normed = grad_normed + mm(grad_pre, weight(l, 1, half, low, low + 512), NT)
        mine = r["du"].at[l, peer, core]
        send(mine, mine, "back", (l, 1), near)
        hat = r["hat1"][l]
        put_row(l, 3, column_sum(grad_normed * hat))
        put_row(l, 4, column_sum(grad_normed))
        grad_first = normalize_back(grad_normed * row(l, 3), hat, r["inv1"][l])
        put_row(l, 2, column_sum(grad_first))
        low_first = grad_first.astype(BF)
        early[l, 1, core] = low_first
        grad_mixed = mm(low_first, attn_weight(l, 3), NT).astype(BF)
        if l == 0:
            scatter.step(1, 1, 1)
            mlp_grads(0, got_second)
        for pair in range(4):
            low = 128 * pair
            keys, values = group_rows(l, 0, low), group_rows(l, 1, low)
            grad_pair = both(grad_mixed[:, low : low + 128])
            probs = r["probs"][l, pair]
            grad_probs = mm(grad_pair, values, NT)
            late[l, 1, core, :, :, low : low + 128] = mm(probs, grad_pair, TN).astype(BF).reshape(2, 256, 128)
            wide = probs.astype(F32)
            row_dot = jnp.sum(grad_probs * wide, axis=-1, keepdims=True)
            grad_scores = (wide * (grad_probs - row_dot)).astype(BF)
            early[l, 0, core, :, low : low + 128] = (joined(mm(grad_scores, keys)) * SCALE).astype(BF)
            grad_keys = mm(grad_scores, both(r["q"][l, :, low : low + 128]), TN) * SCALE
            late[l, 0, core, :, :, low : low + 128] = grad_keys.astype(BF).reshape(2, 256, 128)
            if l == 0 and pair == 1:
                scatter.step(1, 0, 1)
        mine = late.at[l, peer, core]
        send(mine, mine, "back", (l, 3), near)
        mine = early.at[l, peer, core]
        send(mine, mine, "back", (l, 2), near)
        grad_queries = early[l, 0, core]
        put_row(l, 0, column_sum(grad_queries.astype(F32)))
        put_row(l, 1, column_sum(late[l, 1, core].reshape(512, 512).astype(F32)))
        if l == 0:
            for y in range(4):
                r["vtab"][y] = vgrad[:, 128 * y : 128 * y + 128]
            table = Table(place, r["vtab"], r["vgot"].at[1], r["v_send"].at[1], r["v_recv"].at[1])
            table.start("y", "collect")

        def attn_grads():
            act_arrive(l, 1)
            theirs = early.at[l, core, peer]
            remote(theirs, theirs, r["back_send"].at[l, 2], r["back_recv"].at[l, 2], near).wait_recv()
            put_grad(l, 0, 0, two(pairs, l, core), lambda low, high: two(early, l, core), 1)
            theirs = late.at[l, core, peer]
            remote(theirs, theirs, r["back_send"].at[l, 3], r["back_recv"].at[l, 3], near).wait_recv()
            rows = xall[l].reshape(512, 512)
            value = mm(rows, late[l, core, 0].reshape(512, 512), TN) + mm(rows, late[l, core, 1].reshape(512, 512), TN)
            ga[l, 1] = value.astype(BF).reshape(4, 2, 4, 16, 512)
            scatter.step(l, 0, 0)

        if l == 0:
            attn_grads()
        far_near = grad_rows(l, 1 - x_lo)
        own_near = grad_rows(l, x_lo)
        far_way = give_far(l, far_near)
        grad = grad_first + mm(grad_queries, attn_weight(l, 0), NT)
        if l == 1:
            mlp_grads(1, got_second)
            attn_grads()
        else:
            scatter.step(1, 1, 2)
            scatter.step(1, 0, 2)
            table.finish()
            table.start("x")
            scatter.step(0, 1, 1)
            scatter.step(1, 1, 3)
            scatter.step(1, 0, 3)
            hand_out(1)
        own_near.wait_recv()
        far_way.wait_recv()
        grad = grad + dx[l, x_lo, core].astype(F32) + dx_near[l, x_lo].astype(F32) + dx_far[l].astype(F32)
    r["input_grad"][...] = grad
    scatter.step(0, 0, 1)
    table.finish()
    table.start("z")
    scatter.step(0, 1, 2)
    scatter.step(0, 0, 2)
    table.finish()
    table.start("core")
    scatter.step(0, 1, 3)
    scatter.step(0, 0, 3)
    hand_out(0)
    table.finish()
    r["vfin"][...] = pltpu.roll(r["vtab"][place.at["y"]], (128 - 4 * (number % 32)) % 128, 1)
    gather.finish()
    scatter.finish()
    for copy in moved:
        copy.wait_recv()
    for copy in unsent:
        copy.wait_send()


INPUTS = ("tokens", "cotangent", "segments", "w_attn", "w_mlp", "vectors")
OUTPUTS = {
    "block_out": ((128, 512), BF),
    "input_grad": ((128, 512), F32),
    "fin": ((4, 2, 4, 1536), F32),
    "vfin": ((24, 128), F32),
}
DIMS = (2, 2, 2, 4, 2, 4, 16)
HALF = (2, 2, 4, 2, 4, 16)
SCRATCH = {
    "wa": (DIMS + (512,), BF),
    "wm": (DIMS + (1024,), BF),
    "ga": (HALF + (512,), BF),
    "gm": (HALF + (1024,), BF),
    "vec": ((24, 512), F32),
    "vgrad": ((24, 512), F32),
    "tab": ((4, 24, 128), F32),
    "vtab": ((4, 24, 128), F32),
    "t0": ((4, 16, 768), F32),
    "s0": ((4, 16, 768), BF),
    "r0": ((4, 16, 768), BF),
    "s4": ((4, 2, 4, 1536), F32),
    "stage": ((2, 16, 1536), F32),
    "total": ((2, 16, 1536), F32),
    "vgot": ((2, 4, 3, 24, 128), F32),
    "docs": ((4, 1, 128), jnp.int32),
    "bias": ((128, 512), F32),
    "q": ((2, 128, 512), BF),
    "kv": ((2, 2, 2, 256, 512), BF),
    "xall": ((2, 2, 2, 128, 512), BF),
    "probs": ((2, 4, 256, 512), BF),
    "pairs": ((2, 4, 2, 128, 512), BF),
    "act": ((2, 2, 2, 128, 1024), BF),
    "du": ((2, 2, 2, 128, 1024), BF),
    "early": ((2, 2, 2, 128, 512), BF),
    "late": ((2, 2, 2, 2, 256, 512), BF),
    "hat1": ((2, 128, 512), F32),
    "inv1": ((2, 128, 1), F32),
    "slope": ((2, 128, 2048), BF),
    "hat2": ((2, 128, 512), F32),
    "inv2": ((2, 128, 1), F32),
    "dx": ((2, 2, 2, 128, 512), BF),
    "dx_near": ((2, 2, 128, 512), BF),
    "dx_far": ((2, 128, 512), BF),
}
SEMS = {
    "a2a": (3, 4),
    "doc": (4,),
    "ag": (2, 2, 3, 3, 3),
    "sw": (2, 2, 3, 4),
    "rs": (2, 2, 3, 3, 3),
    "x": (2, 3),
    "dx": (2, 3),
    "act": (2, 4),
    "back": (2, 4),
    "v": (2, 4, 3),
}
NAMES = INPUTS + tuple(OUTPUTS) + tuple(SCRATCH) + tuple(f"{n}_{d}" for n in SEMS for d in ("send", "recv"))


def train(*args):
    slots = []
    for phase in range(3):
        for arr in range(2):
            for j in range(3):
                low, high = THIRDS[arr][j]
                rest = dims_of(ORDERS[j][::-1][phase + 1 :])
                slots.append(pltpu.VMEM((2, 3) + rest + (16, high - low), BF))
    scratch = [pltpu.VMEM(*spec) for spec in SCRATCH.values()]
    for shape in SEMS.values():
        scratch += [pltpu.SemaphoreType.DMA(shape)] * 2
    return pl.pallas_call(
        train_kernel,
        out_shape=tuple(jax.ShapeDtypeStruct(*spec) for spec in OUTPUTS.values()),
        in_specs=[pl.BlockSpec(memory_space=pltpu.VMEM)] * len(INPUTS),
        out_specs=[pl.BlockSpec(memory_space=pltpu.VMEM)] * len(OUTPUTS),
        scratch_shapes=scratch + slots,
        compiler_params=pltpu.CompilerParams(
            collective_id=0, has_side_effects=True, vmem_limit_bytes=VMEM_BYTES
        ),
        name="train",
    )(*args)


def adam_update(weight, grad, first, second, rate, decay):
    first_new = BETA_FIRST * first + (1.0 - BETA_FIRST) * grad
    second_new = BETA_SECOND * second + (1.0 - BETA_SECOND) * grad * grad
    first_fix = 1.0 - BETA_FIRST**STEP
    second_fix = 1.0 - BETA_SECOND**STEP
    weight_new = weight - rate * (
        first_new / first_fix / (jnp.sqrt(second_new / second_fix) + ADAM_EPSILON) + decay * weight
    )
    return (first_new, second_new, weight_new)


def adam_kernel(block_in, grad_in, fin, vfin, *refs):
    state, (block_out, grad_out), outs = refs[:9], refs[9:11], refs[11:]
    block_out[...] = block_in[...]
    grad_out[...] = grad_in[...]
    for l in range(2):
        for arr in range(3):
            w, m, v = state[arr], state[3 + arr], state[6 + arr]
            if arr == 2:
                pieces = [(vfin[12 * l : 12 * l + 12, 0:4], slice(0, 4))]
            elif arr == 1:
                pieces = [(fin[s, l, :, 512:1536], slice(1024 * s, 1024 * s + 1024)) for s in range(4)]
            else:
                pieces = [(fin[s, l, :, 0:512], slice(512 * q, 512 * q + 512)) for s, q in enumerate(QUARTERS)]
            rate, decay = (VECTOR_RATE, 0.0) if arr == 2 else (LEARN_RATE, WEIGHT_DECAY)
            for grad, span in pieces:
                new = adam_update(w[l, :, span], grad, m[l, :, span], v[l, :, span], rate, decay)
                for k in range(3):
                    outs[3 * arr + k][l, :, span] = new[k]


def adam(block, grad, fin, vfin, *state):
    shapes = [jax.ShapeDtypeStruct(a.shape, a.dtype) for a in (block, grad)]
    for a in state[:3]:
        shapes += [jax.ShapeDtypeStruct(a.shape, a.dtype)] * 3
    spec = pl.BlockSpec(memory_space=pltpu.VMEM)
    return pl.pallas_call(
        adam_kernel, out_shape=shapes, in_specs=[spec] * 13, out_specs=[spec] * 11, name="adam"
    )(block, grad, fin, vfin, *state)


def local(
    tokens, cotangent, segments, w_attn, w_mlp, vectors, m_attn, m_mlp, m_vec, v_attn, v_mlp, v_vec
):
    made = train(tokens[0], cotangent[0], segments, w_attn, w_mlp, vectors)
    block_out, input_grad, *updated = adam(
        *made, w_attn, w_mlp, vectors, m_attn, m_mlp, m_vec, v_attn, v_mlp, v_vec
    )
    return (block_out[None], input_grad[None], *updated)


def solution(mesh):
    in_specs = (
        P("dp", "seq", None),
        P("dp", "seq", None),
        P("dp", "seq"),
        P(None, ("dp", "seq"), None),
        P(None, ("dp", "seq"), None),
        P(None, None, ("dp", "seq")),
        P(None, ("dp", "seq"), None),
        P(None, ("dp", "seq"), None),
        P(None, None, ("dp", "seq")),
        P(None, ("dp", "seq"), None),
        P(None, ("dp", "seq"), None),
        P(None, None, ("dp", "seq")),
    )
    out_specs = (
        P("dp", "seq", None),
        P("dp", "seq", None),
        P(None, ("dp", "seq"), None),
        P(None, ("dp", "seq"), None),
        P(None, ("dp", "seq"), None),
        P(None, ("dp", "seq"), None),
        P(None, ("dp", "seq"), None),
        P(None, ("dp", "seq"), None),
        P(None, None, ("dp", "seq")),
        P(None, None, ("dp", "seq")),
        P(None, None, ("dp", "seq")),
    )
    return jax.shard_map(local, mesh=mesh, in_specs=in_specs, out_specs=out_specs, check_vma=False)
```

```python
import math

import jax
import jax.numpy as jnp
from jax import lax
from jax.experimental import pallas as pl
from jax.experimental.pallas import tpu as pltpu
from jax.sharding import PartitionSpec as P

STEP = 10
NORM_EPSILON = 1e-06
ADAM_EPSILON = 1e-06
BETA_FIRST = 0.9
BETA_SECOND = 0.999
LEARN_RATE = 0.03
VECTOR_RATE = 0.2
WEIGHT_DECAY = 0.01
MASKED_SCORE = -1e30
VMEM_BYTES = 62 * 2**20
MESH = pl.DeviceIdType.MESH
BF = jnp.bfloat16
F32 = jnp.float32
EVEN = (((0, 128), (128, 256), (256, 512)), ((0, 384), (384, 768), (768, 1024)))
UNEVEN = (((0, 256), (256, 384), (384, 512)), ((0, 384), (384, 640), (640, 1024)))
THIRDS = (EVEN, UNEVEN)
WIDTHS = (512, 1024)
ORDERS = (("x", "y", "z"), ("y", "z", "x"), ("z", "x", "y"))


class Place:
    def __init__(self):
        self.dp = lax.axis_index("dp")
        self.seq = lax.axis_index("seq")
        self.core = self.seq % 2
        self.at = {
            "x": ((self.dp // 4) % 2) * 2 + self.seq // 2,
            "y": self.dp // 8,
            "z": self.dp % 4,
        }

    def device(self, at, core):
        return {
            "dp": (at["y"] * 2 + at["x"] // 2) * 4 + at["z"],
            "seq": (at["x"] % 2) * 2 + core,
        }

    def along(self, axis, step):
        at = dict(self.at)
        at[axis] = (at[axis] + step) % 4
        return at[axis], self.device(at, self.core)

    def other_core(self):
        return self.device(self.at, 1 - self.core)

    def in_group(self, step):
        peer = (self.seq + step) % 4
        return peer, {"dp": self.dp, "seq": peer}


def region(buf, layer, at, core, columns):
    whole = slice(None)
    if "x" in at:
        x_hi, x_lo = at["x"] // 2, at["x"] % 2
    else:
        x_hi, x_lo = whole, whole
    cols = pl.ds(columns[0], columns[1] - columns[0])
    return buf.at[layer, x_lo, core, at.get("y", whole), x_hi, at.get("z", whole), whole, cols]


def greet(place):
    barrier = pltpu.get_barrier_semaphore()
    peers = [place.other_core()]
    for axis in ("x", "y", "z"):
        for step in (1, 2, 3):
            peers.append(place.along(axis, step)[1])
    far = {"dp": place.dp, "seq": (1 - place.seq // 2) * 2 + (1 - place.core)}
    peers.append(far)
    for peer in peers:
        pl.semaphore_signal(barrier, inc=1, device_id=peer, device_id_type=MESH)
    return barrier, len(peers)


def remote(src, dst, send, recv, device):
    return pltpu.make_async_remote_copy(
        src_ref=src, dst_ref=dst, send_sem=send, recv_sem=recv, device_id=device, device_id_type=MESH
    )


class Table:
    ROUNDS = {"core": (0, (1,)), "x": (1, (1, 2, 3)), "y": (2, (1, 2, 3)), "z": (3, (1, 2, 3))}

    def __init__(self, place, blocks, came, send, recv):
        self.place, self.blocks, self.came, self.send, self.recv = place, blocks, came, send, recv
        self.going, self.mode, self.axis = None, None, None

    def start(self, axis, mode="add"):
        number, steps = self.ROUNDS[axis]
        own = self.blocks.at[self.place.at["y"]]
        self.going, self.mode, self.axis = [], mode, axis
        for step in steps:
            if axis == "core":
                device = self.place.other_core()
            else:
                pos, device = self.place.along(axis, step)
            src = self.blocks.at[pos] if mode == "collect" else own
            dst = own if mode == "spread" else self.came.at[number, step - 1]
            copy = remote(src, dst, self.send.at[number, step - 1], self.recv.at[number, step - 1], device)
            copy.start()
            self.going.append(copy)

    def finish(self):
        number, steps = self.ROUNDS[self.axis]
        for copy in self.going:
            copy.wait()
        if self.mode != "spread":
            total = self.blocks[self.place.at["y"]]
            for step in steps:
                total = total + self.came[number, step - 1]
            self.blocks[self.place.at["y"]] = total


def dims_of(axes):
    out = ()
    if "x" in axes:
        out += (2,)
    if "y" in axes:
        out += (4,)
    if "x" in axes:
        out += (2,)
    if "z" in axes:
        out += (4,)
    return out


def each_block(dims, body):
    count = 1
    for size in dims[:-1]:
        count *= size

    def one(i, carry):
        index = ()
        rest = i
        for size in reversed(dims[:-1]):
            index = (rest % size,) + index
            rest = rest // size
        body(index)
        return carry

    if count == 1:
        body(tuple(0 for _ in dims[:-1]))
    else:
        lax.fori_loop(0, count, one, 0)


NT = (((1,), (1,)), ((), ()))
NN = (((1,), (0,)), ((), ()))
TN = (((0,), (0,)), ((), ()))
CHUNKS = ((0, 0), (0, 1), (1, 0), (1, 1))
PIECES = (16, 1536)
SCALE = 0.125
QUARTERS = (0, 3, 1, 2)


def mm(left, right, dims=NN):
    return lax.dot_general(left, right, dims, preferred_element_type=F32)


def column_sum(values):
    return jnp.sum(values, axis=0, keepdims=True)


def normalize(summed):
    center = summed - jnp.mean(summed, axis=-1, keepdims=True)
    spread = jnp.mean(center * center, axis=-1, keepdims=True)
    inverse = lax.rsqrt(spread + NORM_EPSILON)
    return center * inverse, inverse


def normalize_back(grad, hat, inverse):
    mean = jnp.mean(grad, axis=-1, keepdims=True)
    along = jnp.mean(grad * hat, axis=-1, keepdims=True)
    return inverse * (grad - mean - hat * along)


class Gather:
    def __init__(self, place, bufs, send, recv, swap_send, swap_recv):
        self.place, self.bufs = place, bufs
        self.send, self.recv, self.swap_send, self.swap_recv = send, recv, swap_send, swap_recv

    def copies(self, l, arr, phase, coming):
        place = self.place
        out = []
        for j, order in enumerate(ORDERS):
            axis = order[phase]
            here = {a: place.at[a] for a in order[phase:]}
            for step in (1, 2, 3):
                _, device = place.along(axis, step)
                spot = dict(here)
                if coming:
                    spot[axis] = (place.at[axis] - step) % 4
                ref = region(self.bufs[arr], l, spot, place.core, THIRDS[l][arr][j])
                sems = (self.send.at[l, arr, phase, j, step - 1], self.recv.at[l, arr, phase, j, step - 1])
                out.append(remote(ref, ref, *sems, device))
        return out

    def start(self, l, arr, phase):
        for copy in self.copies(l, arr, phase, False):
            copy.start()
        if phase == 2:
            for j in range(3):
                self.swap(l, arr, j, 0).start()

    def arrive(self, l, arr, phase):
        for copy in self.copies(l, arr, phase, True):
            copy.wait_recv()

    def swap(self, l, arr, j, step, coming=False):
        place = self.place
        axis = ORDERS[j][2]
        core = 1 - place.core if coming else place.core
        ref = region(self.bufs[arr], l, {axis: (place.at[axis] - step) % 4}, core, THIRDS[l][arr][j])
        return remote(
            ref, ref, self.swap_send.at[l, arr, j, step], self.swap_recv.at[l, arr, j, step], place.other_core()
        )

    def swap_start(self, l, arr):
        copies = self.copies(l, arr, 2, True)
        for step in (1, 3, 2):
            for j in range(3):
                copies[3 * j + step - 1].wait_recv()
                self.swap(l, arr, j, step).start()

    def swap_arrive(self, l, arr):
        for j in range(3):
            for step in range(4):
                self.swap(l, arr, j, step, True).wait_recv()

    def finish(self):
        for chunk in CHUNKS:
            for phase in range(3):
                for copy in self.copies(*chunk, phase, False):
                    copy.wait_send()
            for j in range(3):
                for step in range(4):
                    self.swap(*chunk, j, step).wait_send()


class Scatter:
    def __init__(self, place, bufs, slots, total, send, recv):
        self.place, self.bufs, self.slots, self.total, self.send, self.recv = place, bufs, slots, total, send, recv

    def slot(self, l, phase, arr, j):
        return self.slots[((l * 3 + phase) * 2 + arr) * 3 + j]

    def part(self, l, arr, at, j):
        whole = slice(None)
        x_hi, x_lo = (at["x"] // 2, at["x"] % 2) if "x" in at else (whole, whole)
        low, high = THIRDS[l][arr][j]
        return self.bufs[arr].at[
            l, x_lo, at.get("y", whole), x_hi, at.get("z", whole), whole, pl.ds(low, high - low)
        ]

    def copies(self, l, arr, phase):
        place = self.place
        out = []
        for j, order in enumerate(ORDERS):
            rev = order[::-1]
            for step in (1, 2, 3):
                there = {a: place.at[a] for a in rev[:phase]}
                there[rev[phase]], device = place.along(rev[phase], step)
                dst = self.slot(l, phase, arr, j).at[step - 1]
                sems = (self.send.at[l, arr, phase, j, step - 1], self.recv.at[l, arr, phase, j, step - 1])
                out.append(remote(self.part(l, arr, there, j), dst, *sems, device))
        return out

    def add_up(self, l, arr, phase):
        for j, order in enumerate(ORDERS):
            rev = order[::-1]
            own = self.part(l, arr, {a: self.place.at[a] for a in rev[: phase + 1]}, j)
            came = self.slot(l, phase, arr, j)
            if phase == 2:
                low, high = THIRDS[l][arr][j]
                total = own[...].astype(F32)
                for k in range(3):
                    total = total + came[k].astype(F32)
                self.total[l, :, 512 * arr + low : 512 * arr + high] = total
                continue

            def body(index, own=own, came=came):
                total = own[index].astype(F32)
                for k in range(3):
                    total = total + came[(k,) + index].astype(F32)
                own[index] = total.astype(BF)

            each_block(dims_of(rev[phase + 1 :]), body)

    def step(self, l, arr, stage):
        if stage > 0:
            for copy in self.copies(l, arr, stage - 1):
                copy.wait_recv()
            self.add_up(l, arr, stage - 1)
        if stage < 3:
            for copy in self.copies(l, arr, stage):
                copy.start()

    def finish(self):
        for chunk in CHUNKS:
            for phase in range(3):
                for copy in self.copies(*chunk, phase):
                    copy.wait_send()


def train_kernel(*refs):
    r = dict(zip(NAMES, refs[: len(NAMES)]))
    slots = refs[len(NAMES) :]
    place = Place()
    seq, core, x_lo = place.seq, place.core, place.seq // 2
    peer = 1 - core
    near = place.other_core()
    across = {"dp": place.dp, "seq": (1 - x_lo) * 2 + core}
    wa, wm, ga, gm, vec, vgrad = r["wa"], r["wm"], r["ga"], r["gm"], r["vec"], r["vgrad"]
    s0, r0, stage, kv = r["s0"], r["r0"], r["stage"], r["kv"]
    unsent = []

    def send(src, dst, sem, index, device):
        copy = remote(src, dst, r[sem + "_send"].at[index], r[sem + "_recv"].at[index], device)
        copy.start()
        unsent.append(copy)
        return copy

    greeted = greet(place)
    t0 = r["t0"]
    for s, q in enumerate(QUARTERS):
        for l in range(2):
            t0[s, 8 * l : 8 * l + 4, 0:512] = r["w_attn"][l, :, 512 * q : 512 * q + 512]
            t0[s, 8 * l : 8 * l + 4, 512:768] = r["w_mlp"][l, :, 1024 * s : 1024 * s + 256]
            t0[s, 8 * l + 4 : 8 * l + 8, :] = r["w_mlp"][l, :, 1024 * s + 256 : 1024 * s + 1024]
    s0[...] = t0[...].astype(BF)
    tab = r["tab"]
    number = place.dp * 4 + seq
    square = r["square"]
    square[...] = jnp.zeros((128, 128), F32)
    for l in range(2):
        square[0:4, 0:12] = r["vectors"][l].astype(BF).astype(F32)
        tab[place.at["y"], 12 * l : 12 * l + 12, :] = square[...].T[0:12, :]
    tab[place.at["y"]] = pltpu.roll(tab[place.at["y"]], 4 * (number % 32), 1)
    r["docs"][seq] = r["segments"][...]
    xall = r["xall"]
    xall[0, x_lo, core] = r["tokens"][...]
    pl.semaphore_wait(*greeted)

    pieces, docs = [], []
    for step in (1, 2, 3):
        member, device = place.in_group(step)
        pieces.append(send(s0.at[member], r0.at[seq], "a2a", (2, step), device))
    table = Table(place, tab, r["vgot"].at[0], r["v_send"].at[0], r["v_recv"].at[0])
    table.start("core")
    for step in (1, 2, 3):
        member, device = place.in_group(step)
        docs.append(send(r["docs"].at[seq], r["docs"].at[seq], "doc", step, device))
    r0[seq] = s0[seq]
    for copy in pieces:
        copy.wait_recv()
    for src in range(4):
        t0[src] = r0[src].astype(F32)
        for l in range(2):
            stage[l, 4 * src : 4 * src + 4, 0:768] = t0[src, 8 * l : 8 * l + 4, :]
            stage[l, 4 * src : 4 * src + 4, 768:1536] = t0[src, 8 * l + 4 : 8 * l + 8, :]
    at = place.at
    for l, arr in CHUNKS:
        block = stage[l, :, 512 * arr : 512 * arr + WIDTHS[arr]].astype(BF)
        (wa, wm)[arr][l, at["x"] % 2, core, at["y"], at["x"] // 2, at["z"]] = block
    gather = Gather(place, (wa, wm), r["ag_send"], r["ag_recv"], r["sw_send"], r["sw_recv"])
    table.finish()
    table.start("x")
    for chunk in CHUNKS:
        gather.start(*chunk, 0)

    def share(l):
        mine = xall.at[l, x_lo, core]
        near_way = send(mine, mine, "x", (l, 0), near)
        return near_way, send(mine, mine, "x", (l, 1), across)

    def pass_on(l, far_way):
        far_way.wait_recv()
        came = xall.at[l, 1 - x_lo, core]
        return send(came, came, "x", (l, 2), near)

    for chunk in CHUNKS[:2]:
        gather.arrive(*chunk, 0)
        gather.start(*chunk, 1)
    table.finish()
    table.start("z")
    gather.arrive(0, 0, 1)
    gather.start(0, 0, 2)
    table.finish()
    table.start("y", "spread")
    first_near, first_far = share(0)
    gather.arrive(0, 1, 1)
    gather.start(0, 1, 2)
    for chunk in CHUNKS[2:]:
        gather.arrive(*chunk, 0)
        gather.start(*chunk, 1)
    for copy in docs:
        copy.wait_recv()
    own_docs = jnp.broadcast_to(r["docs"][seq].astype(F32), (128, 128)).T
    for i in range(4):
        r["bias"][:, 128 * i : 128 * i + 128] = jnp.where(own_docs == r["docs"][i].astype(F32), 0.0, MASKED_SCORE)
    table.finish()
    for y in range(4):
        vec[:, 128 * y : 128 * y + 128] = tab[y]
    gather.swap_start(0, 0)
    first_on = pass_on(0, first_far)
    for chunk in CHUNKS[2:]:
        gather.arrive(*chunk, 1)
        gather.start(*chunk, 2)
    first_near.wait_recv()
    first_on.wait_recv()
    gather.swap_arrive(0, 0)

    def weight(l, arr, s, low=0, high=None):
        high = WIDTHS[arr] if high is None else high
        return (wa, wm)[arr][l, s // 2, s % 2, :, :, :, :, low:high].reshape(512, high - low)

    def attn_weight(l, q):
        return weight(l, 0, QUARTERS.index(q))

    def put_grad(l, arr, plane, left, right, parts):
        width = WIDTHS[arr] // parts
        for i in range(parts):
            value = mm(left, right(width * i, width * i + width), TN)
            (ga, gm)[arr][l, plane, :, :, :, :, width * i : width * i + width] = value.astype(BF).reshape(
                4, 2, 4, 16, width
            )

    def row(l, k):
        return vec[12 * l + k : 12 * l + k + 1, :]

    def put_row(l, k, value):
        vgrad[12 * l + k : 12 * l + k + 1, :] = value

    lanes = lax.broadcasted_iota(jnp.int32, (1, 128), 1)
    first = (lanes < 64).astype(F32)
    second = 1.0 - first
    first_low, second_low = first.astype(BF), second.astype(BF)

    def both(pair):
        return jnp.concatenate([pair * first_low, pair * second_low], axis=0)

    def joined(stacked):
        return stacked[:128] * first + stacked[128:] * second

    def group_rows(l, which, low):
        return kv[l, which, :, :, low : low + 128].reshape(512, 128)

    def chip_keys(l, chip):
        rows = xall[l, chip].reshape(256, 512)
        kv[l, 0, chip] = mm(rows, attn_weight(l, 1)).astype(BF)
        kv[l, 1, chip] = (mm(rows, attn_weight(l, 2)) + row(l, 1)).astype(BF)

    pairs = r["pairs"]
    hidden = r["tokens"][...].astype(F32)
    for l in range(2):
        low_in = hidden.astype(BF)
        if l == 1:
            xall[1, x_lo, core] = low_in
            near_way, far_way = share(1)
            gather.swap_arrive(1, 0)
        r["q"][l] = (mm(low_in, attn_weight(l, 0)) + row(l, 0)).astype(BF)
        if l == 1:
            near_way.wait_recv()
        chip_keys(l, x_lo)
        if l == 1:
            on_way = pass_on(1, far_way)
            gather.swap_start(1, 1)
            on_way.wait_recv()
        chip_keys(l, 1 - x_lo)
        pairs[l, 0] = xall[l, x_lo]
        for pair in range(4):
            low = 128 * pair
            scores = mm(both(r["q"][l, :, low : low + 128]), group_rows(l, 0, low), NT) * SCALE
            bias = r["bias"][...]
            scores = scores + jnp.concatenate([bias, bias], axis=0)
            powers = jnp.exp(scores - jnp.max(scores, axis=-1, keepdims=True))
            probs = (powers * (1.0 / jnp.sum(powers, axis=-1, keepdims=True))).astype(BF)
            r["probs"][l, pair] = probs
            pairs[l, 1, core, :, low : low + 128] = joined(mm(probs, group_rows(l, 1, low))).astype(BF)
            if l == 0 and pair == 1:
                gather.swap_start(0, 1)
        send(pairs.at[l, 1, core], pairs.at[l, 1, core], "act", (l, 1), near)
        if l == 0:
            gather.swap_arrive(0, 1)
        hat, inverse = normalize(hidden + mm(pairs[l, 1, core], attn_weight(l, 3)) + row(l, 2))
        r["hat1"][l] = hat
        r["inv1"][l] = inverse
        normed = hat * row(l, 3) + row(l, 4)
        low_normed = normed.astype(BF)
        pairs[l, 2, core] = low_normed
        send(pairs.at[l, 2, core], pairs.at[l, 2, core], "act", (l, 2), near)
        back = jnp.zeros((128, 512), F32)
        if l == 1:
            gather.swap_arrive(1, 1)
        for i in range(4):
            half, low = i // 2, 512 * (i % 2)
            pre = mm(low_normed, weight(l, 1, half, low, low + 512)) + row(l, 5 + i)
            normal = 0.5 + 0.5 * lax.erf(pre * (0.5**0.5))
            act = (pre * normal).astype(BF)
            r["act"][l, half, core, :, low : low + 512] = act
            slope = normal + pre * (jnp.exp(pre * pre * -0.5) * (1.0 / (2.0 * math.pi) ** 0.5))
            r["slope"][l, :, 512 * i : 512 * i + 512] = slope.astype(BF)
            back = back + mm(act, weight(l, 1, 2 + half, low, low + 512), NT)
        mine = r["act"].at[l, peer, core]
        send(mine, mine, "act", (l, 3), near)
        if l == 0:
            gather.swap_start(1, 0)
        hat, inverse = normalize(normed + back + row(l, 9))
        r["hat2"][l] = hat
        r["inv2"][l] = inverse
        hidden = hat * row(l, 10) + row(l, 11)
    r["block_out"][...] = hidden.astype(BF)

    scatter = Scatter(place, (ga, gm), slots, r["total"], r["rs_send"], r["rs_recv"])
    dx, dx_near, dx_far, late, early = r["dx"], r["dx_near"], r["dx_far"], r["late"], r["early"]

    def grad_rows(l, chip):
        keys, values = late[l, 0, core, chip].reshape(256, 512), late[l, 1, core, chip].reshape(256, 512)
        part = mm(keys, attn_weight(l, 1), NT) + mm(values, attn_weight(l, 2), NT)
        dx[l, chip] = part.astype(BF).reshape(2, 128, 512)
        return send(dx.at[l, chip, peer], dx_near.at[l, chip], "dx", (l, (chip + x_lo) % 2), near)

    def give_far(l, copy):
        copy.wait_recv()
        mine = dx[l, 1 - x_lo, core].astype(F32) + dx_near[l, 1 - x_lo].astype(F32)
        dx[l, 1 - x_lo, core] = mine.astype(BF)
        return send(dx.at[l, 1 - x_lo, core], dx_far.at[l], "dx", (l, 2), across)

    def act_arrive(l, which):
        if which == 3:
            ref = r["act"].at[l, core, peer]
        else:
            ref = pairs.at[l, which, peer]
        remote(ref, ref, r["act_send"].at[l, which], r["act_recv"].at[l, which], near).wait_recv()

    def two(ref, *index):
        return ref[index].reshape(256, -1)

    def mlp_grads(l, got_second):
        got_second.wait_recv()
        act_arrive(l, 2)
        act_arrive(l, 3)
        theirs = r["du"].at[l, core, peer]
        remote(theirs, theirs, r["back_send"].at[l, 1], r["back_recv"].at[l, 1], near).wait_recv()
        put_grad(l, 1, 0, two(pairs, l, 2), lambda low, high: r["du"][l, core, :, :, low:high].reshape(256, -1), 2)
        put_grad(l, 1, 1, two(pairs, l, 3), lambda low, high: r["act"][l, core, :, :, low:high].reshape(256, -1), 2)
        scatter.step(l, 1, 0)

    s4, fin, total = r["s4"], r["fin"], r["total"]
    moved = []

    def hand_out(l):
        for dst in range(4):
            s4[dst, l] = total[l, 4 * dst : 4 * dst + 4, :]
        for step in (1, 2, 3):
            member, device = place.in_group(step)
            moved.append(send(s4.at[member, l], fin.at[seq, l], "a2a", (l, step), device))
        fin[seq, l] = s4[seq, l]

    grad = r["cotangent"][...].astype(F32)
    for l in (1, 0):
        hat = r["hat2"][l]
        put_row(l, 10, column_sum(grad * hat))
        put_row(l, 11, column_sum(grad))
        grad_second = normalize_back(grad * row(l, 10), hat, r["inv2"][l])
        put_row(l, 9, column_sum(grad_second))
        low_second = grad_second.astype(BF)
        pairs[l, 3, core] = low_second
        got_second = send(pairs.at[l, 3, core], pairs.at[l, 3, core], "back", (l, 0), near)
        grad_normed = grad_second
        for i in range(4):
            half, low = i // 2, 512 * (i % 2)
            grad_act = mm(low_second, weight(l, 1, 2 + half, low, low + 512))
            grad_pre = (grad_act * r["slope"][l, :, 512 * i : 512 * i + 512].astype(F32)).astype(BF)
            put_row(l, 5 + i, column_sum(grad_pre.astype(F32)))
            r["du"][l, half, core, :, low : low + 512] = grad_pre
            grad_normed = grad_normed + mm(grad_pre, weight(l, 1, half, low, low + 512), NT)
        mine = r["du"].at[l, peer, core]
        send(mine, mine, "back", (l, 1), near)
        hat = r["hat1"][l]
        put_row(l, 3, column_sum(grad_normed * hat))
        put_row(l, 4, column_sum(grad_normed))
        grad_first = normalize_back(grad_normed * row(l, 3), hat, r["inv1"][l])
        put_row(l, 2, column_sum(grad_first))
        low_first = grad_first.astype(BF)
        early[l, 1, core] = low_first
        grad_mixed = mm(low_first, attn_weight(l, 3), NT).astype(BF)
        if l == 0:
            scatter.step(1, 1, 1)
            mlp_grads(0, got_second)
        for pair in range(4):
            low = 128 * pair
            keys, values = group_rows(l, 0, low), group_rows(l, 1, low)
            grad_pair = both(grad_mixed[:, low : low + 128])
            probs = r["probs"][l, pair]
            grad_probs = mm(grad_pair, values, NT)
            late[l, 1, core, :, :, low : low + 128] = mm(probs, grad_pair, TN).astype(BF).reshape(2, 256, 128)
            wide = probs.astype(F32)
            row_dot = jnp.sum(grad_probs * wide, axis=-1, keepdims=True)
            grad_scores = (wide * (grad_probs - row_dot)).astype(BF)
            early[l, 0, core, :, low : low + 128] = (joined(mm(grad_scores, keys)) * SCALE).astype(BF)
            grad_keys = mm(grad_scores, both(r["q"][l, :, low : low + 128]), TN) * SCALE
            late[l, 0, core, :, :, low : low + 128] = grad_keys.astype(BF).reshape(2, 256, 128)
            if l == 0 and pair == 1:
                scatter.step(1, 0, 1)
        mine = late.at[l, peer, core]
        send(mine, mine, "back", (l, 3), near)
        mine = early.at[l, peer, core]
        send(mine, mine, "back", (l, 2), near)
        grad_queries = early[l, 0, core]
        put_row(l, 0, column_sum(grad_queries.astype(F32)))
        put_row(l, 1, column_sum(late[l, 1, core].reshape(512, 512).astype(F32)))
        if l == 0:
            for y in range(4):
                r["vtab"][y] = vgrad[:, 128 * y : 128 * y + 128]
            table = Table(place, r["vtab"], r["vgot"].at[1], r["v_send"].at[1], r["v_recv"].at[1])
            table.start("y", "collect")

        def attn_grads():
            act_arrive(l, 1)
            theirs = early.at[l, core, peer]
            remote(theirs, theirs, r["back_send"].at[l, 2], r["back_recv"].at[l, 2], near).wait_recv()
            put_grad(l, 0, 0, two(pairs, l, core), lambda low, high: two(early, l, core), 1)
            theirs = late.at[l, core, peer]
            remote(theirs, theirs, r["back_send"].at[l, 3], r["back_recv"].at[l, 3], near).wait_recv()
            rows = xall[l].reshape(512, 512)
            value = mm(rows, late[l, core, 0].reshape(512, 512), TN) + mm(rows, late[l, core, 1].reshape(512, 512), TN)
            ga[l, 1] = value.astype(BF).reshape(4, 2, 4, 16, 512)
            scatter.step(l, 0, 0)

        if l == 0:
            attn_grads()
        far_near = grad_rows(l, 1 - x_lo)
        own_near = grad_rows(l, x_lo)
        far_way = give_far(l, far_near)
        grad = grad_first + mm(grad_queries, attn_weight(l, 0), NT)
        if l == 1:
            mlp_grads(1, got_second)
            attn_grads()
        else:
            scatter.step(1, 1, 2)
            scatter.step(1, 0, 2)
            table.finish()
            table.start("x")
            scatter.step(0, 1, 1)
            scatter.step(1, 1, 3)
            scatter.step(1, 0, 3)
            hand_out(1)
        own_near.wait_recv()
        far_way.wait_recv()
        grad = grad + dx[l, x_lo, core].astype(F32) + dx_near[l, x_lo].astype(F32) + dx_far[l].astype(F32)
    r["input_grad"][...] = grad
    scatter.step(0, 0, 1)
    table.finish()
    table.start("z")
    scatter.step(0, 1, 2)
    scatter.step(0, 0, 2)
    table.finish()
    table.start("core")
    scatter.step(0, 1, 3)
    scatter.step(0, 0, 3)
    hand_out(0)
    table.finish()
    r["vtab"][place.at["y"]] = pltpu.roll(r["vtab"][place.at["y"]], (128 - 4 * (number % 32)) % 128, 1)
    for l in range(2):
        square[0:12, :] = r["vtab"][place.at["y"], 12 * l : 12 * l + 12, :]
        r["vfin"][l] = square[...].T[0:8, :]
    gather.finish()
    scatter.finish()
    for copy in moved:
        copy.wait_recv()
    for copy in unsent:
        copy.wait_send()


INPUTS = ("tokens", "cotangent", "segments", "w_attn", "w_mlp", "vectors")
OUTPUTS = {
    "block_out": ((128, 512), BF),
    "input_grad": ((128, 512), F32),
    "fin": ((4, 2, 4, 1536), F32),
    "vfin": ((2, 8, 128), F32),
}
DIMS = (2, 2, 2, 4, 2, 4, 16)
HALF = (2, 2, 4, 2, 4, 16)
SCRATCH = {
    "wa": (DIMS + (512,), BF),
    "wm": (DIMS + (1024,), BF),
    "ga": (HALF + (512,), BF),
    "gm": (HALF + (1024,), BF),
    "vec": ((24, 512), F32),
    "vgrad": ((24, 512), F32),
    "tab": ((4, 24, 128), F32),
    "vtab": ((4, 24, 128), F32),
    "t0": ((4, 16, 768), F32),
    "square": ((128, 128), F32),
    "s0": ((4, 16, 768), BF),
    "r0": ((4, 16, 768), BF),
    "s4": ((4, 2, 4, 1536), F32),
    "stage": ((2, 16, 1536), F32),
    "total": ((2, 16, 1536), F32),
    "vgot": ((2, 4, 3, 24, 128), F32),
    "docs": ((4, 1, 128), jnp.int32),
    "bias": ((128, 512), F32),
    "q": ((2, 128, 512), BF),
    "kv": ((2, 2, 2, 256, 512), BF),
    "xall": ((2, 2, 2, 128, 512), BF),
    "probs": ((2, 4, 256, 512), BF),
    "pairs": ((2, 4, 2, 128, 512), BF),
    "act": ((2, 2, 2, 128, 1024), BF),
    "du": ((2, 2, 2, 128, 1024), BF),
    "early": ((2, 2, 2, 128, 512), BF),
    "late": ((2, 2, 2, 2, 256, 512), BF),
    "hat1": ((2, 128, 512), F32),
    "inv1": ((2, 128, 1), F32),
    "slope": ((2, 128, 2048), BF),
    "hat2": ((2, 128, 512), F32),
    "inv2": ((2, 128, 1), F32),
    "dx": ((2, 2, 2, 128, 512), BF),
    "dx_near": ((2, 2, 128, 512), BF),
    "dx_far": ((2, 128, 512), BF),
}
SEMS = {
    "a2a": (3, 4),
    "doc": (4,),
    "ag": (2, 2, 3, 3, 3),
    "sw": (2, 2, 3, 4),
    "rs": (2, 2, 3, 3, 3),
    "x": (2, 3),
    "dx": (2, 3),
    "act": (2, 4),
    "back": (2, 4),
    "v": (2, 4, 3),
}
NAMES = INPUTS + tuple(OUTPUTS) + tuple(SCRATCH) + tuple(f"{n}_{d}" for n in SEMS for d in ("send", "recv"))


def train(*args):
    slots = []
    for l in range(2):
        for phase in range(3):
            for arr in range(2):
                for j in range(3):
                    low, high = THIRDS[l][arr][j]
                    rest = dims_of(ORDERS[j][::-1][phase + 1 :])
                    slots.append(pltpu.VMEM((3,) + rest + (16, high - low), BF))
    scratch = [pltpu.VMEM(*spec) for spec in SCRATCH.values()]
    for shape in SEMS.values():
        scratch += [pltpu.SemaphoreType.DMA(shape)] * 2
    return pl.pallas_call(
        train_kernel,
        out_shape=tuple(jax.ShapeDtypeStruct(*spec) for spec in OUTPUTS.values()),
        in_specs=[pl.BlockSpec(memory_space=pltpu.VMEM)] * len(INPUTS),
        out_specs=[pl.BlockSpec(memory_space=pltpu.VMEM)] * len(OUTPUTS),
        scratch_shapes=scratch + slots,
        compiler_params=pltpu.CompilerParams(
            collective_id=0, has_side_effects=True, vmem_limit_bytes=VMEM_BYTES
        ),
        name="train",
    )(*args)


def adam_update(weight, grad, first, second, rate, decay):
    first_new = BETA_FIRST * first + (1.0 - BETA_FIRST) * grad
    second_new = BETA_SECOND * second + (1.0 - BETA_SECOND) * grad * grad
    first_fix = 1.0 - BETA_FIRST**STEP
    second_fix = 1.0 - BETA_SECOND**STEP
    weight_new = weight - rate * (
        first_new / first_fix / (jnp.sqrt(second_new / second_fix) + ADAM_EPSILON) + decay * weight
    )
    return (first_new, second_new, weight_new)


def adam_kernel(block_in, grad_in, fin, vfin, *refs):
    state, (block_out, grad_out), outs = refs[:9], refs[9:11], refs[11:]
    block_out[...] = block_in[...]
    grad_out[...] = grad_in[...]
    for l in range(2):
        for arr in range(3):
            w, m, v = state[arr], state[3 + arr], state[6 + arr]
            if arr == 2:
                pieces = [(vfin[l, 0:4, 0:12], slice(0, 12))]
            elif arr == 1:
                pieces = [(fin[s, l, :, 512:1536], slice(1024 * s, 1024 * s + 1024)) for s in range(4)]
            else:
                pieces = [(fin[s, l, :, 0:512], slice(512 * q, 512 * q + 512)) for s, q in enumerate(QUARTERS)]
            rate, decay = (VECTOR_RATE, 0.0) if arr == 2 else (LEARN_RATE, WEIGHT_DECAY)
            for grad, span in pieces:
                new = adam_update(w[l, :, span], grad, m[l, :, span], v[l, :, span], rate, decay)
                for k in range(3):
                    outs[3 * arr + k][l, :, span] = new[k]


def adam(block, grad, fin, vfin, *state):
    shapes = [jax.ShapeDtypeStruct(a.shape, a.dtype) for a in (block, grad)]
    for a in state[:3]:
        shapes += [jax.ShapeDtypeStruct(a.shape, a.dtype)] * 3
    spec = pl.BlockSpec(memory_space=pltpu.VMEM)
    return pl.pallas_call(
        adam_kernel, out_shape=shapes, in_specs=[spec] * 13, out_specs=[spec] * 11, name="adam"
    )(block, grad, fin, vfin, *state)


def local(
    tokens, cotangent, segments, w_attn, w_mlp, vectors, m_attn, m_mlp, m_vec, v_attn, v_mlp, v_vec
):
    vectors, m_vec, v_vec = (a.transpose(0, 2, 1) for a in (vectors, m_vec, v_vec))
    made = train(tokens[0], cotangent[0], segments, w_attn, w_mlp, vectors)
    block_out, input_grad, *updated = adam(
        *made, w_attn, w_mlp, vectors, m_attn, m_mlp, m_vec, v_attn, v_mlp, v_vec
    )
    return (block_out[None], input_grad[None], *updated[:6], *(a.transpose(0, 2, 1) for a in updated[6:]))


def solution(mesh):
    in_specs = (
        P("dp", "seq", None),
        P("dp", "seq", None),
        P("dp", "seq"),
        P(None, ("dp", "seq"), None),
        P(None, ("dp", "seq"), None),
        P(None, None, ("dp", "seq")),
        P(None, ("dp", "seq"), None),
        P(None, ("dp", "seq"), None),
        P(None, None, ("dp", "seq")),
        P(None, ("dp", "seq"), None),
        P(None, ("dp", "seq"), None),
        P(None, None, ("dp", "seq")),
    )
    out_specs = (
        P("dp", "seq", None),
        P("dp", "seq", None),
        P(None, ("dp", "seq"), None),
        P(None, ("dp", "seq"), None),
        P(None, ("dp", "seq"), None),
        P(None, ("dp", "seq"), None),
        P(None, ("dp", "seq"), None),
        P(None, ("dp", "seq"), None),
        P(None, None, ("dp", "seq")),
        P(None, None, ("dp", "seq")),
        P(None, None, ("dp", "seq")),
    )
    return jax.shard_map(local, mesh=mesh, in_specs=in_specs, out_specs=out_specs, check_vma=False)
```

```python
import math

import jax
import jax.numpy as jnp
from jax import lax
from jax.experimental import pallas as pl
from jax.experimental.pallas import tpu as pltpu
from jax.sharding import PartitionSpec as P

STEP = 10
NORM_EPSILON = 1e-06
ADAM_EPSILON = 1e-06
BETA_FIRST = 0.9
BETA_SECOND = 0.999
LEARN_RATE = 0.03
VECTOR_RATE = 0.2
WEIGHT_DECAY = 0.01
MASKED_SCORE = -1e30
VMEM_BYTES = 62 * 2**20
MESH = pl.DeviceIdType.MESH
BF = jnp.bfloat16
F32 = jnp.float32
EVEN = (((0, 128), (128, 256), (256, 512)), ((0, 384), (384, 768), (768, 1024)))
UNEVEN = (((0, 256), (256, 384), (384, 512)), ((0, 384), (384, 640), (640, 1024)))
THIRDS = (EVEN, UNEVEN)
WIDTHS = (512, 1024)
ORDERS = (("x", "y", "z"), ("y", "z", "x"), ("z", "x", "y"))


class Place:
    def __init__(self):
        self.dp = lax.axis_index("dp")
        self.seq = lax.axis_index("seq")
        self.core = self.seq % 2
        self.at = {
            "x": ((self.dp // 4) % 2) * 2 + self.seq // 2,
            "y": self.dp // 8,
            "z": self.dp % 4,
        }

    def device(self, at, core):
        return {
            "dp": (at["y"] * 2 + at["x"] // 2) * 4 + at["z"],
            "seq": (at["x"] % 2) * 2 + core,
        }

    def along(self, axis, step):
        at = dict(self.at)
        at[axis] = (at[axis] + step) % 4
        return at[axis], self.device(at, self.core)

    def other_core(self):
        return self.device(self.at, 1 - self.core)

    def in_group(self, step):
        peer = (self.seq + step) % 4
        return peer, {"dp": self.dp, "seq": peer}


def region(buf, layer, at, core, columns):
    whole = slice(None)
    if "x" in at:
        x_hi, x_lo = at["x"] // 2, at["x"] % 2
    else:
        x_hi, x_lo = whole, whole
    cols = pl.ds(columns[0], columns[1] - columns[0])
    return buf.at[layer, x_lo, core, at.get("y", whole), x_hi, at.get("z", whole), whole, cols]


def greet(place):
    barrier = pltpu.get_barrier_semaphore()
    peers = [place.other_core()]
    for axis in ("x", "y", "z"):
        for step in (1, 2, 3):
            peers.append(place.along(axis, step)[1])
    far = {"dp": place.dp, "seq": (1 - place.seq // 2) * 2 + (1 - place.core)}
    peers.append(far)
    for peer in peers:
        pl.semaphore_signal(barrier, inc=1, device_id=peer, device_id_type=MESH)
    return barrier, len(peers)


def remote(src, dst, send, recv, device):
    return pltpu.make_async_remote_copy(
        src_ref=src, dst_ref=dst, send_sem=send, recv_sem=recv, device_id=device, device_id_type=MESH
    )


class Table:
    ROUNDS = {"core": (0, (1,)), "x": (1, (1, 2, 3)), "y": (2, (1, 2, 3)), "z": (3, (1, 2, 3))}

    def __init__(self, place, blocks, came, send, recv):
        self.place, self.blocks, self.came, self.send, self.recv = place, blocks, came, send, recv
        self.going, self.mode, self.axis = None, None, None

    def start(self, axis, mode="add"):
        number, steps = self.ROUNDS[axis]
        own = self.blocks.at[self.place.at["y"]]
        self.going, self.mode, self.axis = [], mode, axis
        for step in steps:
            if axis == "core":
                device = self.place.other_core()
            else:
                pos, device = self.place.along(axis, step)
            src = self.blocks.at[pos] if mode == "collect" else own
            dst = own if mode == "spread" else self.came.at[number, step - 1]
            copy = remote(src, dst, self.send.at[number, step - 1], self.recv.at[number, step - 1], device)
            copy.start()
            self.going.append(copy)

    def finish(self):
        number, steps = self.ROUNDS[self.axis]
        for copy in self.going:
            copy.wait()
        if self.mode != "spread":
            total = self.blocks[self.place.at["y"]]
            for step in steps:
                total = total + self.came[number, step - 1]
            self.blocks[self.place.at["y"]] = total


def dims_of(axes):
    out = ()
    if "x" in axes:
        out += (2,)
    if "y" in axes:
        out += (4,)
    if "x" in axes:
        out += (2,)
    if "z" in axes:
        out += (4,)
    return out


def each_block(dims, body):
    count = 1
    for size in dims[:-1]:
        count *= size

    def one(i, carry):
        index = ()
        rest = i
        for size in reversed(dims[:-1]):
            index = (rest % size,) + index
            rest = rest // size
        body(index)
        return carry

    if count == 1:
        body(tuple(0 for _ in dims[:-1]))
    else:
        lax.fori_loop(0, count, one, 0)


NT = (((1,), (1,)), ((), ()))
NN = (((1,), (0,)), ((), ()))
TN = (((0,), (0,)), ((), ()))
CHUNKS = ((0, 0), (0, 1), (1, 0), (1, 1))
PIECES = (16, 1536)
SCALE = 0.125
QUARTERS = (0, 3, 1, 2)


def mm(left, right, dims=NN):
    return lax.dot_general(left, right, dims, preferred_element_type=F32)


def column_sum(values):
    return jnp.sum(values, axis=0, keepdims=True)


def normalize(summed):
    center = summed - jnp.mean(summed, axis=-1, keepdims=True)
    spread = jnp.mean(center * center, axis=-1, keepdims=True)
    inverse = lax.rsqrt(spread + NORM_EPSILON)
    return center * inverse, inverse


def normalize_back(grad, hat, inverse):
    mean = jnp.mean(grad, axis=-1, keepdims=True)
    along = jnp.mean(grad * hat, axis=-1, keepdims=True)
    return inverse * (grad - mean - hat * along)


class Gather:
    def __init__(self, place, bufs, send, recv, swap_send, swap_recv):
        self.place, self.bufs = place, bufs
        self.send, self.recv, self.swap_send, self.swap_recv = send, recv, swap_send, swap_recv

    def copies(self, l, arr, phase, coming):
        place = self.place
        out = []
        for j, order in enumerate(ORDERS):
            axis = order[phase]
            here = {a: place.at[a] for a in order[phase:]}
            for step in (1, 2, 3):
                _, device = place.along(axis, step)
                spot = dict(here)
                if coming:
                    spot[axis] = (place.at[axis] - step) % 4
                ref = region(self.bufs[arr], l, spot, place.core, THIRDS[l][arr][j])
                sems = (self.send.at[l, arr, phase, j, step - 1], self.recv.at[l, arr, phase, j, step - 1])
                out.append(remote(ref, ref, *sems, device))
        return out

    def start(self, l, arr, phase):
        for copy in self.copies(l, arr, phase, False):
            copy.start()
        if phase == 2:
            for j in range(3):
                self.swap(l, arr, j, 0).start()

    def arrive(self, l, arr, phase):
        for copy in self.copies(l, arr, phase, True):
            copy.wait_recv()

    def swap(self, l, arr, j, step, coming=False):
        place = self.place
        axis = ORDERS[j][2]
        core = 1 - place.core if coming else place.core
        ref = region(self.bufs[arr], l, {axis: (place.at[axis] - step) % 4}, core, THIRDS[l][arr][j])
        return remote(
            ref, ref, self.swap_send.at[l, arr, j, step], self.swap_recv.at[l, arr, j, step], place.other_core()
        )

    def swap_start(self, l, arr):
        copies = self.copies(l, arr, 2, True)
        for step in (1, 3, 2):
            for j in range(3):
                copies[3 * j + step - 1].wait_recv()
                self.swap(l, arr, j, step).start()

    def swap_arrive(self, l, arr):
        for j in range(3):
            for step in range(4):
                self.swap(l, arr, j, step, True).wait_recv()

    def finish(self):
        for chunk in CHUNKS:
            for phase in range(3):
                for copy in self.copies(*chunk, phase, False):
                    copy.wait_send()
            for j in range(3):
                for step in range(4):
                    self.swap(*chunk, j, step).wait_send()


class Scatter:
    def __init__(self, place, bufs, slots, total, send, recv):
        self.place, self.bufs, self.slots, self.total, self.send, self.recv = place, bufs, slots, total, send, recv

    def slot(self, l, phase, arr, j):
        return self.slots[((l * 3 + phase) * 2 + arr) * 3 + j]

    def part(self, l, arr, at, j):
        whole = slice(None)
        x_hi, x_lo = (at["x"] // 2, at["x"] % 2) if "x" in at else (whole, whole)
        low, high = THIRDS[l][arr][j]
        return self.bufs[arr].at[
            l, x_lo, at.get("y", whole), x_hi, at.get("z", whole), whole, pl.ds(low, high - low)
        ]

    def copies(self, l, arr, phase):
        place = self.place
        out = []
        for j, order in enumerate(ORDERS):
            rev = order[::-1]
            for step in (1, 2, 3):
                there = {a: place.at[a] for a in rev[:phase]}
                there[rev[phase]], device = place.along(rev[phase], step)
                dst = self.slot(l, phase, arr, j).at[step - 1]
                sems = (self.send.at[l, arr, phase, j, step - 1], self.recv.at[l, arr, phase, j, step - 1])
                out.append(remote(self.part(l, arr, there, j), dst, *sems, device))
        return out

    def add_up(self, l, arr, phase):
        for j, order in enumerate(ORDERS):
            rev = order[::-1]
            own = self.part(l, arr, {a: self.place.at[a] for a in rev[: phase + 1]}, j)
            came = self.slot(l, phase, arr, j)
            if phase == 2:
                low, high = THIRDS[l][arr][j]
                total = own[...].astype(F32)
                for k in range(3):
                    total = total + came[k].astype(F32)
                self.total[l, :, 512 * arr + low : 512 * arr + high] = total
                continue

            def body(index, own=own, came=came):
                total = own[index].astype(F32)
                for k in range(3):
                    total = total + came[(k,) + index].astype(F32)
                own[index] = total.astype(BF)

            each_block(dims_of(rev[phase + 1 :]), body)

    def step(self, l, arr, stage):
        if stage > 0:
            for copy in self.copies(l, arr, stage - 1):
                copy.wait_recv()
            self.add_up(l, arr, stage - 1)
        if stage < 3:
            for copy in self.copies(l, arr, stage):
                copy.start()

    def finish(self):
        for chunk in CHUNKS:
            for phase in range(3):
                for copy in self.copies(*chunk, phase):
                    copy.wait_send()


def train_kernel(*refs):
    r = dict(zip(NAMES, refs[: len(NAMES)]))
    slots = refs[len(NAMES) :]
    place = Place()
    seq, core, x_lo = place.seq, place.core, place.seq // 2
    peer = 1 - core
    near = place.other_core()
    across = {"dp": place.dp, "seq": (1 - x_lo) * 2 + core}
    wa, wm, ga, gm, vec, vgrad = r["wa"], r["wm"], r["ga"], r["gm"], r["vec"], r["vgrad"]
    s0, r0, stage, kv = r["s0"], r["r0"], r["stage"], r["kv"]
    unsent = []

    def send(src, dst, sem, index, device):
        copy = remote(src, dst, r[sem + "_send"].at[index], r[sem + "_recv"].at[index], device)
        copy.start()
        unsent.append(copy)
        return copy

    greeted = greet(place)
    t0 = r["t0"]
    for s, q in enumerate(QUARTERS):
        for l in range(2):
            t0[s, 8 * l : 8 * l + 4, 0:512] = r["w_attn"][l, :, 512 * q : 512 * q + 512]
            t0[s, 8 * l : 8 * l + 4, 512:768] = r["w_mlp"][l, :, 1024 * s : 1024 * s + 256]
            t0[s, 8 * l + 4 : 8 * l + 8, :] = r["w_mlp"][l, :, 1024 * s + 256 : 1024 * s + 1024]
    s0[...] = t0[...].astype(BF)
    tab = r["tab"]
    number = place.dp * 4 + seq
    square = r["square"]
    square[...] = jnp.zeros((128, 128), F32)
    for l in range(2):
        square[0:4, 0:12] = r["vectors"][l].astype(BF).astype(F32)
        tab[place.at["y"], 12 * l : 12 * l + 12, :] = square[...].T[0:12, :]
    tab[place.at["y"]] = pltpu.roll(tab[place.at["y"]], 4 * (number % 32), 1)
    r["docs"][seq] = r["segments"][...]
    xall = r["xall"]
    xall[0, x_lo, core] = r["tokens"][...]
    pl.semaphore_wait(*greeted)

    pieces, docs = [], []
    for step in (1, 2, 3):
        member, device = place.in_group(step)
        pieces.append(send(s0.at[member], r0.at[seq], "a2a", (2, step), device))
    table = Table(place, tab, r["vgot"].at[0], r["v_send"].at[0], r["v_recv"].at[0])
    table.start("core")
    for step in (1, 2, 3):
        member, device = place.in_group(step)
        docs.append(send(r["docs"].at[seq], r["docs"].at[seq], "doc", step, device))
    def share(l):
        mine = xall.at[l, x_lo, core]
        near_way = send(mine, mine, "x", (l, 0), near)
        return near_way, send(mine, mine, "x", (l, 1), across)

    def pass_on(l, far_way):
        far_way.wait_recv()
        came = xall.at[l, 1 - x_lo, core]
        return send(came, came, "x", (l, 2), near)

    first_near, first_far = share(0)
    r0[seq] = s0[seq]
    for copy in pieces:
        copy.wait_recv()
    for src in range(4):
        t0[src] = r0[src].astype(F32)
        for l in range(2):
            stage[l, 4 * src : 4 * src + 4, 0:768] = t0[src, 8 * l : 8 * l + 4, :]
            stage[l, 4 * src : 4 * src + 4, 768:1536] = t0[src, 8 * l + 4 : 8 * l + 8, :]
    at = place.at
    for l, arr in CHUNKS:
        block = stage[l, :, 512 * arr : 512 * arr + WIDTHS[arr]].astype(BF)
        (wa, wm)[arr][l, at["x"] % 2, core, at["y"], at["x"] // 2, at["z"]] = block
    gather = Gather(place, (wa, wm), r["ag_send"], r["ag_recv"], r["sw_send"], r["sw_recv"])
    table.finish()
    table.start("x")
    for chunk in CHUNKS:
        gather.start(*chunk, 0)

    for chunk in CHUNKS[:2]:
        gather.arrive(*chunk, 0)
        gather.start(*chunk, 1)
    table.finish()
    table.start("z")
    first_on = pass_on(0, first_far)
    gather.arrive(0, 0, 1)
    gather.start(0, 0, 2)
    table.finish()
    table.start("y", "spread")
    gather.arrive(0, 1, 1)
    gather.start(0, 1, 2)
    for chunk in CHUNKS[2:]:
        gather.arrive(*chunk, 0)
        gather.start(*chunk, 1)
    for copy in docs:
        copy.wait_recv()
    own_docs = jnp.broadcast_to(r["docs"][seq].astype(F32), (128, 128)).T
    for i in range(4):
        r["bias"][:, 128 * i : 128 * i + 128] = jnp.where(own_docs == r["docs"][i].astype(F32), 0.0, MASKED_SCORE)
    table.finish()
    for y in range(4):
        vec[:, 128 * y : 128 * y + 128] = tab[y]
    gather.swap_start(0, 0)
    for chunk in CHUNKS[2:]:
        gather.arrive(*chunk, 1)
        gather.start(*chunk, 2)
    first_near.wait_recv()
    first_on.wait_recv()
    gather.swap_arrive(0, 0)

    def weight(l, arr, s, low=0, high=None):
        high = WIDTHS[arr] if high is None else high
        return (wa, wm)[arr][l, s // 2, s % 2, :, :, :, :, low:high].reshape(512, high - low)

    def attn_weight(l, q):
        return weight(l, 0, QUARTERS.index(q))

    def put_grad(l, arr, plane, left, right, parts):
        width = WIDTHS[arr] // parts
        for i in range(parts):
            value = mm(left, right(width * i, width * i + width), TN)
            (ga, gm)[arr][l, plane, :, :, :, :, width * i : width * i + width] = value.astype(BF).reshape(
                4, 2, 4, 16, width
            )

    def row(l, k):
        return vec[12 * l + k : 12 * l + k + 1, :]

    def put_row(l, k, value):
        vgrad[12 * l + k : 12 * l + k + 1, :] = value

    lanes = lax.broadcasted_iota(jnp.int32, (1, 128), 1)
    first = (lanes < 64).astype(F32)
    second = 1.0 - first
    first_low, second_low = first.astype(BF), second.astype(BF)

    def both(pair):
        return jnp.concatenate([pair * first_low, pair * second_low], axis=0)

    def joined(stacked):
        return stacked[:128] * first + stacked[128:] * second

    def group_rows(l, which, low):
        return kv[l, which, :, :, low : low + 128].reshape(512, 128)

    def chip_keys(l, chip):
        rows = xall[l, chip].reshape(256, 512)
        kv[l, 0, chip] = mm(rows, attn_weight(l, 1)).astype(BF)
        kv[l, 1, chip] = (mm(rows, attn_weight(l, 2)) + row(l, 1)).astype(BF)

    pairs = r["pairs"]
    hidden = r["tokens"][...].astype(F32)
    for l in range(2):
        low_in = hidden.astype(BF)
        if l == 1:
            xall[1, x_lo, core] = low_in
            near_way, far_way = share(1)
            gather.swap_arrive(1, 0)
        r["q"][l] = (mm(low_in, attn_weight(l, 0)) + row(l, 0)).astype(BF)
        if l == 1:
            near_way.wait_recv()
        chip_keys(l, x_lo)
        if l == 1:
            on_way = pass_on(1, far_way)
            gather.swap_start(1, 1)
            on_way.wait_recv()
        chip_keys(l, 1 - x_lo)
        pairs[l, 0] = xall[l, x_lo]
        for pair in range(4):
            low = 128 * pair
            scores = mm(both(r["q"][l, :, low : low + 128]), group_rows(l, 0, low), NT) * SCALE
            bias = r["bias"][...]
            scores = scores + jnp.concatenate([bias, bias], axis=0)
            powers = jnp.exp(scores - jnp.max(scores, axis=-1, keepdims=True))
            probs = (powers * (1.0 / jnp.sum(powers, axis=-1, keepdims=True))).astype(BF)
            r["probs"][l, pair] = probs
            pairs[l, 1, core, :, low : low + 128] = joined(mm(probs, group_rows(l, 1, low))).astype(BF)
            if l == 0 and pair == 1:
                gather.swap_start(0, 1)
        send(pairs.at[l, 1, core], pairs.at[l, 1, core], "act", (l, 1), near)
        if l == 0:
            gather.swap_arrive(0, 1)
        hat, inverse = normalize(hidden + mm(pairs[l, 1, core], attn_weight(l, 3)) + row(l, 2))
        r["hat1"][l] = hat
        r["inv1"][l] = inverse
        normed = hat * row(l, 3) + row(l, 4)
        low_normed = normed.astype(BF)
        pairs[l, 2, core] = low_normed
        send(pairs.at[l, 2, core], pairs.at[l, 2, core], "act", (l, 2), near)
        back = jnp.zeros((128, 512), F32)
        if l == 1:
            gather.swap_arrive(1, 1)
        for i in range(4):
            half, low = i // 2, 512 * (i % 2)
            pre = mm(low_normed, weight(l, 1, half, low, low + 512)) + row(l, 5 + i)
            normal = 0.5 + 0.5 * lax.erf(pre * (0.5**0.5))
            act = (pre * normal).astype(BF)
            r["act"][l, half, core, :, low : low + 512] = act
            slope = normal + pre * (jnp.exp(pre * pre * -0.5) * (1.0 / (2.0 * math.pi) ** 0.5))
            r["slope"][l, :, 512 * i : 512 * i + 512] = slope.astype(BF)
            back = back + mm(act, weight(l, 1, 2 + half, low, low + 512), NT)
        mine = r["act"].at[l, peer, core]
        send(mine, mine, "act", (l, 3), near)
        if l == 0:
            gather.swap_start(1, 0)
        hat, inverse = normalize(normed + back + row(l, 9))
        r["hat2"][l] = hat
        r["inv2"][l] = inverse
        hidden = hat * row(l, 10) + row(l, 11)
    r["block_out"][...] = hidden.astype(BF)

    scatter = Scatter(place, (ga, gm), slots, r["total"], r["rs_send"], r["rs_recv"])
    dx, dx_near, dx_far, late, early = r["dx"], r["dx_near"], r["dx_far"], r["late"], r["early"]

    def grad_rows(l, chip):
        keys, values = late[l, 0, core, chip].reshape(256, 512), late[l, 1, core, chip].reshape(256, 512)
        part = mm(keys, attn_weight(l, 1), NT) + mm(values, attn_weight(l, 2), NT)
        dx[l, chip] = part.astype(BF).reshape(2, 128, 512)
        return send(dx.at[l, chip, peer], dx_near.at[l, chip], "dx", (l, (chip + x_lo) % 2), near)

    def give_far(l, copy):
        copy.wait_recv()
        mine = dx[l, 1 - x_lo, core].astype(F32) + dx_near[l, 1 - x_lo].astype(F32)
        dx[l, 1 - x_lo, core] = mine.astype(BF)
        return send(dx.at[l, 1 - x_lo, core], dx_far.at[l], "dx", (l, 2), across)

    def act_arrive(l, which):
        if which == 3:
            ref = r["act"].at[l, core, peer]
        else:
            ref = pairs.at[l, which, peer]
        remote(ref, ref, r["act_send"].at[l, which], r["act_recv"].at[l, which], near).wait_recv()

    def two(ref, *index):
        return ref[index].reshape(256, -1)

    def mlp_grads(l, got_second):
        got_second.wait_recv()
        act_arrive(l, 3)
        put_grad(l, 1, 1, two(pairs, l, 3), lambda low, high: r["act"][l, core, :, :, low:high].reshape(256, -1), 2)
        act_arrive(l, 2)
        theirs = r["du"].at[l, core, peer]
        remote(theirs, theirs, r["back_send"].at[l, 1], r["back_recv"].at[l, 1], near).wait_recv()
        put_grad(l, 1, 0, two(pairs, l, 2), lambda low, high: r["du"][l, core, :, :, low:high].reshape(256, -1), 2)
        scatter.step(l, 1, 0)

    s4, fin, total = r["s4"], r["fin"], r["total"]
    moved = []

    def hand_out(l):
        for dst in range(4):
            s4[dst, l] = total[l, 4 * dst : 4 * dst + 4, :]
        for step in (1, 2, 3):
            member, device = place.in_group(step)
            moved.append(send(s4.at[member, l], fin.at[seq, l], "a2a", (l, step), device))
        fin[seq, l] = s4[seq, l]

    grad = r["cotangent"][...].astype(F32)
    for l in (1, 0):
        hat = r["hat2"][l]
        put_row(l, 10, column_sum(grad * hat))
        put_row(l, 11, column_sum(grad))
        grad_second = normalize_back(grad * row(l, 10), hat, r["inv2"][l])
        put_row(l, 9, column_sum(grad_second))
        low_second = grad_second.astype(BF)
        pairs[l, 3, core] = low_second
        got_second = send(pairs.at[l, 3, core], pairs.at[l, 3, core], "back", (l, 0), near)
        grad_normed = grad_second
        for i in range(4):
            half, low = i // 2, 512 * (i % 2)
            grad_act = mm(low_second, weight(l, 1, 2 + half, low, low + 512))
            grad_pre = (grad_act * r["slope"][l, :, 512 * i : 512 * i + 512].astype(F32)).astype(BF)
            put_row(l, 5 + i, column_sum(grad_pre.astype(F32)))
            r["du"][l, half, core, :, low : low + 512] = grad_pre
            grad_normed = grad_normed + mm(grad_pre, weight(l, 1, half, low, low + 512), NT)
        mine = r["du"].at[l, peer, core]
        send(mine, mine, "back", (l, 1), near)
        if l == 0:
            scatter.step(1, 1, 1)
        mlp_grads(l, got_second)
        hat = r["hat1"][l]
        put_row(l, 3, column_sum(grad_normed * hat))
        put_row(l, 4, column_sum(grad_normed))
        grad_first = normalize_back(grad_normed * row(l, 3), hat, r["inv1"][l])
        put_row(l, 2, column_sum(grad_first))
        low_first = grad_first.astype(BF)
        early[l, 1, core] = low_first
        grad_mixed = mm(low_first, attn_weight(l, 3), NT).astype(BF)
        for pair in range(4):
            low = 128 * pair
            keys, values = group_rows(l, 0, low), group_rows(l, 1, low)
            grad_pair = both(grad_mixed[:, low : low + 128])
            probs = r["probs"][l, pair]
            grad_probs = mm(grad_pair, values, NT)
            late[l, 1, core, :, :, low : low + 128] = mm(probs, grad_pair, TN).astype(BF).reshape(2, 256, 128)
            wide = probs.astype(F32)
            row_dot = jnp.sum(grad_probs * wide, axis=-1, keepdims=True)
            grad_scores = (wide * (grad_probs - row_dot)).astype(BF)
            early[l, 0, core, :, low : low + 128] = (joined(mm(grad_scores, keys)) * SCALE).astype(BF)
            grad_keys = mm(grad_scores, both(r["q"][l, :, low : low + 128]), TN) * SCALE
            late[l, 0, core, :, :, low : low + 128] = grad_keys.astype(BF).reshape(2, 256, 128)
            if l == 0 and pair == 1:
                scatter.step(1, 0, 1)
        mine = late.at[l, peer, core]
        send(mine, mine, "back", (l, 3), near)
        mine = early.at[l, peer, core]
        send(mine, mine, "back", (l, 2), near)
        grad_queries = early[l, 0, core]
        put_row(l, 0, column_sum(grad_queries.astype(F32)))
        put_row(l, 1, column_sum(late[l, 1, core].reshape(512, 512).astype(F32)))
        if l == 0:
            for y in range(4):
                r["vtab"][y] = vgrad[:, 128 * y : 128 * y + 128]
            table = Table(place, r["vtab"], r["vgot"].at[1], r["v_send"].at[1], r["v_recv"].at[1])
            table.start("y", "collect")

        def attn_grads():
            act_arrive(l, 1)
            theirs = early.at[l, core, peer]
            remote(theirs, theirs, r["back_send"].at[l, 2], r["back_recv"].at[l, 2], near).wait_recv()
            put_grad(l, 0, 0, two(pairs, l, core), lambda low, high: two(early, l, core), 1)
            theirs = late.at[l, core, peer]
            remote(theirs, theirs, r["back_send"].at[l, 3], r["back_recv"].at[l, 3], near).wait_recv()
            rows = xall[l].reshape(512, 512)
            value = mm(rows, late[l, core, 0].reshape(512, 512), TN) + mm(rows, late[l, core, 1].reshape(512, 512), TN)
            ga[l, 1] = value.astype(BF).reshape(4, 2, 4, 16, 512)
            scatter.step(l, 0, 0)

        if l == 0:
            attn_grads()
        far_near = grad_rows(l, 1 - x_lo)
        own_near = grad_rows(l, x_lo)
        far_way = give_far(l, far_near)
        grad = grad_first + mm(grad_queries, attn_weight(l, 0), NT)
        if l == 1:
            attn_grads()
        else:
            scatter.step(1, 1, 2)
            scatter.step(1, 0, 2)
            table.finish()
            table.start("x")
            scatter.step(0, 1, 1)
            scatter.step(1, 1, 3)
            scatter.step(1, 0, 3)
            hand_out(1)
        own_near.wait_recv()
        far_way.wait_recv()
        grad = grad + dx[l, x_lo, core].astype(F32) + dx_near[l, x_lo].astype(F32) + dx_far[l].astype(F32)
    r["input_grad"][...] = grad
    scatter.step(0, 0, 1)
    table.finish()
    table.start("z")
    scatter.step(0, 1, 2)
    scatter.step(0, 0, 2)
    table.finish()
    table.start("core")
    scatter.step(0, 1, 3)
    scatter.step(0, 0, 3)
    hand_out(0)
    table.finish()
    r["vtab"][place.at["y"]] = pltpu.roll(r["vtab"][place.at["y"]], (128 - 4 * (number % 32)) % 128, 1)
    for l in range(2):
        square[0:12, :] = r["vtab"][place.at["y"], 12 * l : 12 * l + 12, :]
        r["vfin"][l] = square[...].T[0:8, :]
    gather.finish()
    scatter.finish()
    for copy in moved:
        copy.wait_recv()
    for copy in unsent:
        copy.wait_send()


INPUTS = ("tokens", "cotangent", "segments", "w_attn", "w_mlp", "vectors")
OUTPUTS = {
    "block_out": ((128, 512), BF),
    "input_grad": ((128, 512), F32),
    "fin": ((4, 2, 4, 1536), F32),
    "vfin": ((2, 8, 128), F32),
}
DIMS = (2, 2, 2, 4, 2, 4, 16)
HALF = (2, 2, 4, 2, 4, 16)
SCRATCH = {
    "wa": (DIMS + (512,), BF),
    "wm": (DIMS + (1024,), BF),
    "ga": (HALF + (512,), BF),
    "gm": (HALF + (1024,), BF),
    "vec": ((24, 512), F32),
    "vgrad": ((24, 512), F32),
    "tab": ((4, 24, 128), F32),
    "vtab": ((4, 24, 128), F32),
    "t0": ((4, 16, 768), F32),
    "square": ((128, 128), F32),
    "s0": ((4, 16, 768), BF),
    "r0": ((4, 16, 768), BF),
    "s4": ((4, 2, 4, 1536), F32),
    "stage": ((2, 16, 1536), F32),
    "total": ((2, 16, 1536), F32),
    "vgot": ((2, 4, 3, 24, 128), F32),
    "docs": ((4, 1, 128), jnp.int32),
    "bias": ((128, 512), F32),
    "q": ((2, 128, 512), BF),
    "kv": ((2, 2, 2, 256, 512), BF),
    "xall": ((2, 2, 2, 128, 512), BF),
    "probs": ((2, 4, 256, 512), BF),
    "pairs": ((2, 4, 2, 128, 512), BF),
    "act": ((2, 2, 2, 128, 1024), BF),
    "du": ((2, 2, 2, 128, 1024), BF),
    "early": ((2, 2, 2, 128, 512), BF),
    "late": ((2, 2, 2, 2, 256, 512), BF),
    "hat1": ((2, 128, 512), F32),
    "inv1": ((2, 128, 1), F32),
    "slope": ((2, 128, 2048), BF),
    "hat2": ((2, 128, 512), F32),
    "inv2": ((2, 128, 1), F32),
    "dx": ((2, 2, 2, 128, 512), BF),
    "dx_near": ((2, 2, 128, 512), BF),
    "dx_far": ((2, 128, 512), BF),
}
SEMS = {
    "a2a": (3, 4),
    "doc": (4,),
    "ag": (2, 2, 3, 3, 3),
    "sw": (2, 2, 3, 4),
    "rs": (2, 2, 3, 3, 3),
    "x": (2, 3),
    "dx": (2, 3),
    "act": (2, 4),
    "back": (2, 4),
    "v": (2, 4, 3),
}
NAMES = INPUTS + tuple(OUTPUTS) + tuple(SCRATCH) + tuple(f"{n}_{d}" for n in SEMS for d in ("send", "recv"))


def train(*args):
    slots = []
    for l in range(2):
        for phase in range(3):
            for arr in range(2):
                for j in range(3):
                    low, high = THIRDS[l][arr][j]
                    rest = dims_of(ORDERS[j][::-1][phase + 1 :])
                    slots.append(pltpu.VMEM((3,) + rest + (16, high - low), BF))
    scratch = [pltpu.VMEM(*spec) for spec in SCRATCH.values()]
    for shape in SEMS.values():
        scratch += [pltpu.SemaphoreType.DMA(shape)] * 2
    return pl.pallas_call(
        train_kernel,
        out_shape=tuple(jax.ShapeDtypeStruct(*spec) for spec in OUTPUTS.values()),
        in_specs=[pl.BlockSpec(memory_space=pltpu.VMEM)] * len(INPUTS),
        out_specs=[pl.BlockSpec(memory_space=pltpu.VMEM)] * len(OUTPUTS),
        scratch_shapes=scratch + slots,
        compiler_params=pltpu.CompilerParams(
            collective_id=0, has_side_effects=True, vmem_limit_bytes=VMEM_BYTES
        ),
        name="train",
    )(*args)


def adam_update(weight, grad, first, second, rate, decay):
    first_new = BETA_FIRST * first + (1.0 - BETA_FIRST) * grad
    second_new = BETA_SECOND * second + (1.0 - BETA_SECOND) * grad * grad
    first_fix = 1.0 - BETA_FIRST**STEP
    second_fix = 1.0 - BETA_SECOND**STEP
    weight_new = weight - rate * (
        first_new / first_fix / (jnp.sqrt(second_new / second_fix) + ADAM_EPSILON) + decay * weight
    )
    return (first_new, second_new, weight_new)


def adam_kernel(block_in, grad_in, fin, vfin, *refs):
    state, (block_out, grad_out), outs = refs[:9], refs[9:11], refs[11:]
    block_out[...] = block_in[...]
    grad_out[...] = grad_in[...]
    for l in range(2):
        for arr in range(3):
            w, m, v = state[arr], state[3 + arr], state[6 + arr]
            if arr == 2:
                pieces = [(vfin[l, 0:4, 0:12], slice(0, 12))]
            elif arr == 1:
                pieces = [(fin[s, l, :, 512:1536], slice(1024 * s, 1024 * s + 1024)) for s in range(4)]
            else:
                pieces = [(fin[s, l, :, 0:512], slice(512 * q, 512 * q + 512)) for s, q in enumerate(QUARTERS)]
            rate, decay = (VECTOR_RATE, 0.0) if arr == 2 else (LEARN_RATE, WEIGHT_DECAY)
            for grad, span in pieces:
                new = adam_update(w[l, :, span], grad, m[l, :, span], v[l, :, span], rate, decay)
                for k in range(3):
                    outs[3 * arr + k][l, :, span] = new[k]


def adam(block, grad, fin, vfin, *state):
    shapes = [jax.ShapeDtypeStruct(a.shape, a.dtype) for a in (block, grad)]
    for a in state[:3]:
        shapes += [jax.ShapeDtypeStruct(a.shape, a.dtype)] * 3
    spec = pl.BlockSpec(memory_space=pltpu.VMEM)
    return pl.pallas_call(
        adam_kernel, out_shape=shapes, in_specs=[spec] * 13, out_specs=[spec] * 11, name="adam"
    )(block, grad, fin, vfin, *state)


def local(
    tokens, cotangent, segments, w_attn, w_mlp, vectors, m_attn, m_mlp, m_vec, v_attn, v_mlp, v_vec
):
    vectors, m_vec, v_vec = (a.transpose(0, 2, 1) for a in (vectors, m_vec, v_vec))
    made = train(tokens[0], cotangent[0], segments, w_attn, w_mlp, vectors)
    block_out, input_grad, *updated = adam(
        *made, w_attn, w_mlp, vectors, m_attn, m_mlp, m_vec, v_attn, v_mlp, v_vec
    )
    return (block_out[None], input_grad[None], *updated[:6], *(a.transpose(0, 2, 1) for a in updated[6:]))


def solution(mesh):
    in_specs = (
        P("dp", "seq", None),
        P("dp", "seq", None),
        P("dp", "seq"),
        P(None, ("dp", "seq"), None),
        P(None, ("dp", "seq"), None),
        P(None, None, ("dp", "seq")),
        P(None, ("dp", "seq"), None),
        P(None, ("dp", "seq"), None),
        P(None, None, ("dp", "seq")),
        P(None, ("dp", "seq"), None),
        P(None, ("dp", "seq"), None),
        P(None, None, ("dp", "seq")),
    )
    out_specs = (
        P("dp", "seq", None),
        P("dp", "seq", None),
        P(None, ("dp", "seq"), None),
        P(None, ("dp", "seq"), None),
        P(None, ("dp", "seq"), None),
        P(None, ("dp", "seq"), None),
        P(None, ("dp", "seq"), None),
        P(None, ("dp", "seq"), None),
        P(None, None, ("dp", "seq")),
        P(None, None, ("dp", "seq")),
        P(None, None, ("dp", "seq")),
    )
    return jax.shard_map(local, mesh=mesh, in_specs=in_specs, out_specs=out_specs, check_vma=False)
```

```python
import math

import jax
import jax.numpy as jnp
from jax import lax
from jax.experimental import pallas as pl
from jax.experimental.pallas import tpu as pltpu
from jax.sharding import PartitionSpec as P

STEP = 10
NORM_EPSILON = 1e-06
ADAM_EPSILON = 1e-06
BETA_FIRST = 0.9
BETA_SECOND = 0.999
LEARN_RATE = 0.03
VECTOR_RATE = 0.2
WEIGHT_DECAY = 0.01
MASKED_SCORE = -1e30
VMEM_BYTES = 62 * 2**20
MESH = pl.DeviceIdType.MESH
BF = jnp.bfloat16
F32 = jnp.float32
EVEN = (((0, 128), (128, 256), (256, 512)), ((0, 384), (384, 768), (768, 1024)))
UNEVEN = (((0, 256), (256, 384), (384, 512)), ((0, 384), (384, 640), (640, 1024)))
THIRDS = (EVEN, UNEVEN)
WIDTHS = (512, 1024)
ORDERS = (("x", "y", "z"), ("y", "z", "x"), ("z", "x", "y"))


class Place:
    def __init__(self):
        self.dp = lax.axis_index("dp")
        self.seq = lax.axis_index("seq")
        self.core = self.seq % 2
        self.at = {
            "x": ((self.dp // 4) % 2) * 2 + self.seq // 2,
            "y": self.dp // 8,
            "z": self.dp % 4,
        }

    def device(self, at, core):
        return {
            "dp": (at["y"] * 2 + at["x"] // 2) * 4 + at["z"],
            "seq": (at["x"] % 2) * 2 + core,
        }

    def along(self, axis, step):
        at = dict(self.at)
        at[axis] = (at[axis] + step) % 4
        return at[axis], self.device(at, self.core)

    def other_core(self):
        return self.device(self.at, 1 - self.core)

    def in_group(self, step):
        peer = (self.seq + step) % 4
        return peer, {"dp": self.dp, "seq": peer}


def region(buf, layer, at, core, columns):
    whole = slice(None)
    if "x" in at:
        x_hi, x_lo = at["x"] // 2, at["x"] % 2
    else:
        x_hi, x_lo = whole, whole
    cols = pl.ds(columns[0], columns[1] - columns[0])
    return buf.at[layer, x_lo, core, at.get("y", whole), x_hi, at.get("z", whole), whole, cols]


def greet(place):
    barrier = pltpu.get_barrier_semaphore()
    peers = [place.other_core()]
    for axis in ("x", "y", "z"):
        for step in (1, 2, 3):
            peers.append(place.along(axis, step)[1])
    far = {"dp": place.dp, "seq": (1 - place.seq // 2) * 2 + (1 - place.core)}
    peers.append(far)
    for peer in peers:
        pl.semaphore_signal(barrier, inc=1, device_id=peer, device_id_type=MESH)
    return barrier, len(peers)


def remote(src, dst, send, recv, device):
    return pltpu.make_async_remote_copy(
        src_ref=src, dst_ref=dst, send_sem=send, recv_sem=recv, device_id=device, device_id_type=MESH
    )


class Table:
    ROUNDS = {"core": (0, (1,)), "x": (1, (1, 2, 3)), "y": (2, (1, 2, 3)), "z": (3, (1, 2, 3))}

    def __init__(self, place, blocks, came, send, recv):
        self.place, self.blocks, self.came, self.send, self.recv = place, blocks, came, send, recv
        self.going, self.mode, self.axis = None, None, None

    def start(self, axis, mode="add"):
        number, steps = self.ROUNDS[axis]
        own = self.blocks.at[self.place.at["y"]]
        self.going, self.mode, self.axis = [], mode, axis
        for step in steps:
            if axis == "core":
                device = self.place.other_core()
            else:
                pos, device = self.place.along(axis, step)
            src = self.blocks.at[pos] if mode == "collect" else own
            dst = own if mode == "spread" else self.came.at[number, step - 1]
            copy = remote(src, dst, self.send.at[number, step - 1], self.recv.at[number, step - 1], device)
            copy.start()
            self.going.append(copy)

    def finish(self):
        number, steps = self.ROUNDS[self.axis]
        for copy in self.going:
            copy.wait()
        if self.mode != "spread":
            total = self.blocks[self.place.at["y"]]
            for step in steps:
                total = total + self.came[number, step - 1]
            self.blocks[self.place.at["y"]] = total


def dims_of(axes):
    out = ()
    if "x" in axes:
        out += (2,)
    if "y" in axes:
        out += (4,)
    if "x" in axes:
        out += (2,)
    if "z" in axes:
        out += (4,)
    return out


def each_block(dims, body):
    count = 1
    for size in dims[:-1]:
        count *= size

    def one(i, carry):
        index = ()
        rest = i
        for size in reversed(dims[:-1]):
            index = (rest % size,) + index
            rest = rest // size
        body(index)
        return carry

    if count == 1:
        body(tuple(0 for _ in dims[:-1]))
    else:
        lax.fori_loop(0, count, one, 0)


NT = (((1,), (1,)), ((), ()))
NN = (((1,), (0,)), ((), ()))
TN = (((0,), (0,)), ((), ()))
CHUNKS = ((0, 0), (0, 1), (1, 0), (1, 1))
PIECES = (16, 1536)
SCALE = 0.125
QUARTERS = (0, 3, 1, 2)


def mm(left, right, dims=NN):
    return lax.dot_general(left, right, dims, preferred_element_type=F32)


def column_sum(values):
    return jnp.sum(values, axis=0, keepdims=True)


def normalize(summed):
    center = summed - jnp.mean(summed, axis=-1, keepdims=True)
    spread = jnp.mean(center * center, axis=-1, keepdims=True)
    inverse = lax.rsqrt(spread + NORM_EPSILON)
    return center * inverse, inverse


def normalize_back(grad, hat, inverse):
    mean = jnp.mean(grad, axis=-1, keepdims=True)
    along = jnp.mean(grad * hat, axis=-1, keepdims=True)
    return inverse * (grad - mean - hat * along)


class Gather:
    def __init__(self, place, bufs, send, recv, swap_send, swap_recv):
        self.place, self.bufs = place, bufs
        self.send, self.recv, self.swap_send, self.swap_recv = send, recv, swap_send, swap_recv

    def copies(self, l, arr, phase, coming):
        place = self.place
        out = []
        for j, order in enumerate(ORDERS):
            axis = order[phase]
            here = {a: place.at[a] for a in order[phase:]}
            for step in (1, 2, 3):
                _, device = place.along(axis, step)
                spot = dict(here)
                if coming:
                    spot[axis] = (place.at[axis] - step) % 4
                ref = region(self.bufs[arr], l, spot, place.core, THIRDS[l][arr][j])
                sems = (self.send.at[l, arr, phase, j, step - 1], self.recv.at[l, arr, phase, j, step - 1])
                out.append(remote(ref, ref, *sems, device))
        return out

    def start(self, l, arr, phase):
        for copy in self.copies(l, arr, phase, False):
            copy.start()
        if phase == 2:
            for j in range(3):
                self.swap(l, arr, j, 0).start()

    def arrive(self, l, arr, phase):
        for copy in self.copies(l, arr, phase, True):
            copy.wait_recv()

    def swap(self, l, arr, j, step, coming=False):
        place = self.place
        axis = ORDERS[j][2]
        core = 1 - place.core if coming else place.core
        ref = region(self.bufs[arr], l, {axis: (place.at[axis] - step) % 4}, core, THIRDS[l][arr][j])
        return remote(
            ref, ref, self.swap_send.at[l, arr, j, step], self.swap_recv.at[l, arr, j, step], place.other_core()
        )

    def swap_start(self, l, arr):
        copies = self.copies(l, arr, 2, True)
        for step in (1, 3, 2):
            for j in range(3):
                copies[3 * j + step - 1].wait_recv()
                self.swap(l, arr, j, step).start()

    def swap_arrive(self, l, arr):
        for j in range(3):
            for step in range(4):
                self.swap(l, arr, j, step, True).wait_recv()

    def finish(self):
        for chunk in CHUNKS:
            for phase in range(3):
                for copy in self.copies(*chunk, phase, False):
                    copy.wait_send()
            for j in range(3):
                for step in range(4):
                    self.swap(*chunk, j, step).wait_send()


class Scatter:
    def __init__(self, place, bufs, slots, total, send, recv):
        self.place, self.bufs, self.slots, self.total, self.send, self.recv = place, bufs, slots, total, send, recv

    def slot(self, l, phase, arr, j):
        return self.slots[((l * 3 + phase) * 2 + arr) * 3 + j]

    def part(self, l, arr, at, j):
        whole = slice(None)
        x_hi, x_lo = (at["x"] // 2, at["x"] % 2) if "x" in at else (whole, whole)
        low, high = THIRDS[l][arr][j]
        return self.bufs[arr].at[
            l, x_lo, at.get("y", whole), x_hi, at.get("z", whole), whole, pl.ds(low, high - low)
        ]

    def copies(self, l, arr, phase):
        place = self.place
        out = []
        for j, order in enumerate(ORDERS):
            rev = order[::-1]
            for step in (1, 2, 3):
                there = {a: place.at[a] for a in rev[:phase]}
                there[rev[phase]], device = place.along(rev[phase], step)
                dst = self.slot(l, phase, arr, j).at[step - 1]
                sems = (self.send.at[l, arr, phase, j, step - 1], self.recv.at[l, arr, phase, j, step - 1])
                out.append(remote(self.part(l, arr, there, j), dst, *sems, device))
        return out

    def add_up(self, l, arr, phase):
        for j, order in enumerate(ORDERS):
            rev = order[::-1]
            own = self.part(l, arr, {a: self.place.at[a] for a in rev[: phase + 1]}, j)
            came = self.slot(l, phase, arr, j)
            if phase == 2:
                low, high = THIRDS[l][arr][j]
                total = own[...].astype(F32)
                for k in range(3):
                    total = total + came[k].astype(F32)
                self.total[l, :, 512 * arr + low : 512 * arr + high] = total
                continue

            def body(index, own=own, came=came):
                total = own[index].astype(F32)
                for k in range(3):
                    total = total + came[(k,) + index].astype(F32)
                own[index] = total.astype(BF)

            each_block(dims_of(rev[phase + 1 :]), body)

    def step(self, l, arr, stage):
        if stage > 0:
            for copy in self.copies(l, arr, stage - 1):
                copy.wait_recv()
            self.add_up(l, arr, stage - 1)
        if stage < 3:
            for copy in self.copies(l, arr, stage):
                copy.start()

    def finish(self):
        for chunk in CHUNKS:
            for phase in range(3):
                for copy in self.copies(*chunk, phase):
                    copy.wait_send()


def train_kernel(*refs):
    r = dict(zip(NAMES, refs[: len(NAMES)]))
    slots = refs[len(NAMES) :]
    place = Place()
    seq, core, x_lo = place.seq, place.core, place.seq // 2
    peer = 1 - core
    near = place.other_core()
    across = {"dp": place.dp, "seq": (1 - x_lo) * 2 + core}
    wa, wm, ga, gm, vec, vgrad = r["wa"], r["wm"], r["ga"], r["gm"], r["vec"], r["vgrad"]
    s0, r0, stage, kv = r["s0"], r["r0"], r["stage"], r["kv"]
    unsent = []

    def send(src, dst, sem, index, device):
        copy = remote(src, dst, r[sem + "_send"].at[index], r[sem + "_recv"].at[index], device)
        copy.start()
        unsent.append(copy)
        return copy

    greeted = greet(place)
    t0 = r["t0"]
    for s, q in enumerate(QUARTERS):
        for l in range(2):
            t0[s, 8 * l : 8 * l + 4, 0:512] = r["w_attn"][l, :, 512 * q : 512 * q + 512]
            t0[s, 8 * l : 8 * l + 4, 512:768] = r["w_mlp"][l, :, 1024 * s : 1024 * s + 256]
            t0[s, 8 * l + 4 : 8 * l + 8, :] = r["w_mlp"][l, :, 1024 * s + 256 : 1024 * s + 1024]
    s0[...] = t0[...].astype(BF)
    tab = r["tab"]
    number = place.dp * 4 + seq
    square = r["square"]
    square[...] = jnp.zeros((128, 128), F32)
    for l in range(2):
        square[0:4, 0:12] = r["vectors"][l].astype(BF).astype(F32)
        tab[place.at["y"], 12 * l : 12 * l + 12, :] = square[...].T[0:12, :]
    tab[place.at["y"]] = pltpu.roll(tab[place.at["y"]], 4 * (number % 32), 1)
    r["docs"][seq] = r["segments"][...]
    xall = r["xall"]
    xall[0, x_lo, core] = r["tokens"][...]
    pl.semaphore_wait(*greeted)

    pieces, docs = [], []
    for step in (1, 2, 3):
        member, device = place.in_group(step)
        pieces.append(send(s0.at[member], r0.at[seq], "a2a", (2, step), device))
    table = Table(place, tab, r["vgot"].at[0], r["v_send"].at[0], r["v_recv"].at[0])
    table.start("core")
    for step in (1, 2, 3):
        member, device = place.in_group(step)
        docs.append(send(r["docs"].at[seq], r["docs"].at[seq], "doc", step, device))
    def share(l):
        mine = xall.at[l, x_lo, core]
        near_way = send(mine, mine, "x", (l, 0), near)
        return near_way, send(mine, mine, "x", (l, 1), across)

    def pass_on(l, far_way):
        far_way.wait_recv()
        came = xall.at[l, 1 - x_lo, core]
        return send(came, came, "x", (l, 2), near)

    first_near, first_far = share(0)
    r0[seq] = s0[seq]
    for copy in pieces:
        copy.wait_recv()
    for src in range(4):
        t0[src] = r0[src].astype(F32)
        for l in range(2):
            stage[l, 4 * src : 4 * src + 4, 0:768] = t0[src, 8 * l : 8 * l + 4, :]
            stage[l, 4 * src : 4 * src + 4, 768:1536] = t0[src, 8 * l + 4 : 8 * l + 8, :]
    at = place.at
    for l, arr in CHUNKS:
        block = stage[l, :, 512 * arr : 512 * arr + WIDTHS[arr]].astype(BF)
        (wa, wm)[arr][l, at["x"] % 2, core, at["y"], at["x"] // 2, at["z"]] = block
    gather = Gather(place, (wa, wm), r["ag_send"], r["ag_recv"], r["sw_send"], r["sw_recv"])
    table.finish()
    table.start("x")
    for chunk in CHUNKS:
        gather.start(*chunk, 0)

    for chunk in CHUNKS[:2]:
        gather.arrive(*chunk, 0)
        gather.start(*chunk, 1)
    table.finish()
    table.start("z")
    first_on = pass_on(0, first_far)
    gather.arrive(0, 0, 1)
    gather.start(0, 0, 2)
    table.finish()
    table.start("y", "spread")
    gather.arrive(0, 1, 1)
    gather.start(0, 1, 2)
    for chunk in CHUNKS[2:]:
        gather.arrive(*chunk, 0)
        gather.start(*chunk, 1)
    for copy in docs:
        copy.wait_recv()
    own_docs = jnp.broadcast_to(r["docs"][seq].astype(F32), (128, 128)).T
    for i in range(4):
        r["bias"][:, 128 * i : 128 * i + 128] = jnp.where(own_docs == r["docs"][i].astype(F32), 0.0, MASKED_SCORE)
    table.finish()
    for y in range(4):
        vec[:, 128 * y : 128 * y + 128] = tab[y]
    gather.swap_start(0, 0)
    for chunk in CHUNKS[2:]:
        gather.arrive(*chunk, 1)
        gather.start(*chunk, 2)
    first_near.wait_recv()
    first_on.wait_recv()
    gather.swap_arrive(0, 0)

    def weight(l, arr, s, low=0, high=None):
        high = WIDTHS[arr] if high is None else high
        return (wa, wm)[arr][l, s // 2, s % 2, :, :, :, :, low:high].reshape(512, high - low)

    def attn_weight(l, q):
        return weight(l, 0, QUARTERS.index(q))

    def put_grad(l, arr, plane, left, right, parts):
        width = WIDTHS[arr] // parts
        for i in range(parts):
            value = mm(left, right(width * i, width * i + width), TN)
            (ga, gm)[arr][l, plane, :, :, :, :, width * i : width * i + width] = value.astype(BF).reshape(
                4, 2, 4, 16, width
            )

    def row(l, k):
        return vec[12 * l + k : 12 * l + k + 1, :]

    def put_row(l, k, value):
        vgrad[12 * l + k : 12 * l + k + 1, :] = value

    lanes = lax.broadcasted_iota(jnp.int32, (1, 128), 1)
    first = (lanes < 64).astype(F32)
    second = 1.0 - first
    first_low, second_low = first.astype(BF), second.astype(BF)

    def both(pair):
        return jnp.concatenate([pair * first_low, pair * second_low], axis=0)

    def joined(stacked):
        return stacked[:128] * first + stacked[128:] * second

    def group_rows(l, which, low):
        return kv[l, which, :, :, low : low + 128].reshape(512, 128)

    def chip_keys(l, chip):
        rows = xall[l, chip].reshape(256, 512)
        kv[l, 0, chip] = mm(rows, attn_weight(l, 1)).astype(BF)
        kv[l, 1, chip] = (mm(rows, attn_weight(l, 2)) + row(l, 1)).astype(BF)

    pairs = r["pairs"]
    hidden = r["tokens"][...].astype(F32)
    for l in range(2):
        low_in = hidden.astype(BF)
        if l == 1:
            xall[1, x_lo, core] = low_in
            near_way, far_way = share(1)
            gather.swap_arrive(1, 0)
        r["q"][l] = (mm(low_in, attn_weight(l, 0)) + row(l, 0)).astype(BF)
        if l == 1:
            near_way.wait_recv()
        chip_keys(l, x_lo)
        if l == 1:
            on_way = pass_on(1, far_way)
            gather.swap_start(1, 1)
            on_way.wait_recv()
        chip_keys(l, 1 - x_lo)
        pairs[l, 0] = xall[l, x_lo]
        for pair in range(4):
            low = 128 * pair
            scores = mm(both(r["q"][l, :, low : low + 128]), group_rows(l, 0, low), NT) * SCALE
            bias = r["bias"][...]
            scores = scores + jnp.concatenate([bias, bias], axis=0)
            powers = jnp.exp(scores - jnp.max(scores, axis=-1, keepdims=True))
            probs = (powers * (1.0 / jnp.sum(powers, axis=-1, keepdims=True))).astype(BF)
            r["probs"][l, pair] = probs
            pairs[l, 1, core, :, low : low + 128] = joined(mm(probs, group_rows(l, 1, low))).astype(BF)
            if l == 0 and pair == 1:
                gather.swap_start(0, 1)
        send(pairs.at[l, 1, core], pairs.at[l, 1, core], "act", (l, 1), near)
        if l == 0:
            gather.swap_arrive(0, 1)
        hat, inverse = normalize(hidden + mm(pairs[l, 1, core], attn_weight(l, 3)) + row(l, 2))
        r["hat1"][l] = hat
        r["inv1"][l] = inverse
        normed = hat * row(l, 3) + row(l, 4)
        low_normed = normed.astype(BF)
        pairs[l, 2, core] = low_normed
        send(pairs.at[l, 2, core], pairs.at[l, 2, core], "act", (l, 2), near)
        back = jnp.zeros((128, 512), F32)
        if l == 1:
            gather.swap_arrive(1, 1)
        for i in range(4):
            half, low = i // 2, 512 * (i % 2)
            pre = mm(low_normed, weight(l, 1, half, low, low + 512)) + row(l, 5 + i)
            normal = 0.5 + 0.5 * lax.erf(pre * (0.5**0.5))
            act = (pre * normal).astype(BF)
            r["act"][l, half, core, :, low : low + 512] = act
            slope = normal + pre * (jnp.exp(pre * pre * -0.5) * (1.0 / (2.0 * math.pi) ** 0.5))
            r["slope"][l, :, 512 * i : 512 * i + 512] = slope.astype(BF)
            back = back + mm(act, weight(l, 1, 2 + half, low, low + 512), NT)
        mine = r["act"].at[l, peer, core]
        send(mine, mine, "act", (l, 3), near)
        if l == 0:
            gather.swap_start(1, 0)
        hat, inverse = normalize(normed + back + row(l, 9))
        r["hat2"][l] = hat
        r["inv2"][l] = inverse
        hidden = hat * row(l, 10) + row(l, 11)
    r["block_out"][...] = hidden.astype(BF)

    scatter = Scatter(place, (ga, gm), slots, r["total"], r["rs_send"], r["rs_recv"])
    dx, dx_near, dx_far, late, early = r["dx"], r["dx_near"], r["dx_far"], r["late"], r["early"]

    def grad_rows(l, chip):
        keys, values = late[l, 0, core, chip].reshape(256, 512), late[l, 1, core, chip].reshape(256, 512)
        part = mm(keys, attn_weight(l, 1), NT) + mm(values, attn_weight(l, 2), NT)
        dx[l, chip] = part.astype(BF).reshape(2, 128, 512)
        return send(dx.at[l, chip, peer], dx_near.at[l, chip], "dx", (l, (chip + x_lo) % 2), near)

    def give_far(l, copy):
        copy.wait_recv()
        mine = dx[l, 1 - x_lo, core].astype(F32) + dx_near[l, 1 - x_lo].astype(F32)
        dx[l, 1 - x_lo, core] = mine.astype(BF)
        return send(dx.at[l, 1 - x_lo, core], dx_far.at[l], "dx", (l, 2), across)

    def act_arrive(l, which):
        if which == 3:
            ref = r["act"].at[l, core, peer]
        else:
            ref = pairs.at[l, which, peer]
        remote(ref, ref, r["act_send"].at[l, which], r["act_recv"].at[l, which], near).wait_recv()

    def two(ref, *index):
        return ref[index].reshape(256, -1)

    def mlp_grads(l, got_second):
        got_second.wait_recv()
        act_arrive(l, 3)
        put_grad(l, 1, 1, two(pairs, l, 3), lambda low, high: r["act"][l, core, :, :, low:high].reshape(256, -1), 2)
        act_arrive(l, 2)
        theirs = r["du"].at[l, core, peer]
        remote(theirs, theirs, r["back_send"].at[l, 1], r["back_recv"].at[l, 1], near).wait_recv()
        put_grad(l, 1, 0, two(pairs, l, 2), lambda low, high: r["du"][l, core, :, :, low:high].reshape(256, -1), 2)
        scatter.step(l, 1, 0)

    s4, fin, total = r["s4"], r["fin"], r["total"]
    moved = []

    def hand_out(l):
        for dst in range(4):
            s4[dst, l] = total[l, 4 * dst : 4 * dst + 4, :]
        for step in (1, 2, 3):
            member, device = place.in_group(step)
            moved.append(send(s4.at[member, l], fin.at[seq, l], "a2a", (l, step), device))
        fin[seq, l] = s4[seq, l]

    grad = r["cotangent"][...].astype(F32)
    for l in (1, 0):
        hat = r["hat2"][l]
        put_row(l, 10, column_sum(grad * hat))
        put_row(l, 11, column_sum(grad))
        grad_second = normalize_back(grad * row(l, 10), hat, r["inv2"][l])
        put_row(l, 9, column_sum(grad_second))
        low_second = grad_second.astype(BF)
        pairs[l, 3, core] = low_second
        got_second = send(pairs.at[l, 3, core], pairs.at[l, 3, core], "back", (l, 0), near)
        grad_normed = grad_second
        for i in range(4):
            half, low = i // 2, 512 * (i % 2)
            grad_act = mm(low_second, weight(l, 1, 2 + half, low, low + 512))
            grad_pre = (grad_act * r["slope"][l, :, 512 * i : 512 * i + 512].astype(F32)).astype(BF)
            put_row(l, 5 + i, column_sum(grad_pre.astype(F32)))
            r["du"][l, half, core, :, low : low + 512] = grad_pre
            grad_normed = grad_normed + mm(grad_pre, weight(l, 1, half, low, low + 512), NT)
            if l == 0 and i == 1:
                scatter.step(1, 1, 1)
        mine = r["du"].at[l, peer, core]
        send(mine, mine, "back", (l, 1), near)
        mlp_grads(l, got_second)
        hat = r["hat1"][l]
        put_row(l, 3, column_sum(grad_normed * hat))
        put_row(l, 4, column_sum(grad_normed))
        grad_first = normalize_back(grad_normed * row(l, 3), hat, r["inv1"][l])
        put_row(l, 2, column_sum(grad_first))
        low_first = grad_first.astype(BF)
        early[l, 1, core] = low_first
        grad_mixed = mm(low_first, attn_weight(l, 3), NT).astype(BF)
        for pair in range(4):
            low = 128 * pair
            keys, values = group_rows(l, 0, low), group_rows(l, 1, low)
            grad_pair = both(grad_mixed[:, low : low + 128])
            probs = r["probs"][l, pair]
            grad_probs = mm(grad_pair, values, NT)
            late[l, 1, core, :, :, low : low + 128] = mm(probs, grad_pair, TN).astype(BF).reshape(2, 256, 128)
            wide = probs.astype(F32)
            row_dot = jnp.sum(grad_probs * wide, axis=-1, keepdims=True)
            grad_scores = (wide * (grad_probs - row_dot)).astype(BF)
            early[l, 0, core, :, low : low + 128] = (joined(mm(grad_scores, keys)) * SCALE).astype(BF)
            grad_keys = mm(grad_scores, both(r["q"][l, :, low : low + 128]), TN) * SCALE
            late[l, 0, core, :, :, low : low + 128] = grad_keys.astype(BF).reshape(2, 256, 128)
            if l == 0 and pair == 1:
                scatter.step(1, 0, 1)
        mine = late.at[l, peer, core]
        send(mine, mine, "back", (l, 3), near)
        mine = early.at[l, peer, core]
        send(mine, mine, "back", (l, 2), near)
        grad_queries = early[l, 0, core]
        put_row(l, 0, column_sum(grad_queries.astype(F32)))
        put_row(l, 1, column_sum(late[l, 1, core].reshape(512, 512).astype(F32)))
        if l == 0:
            for y in range(4):
                r["vtab"][y] = vgrad[:, 128 * y : 128 * y + 128]
            table = Table(place, r["vtab"], r["vgot"].at[1], r["v_send"].at[1], r["v_recv"].at[1])
            table.start("y", "collect")

        def attn_grads():
            act_arrive(l, 1)
            theirs = early.at[l, core, peer]
            remote(theirs, theirs, r["back_send"].at[l, 2], r["back_recv"].at[l, 2], near).wait_recv()
            put_grad(l, 0, 0, two(pairs, l, core), lambda low, high: two(early, l, core), 1)
            theirs = late.at[l, core, peer]
            remote(theirs, theirs, r["back_send"].at[l, 3], r["back_recv"].at[l, 3], near).wait_recv()
            rows = xall[l].reshape(512, 512)
            value = mm(rows, late[l, core, 0].reshape(512, 512), TN) + mm(rows, late[l, core, 1].reshape(512, 512), TN)
            ga[l, 1] = value.astype(BF).reshape(4, 2, 4, 16, 512)
            scatter.step(l, 0, 0)

        if l == 0:
            attn_grads()
        far_near = grad_rows(l, 1 - x_lo)
        own_near = grad_rows(l, x_lo)
        far_way = give_far(l, far_near)
        grad = grad_first + mm(grad_queries, attn_weight(l, 0), NT)
        if l == 1:
            attn_grads()
        else:
            scatter.step(1, 1, 2)
            scatter.step(1, 0, 2)
            table.finish()
            table.start("x")
            scatter.step(1, 1, 3)
            scatter.step(1, 0, 3)
            hand_out(1)
            scatter.step(0, 1, 1)
        own_near.wait_recv()
        far_way.wait_recv()
        grad = grad + dx[l, x_lo, core].astype(F32) + dx_near[l, x_lo].astype(F32) + dx_far[l].astype(F32)
    r["input_grad"][...] = grad
    scatter.step(0, 0, 1)
    table.finish()
    table.start("z")
    scatter.step(0, 1, 2)
    scatter.step(0, 0, 2)
    table.finish()
    table.start("core")
    scatter.step(0, 1, 3)
    scatter.step(0, 0, 3)
    hand_out(0)
    table.finish()
    r["vtab"][place.at["y"]] = pltpu.roll(r["vtab"][place.at["y"]], (128 - 4 * (number % 32)) % 128, 1)
    for l in range(2):
        square[0:12, :] = r["vtab"][place.at["y"], 12 * l : 12 * l + 12, :]
        r["vfin"][l] = square[...].T[0:8, :]
    gather.finish()
    scatter.finish()
    for copy in moved:
        copy.wait_recv()
    for copy in unsent:
        copy.wait_send()


INPUTS = ("tokens", "cotangent", "segments", "w_attn", "w_mlp", "vectors")
OUTPUTS = {
    "block_out": ((128, 512), BF),
    "input_grad": ((128, 512), F32),
    "fin": ((4, 2, 4, 1536), F32),
    "vfin": ((2, 8, 128), F32),
}
DIMS = (2, 2, 2, 4, 2, 4, 16)
HALF = (2, 2, 4, 2, 4, 16)
SCRATCH = {
    "wa": (DIMS + (512,), BF),
    "wm": (DIMS + (1024,), BF),
    "ga": (HALF + (512,), BF),
    "gm": (HALF + (1024,), BF),
    "vec": ((24, 512), F32),
    "vgrad": ((24, 512), F32),
    "tab": ((4, 24, 128), F32),
    "vtab": ((4, 24, 128), F32),
    "t0": ((4, 16, 768), F32),
    "square": ((128, 128), F32),
    "s0": ((4, 16, 768), BF),
    "r0": ((4, 16, 768), BF),
    "s4": ((4, 2, 4, 1536), F32),
    "stage": ((2, 16, 1536), F32),
    "total": ((2, 16, 1536), F32),
    "vgot": ((2, 4, 3, 24, 128), F32),
    "docs": ((4, 1, 128), jnp.int32),
    "bias": ((128, 512), F32),
    "q": ((2, 128, 512), BF),
    "kv": ((2, 2, 2, 256, 512), BF),
    "xall": ((2, 2, 2, 128, 512), BF),
    "probs": ((2, 4, 256, 512), BF),
    "pairs": ((2, 4, 2, 128, 512), BF),
    "act": ((2, 2, 2, 128, 1024), BF),
    "du": ((2, 2, 2, 128, 1024), BF),
    "early": ((2, 2, 2, 128, 512), BF),
    "late": ((2, 2, 2, 2, 256, 512), BF),
    "hat1": ((2, 128, 512), F32),
    "inv1": ((2, 128, 1), F32),
    "slope": ((2, 128, 2048), BF),
    "hat2": ((2, 128, 512), F32),
    "inv2": ((2, 128, 1), F32),
    "dx": ((2, 2, 2, 128, 512), BF),
    "dx_near": ((2, 2, 128, 512), BF),
    "dx_far": ((2, 128, 512), BF),
}
SEMS = {
    "a2a": (3, 4),
    "doc": (4,),
    "ag": (2, 2, 3, 3, 3),
    "sw": (2, 2, 3, 4),
    "rs": (2, 2, 3, 3, 3),
    "x": (2, 3),
    "dx": (2, 3),
    "act": (2, 4),
    "back": (2, 4),
    "v": (2, 4, 3),
}
NAMES = INPUTS + tuple(OUTPUTS) + tuple(SCRATCH) + tuple(f"{n}_{d}" for n in SEMS for d in ("send", "recv"))


def train(*args):
    slots = []
    for l in range(2):
        for phase in range(3):
            for arr in range(2):
                for j in range(3):
                    low, high = THIRDS[l][arr][j]
                    rest = dims_of(ORDERS[j][::-1][phase + 1 :])
                    slots.append(pltpu.VMEM((3,) + rest + (16, high - low), BF))
    scratch = [pltpu.VMEM(*spec) for spec in SCRATCH.values()]
    for shape in SEMS.values():
        scratch += [pltpu.SemaphoreType.DMA(shape)] * 2
    return pl.pallas_call(
        train_kernel,
        out_shape=tuple(jax.ShapeDtypeStruct(*spec) for spec in OUTPUTS.values()),
        in_specs=[pl.BlockSpec(memory_space=pltpu.VMEM)] * len(INPUTS),
        out_specs=[pl.BlockSpec(memory_space=pltpu.VMEM)] * len(OUTPUTS),
        scratch_shapes=scratch + slots,
        compiler_params=pltpu.CompilerParams(
            collective_id=0, has_side_effects=True, vmem_limit_bytes=VMEM_BYTES
        ),
        name="train",
    )(*args)


def adam_update(weight, grad, first, second, rate, decay):
    first_new = BETA_FIRST * first + (1.0 - BETA_FIRST) * grad
    second_new = BETA_SECOND * second + (1.0 - BETA_SECOND) * grad * grad
    first_fix = 1.0 - BETA_FIRST**STEP
    second_fix = 1.0 - BETA_SECOND**STEP
    weight_new = weight - rate * (
        first_new / first_fix / (jnp.sqrt(second_new / second_fix) + ADAM_EPSILON) + decay * weight
    )
    return (first_new, second_new, weight_new)


def adam_kernel(block_in, grad_in, fin, vfin, *refs):
    state, (block_out, grad_out), outs = refs[:9], refs[9:11], refs[11:]
    block_out[...] = block_in[...]
    grad_out[...] = grad_in[...]
    for l in range(2):
        for arr in range(3):
            w, m, v = state[arr], state[3 + arr], state[6 + arr]
            if arr == 2:
                pieces = [(vfin[l, 0:4, 0:12], slice(0, 12))]
            elif arr == 1:
                pieces = [(fin[s, l, :, 512:1536], slice(1024 * s, 1024 * s + 1024)) for s in range(4)]
            else:
                pieces = [(fin[s, l, :, 0:512], slice(512 * q, 512 * q + 512)) for s, q in enumerate(QUARTERS)]
            rate, decay = (VECTOR_RATE, 0.0) if arr == 2 else (LEARN_RATE, WEIGHT_DECAY)
            for grad, span in pieces:
                new = adam_update(w[l, :, span], grad, m[l, :, span], v[l, :, span], rate, decay)
                for k in range(3):
                    outs[3 * arr + k][l, :, span] = new[k]


def adam(block, grad, fin, vfin, *state):
    shapes = [jax.ShapeDtypeStruct(a.shape, a.dtype) for a in (block, grad)]
    for a in state[:3]:
        shapes += [jax.ShapeDtypeStruct(a.shape, a.dtype)] * 3
    spec = pl.BlockSpec(memory_space=pltpu.VMEM)
    return pl.pallas_call(
        adam_kernel, out_shape=shapes, in_specs=[spec] * 13, out_specs=[spec] * 11, name="adam"
    )(block, grad, fin, vfin, *state)


def local(
    tokens, cotangent, segments, w_attn, w_mlp, vectors, m_attn, m_mlp, m_vec, v_attn, v_mlp, v_vec
):
    vectors, m_vec, v_vec = (a.transpose(0, 2, 1) for a in (vectors, m_vec, v_vec))
    made = train(tokens[0], cotangent[0], segments, w_attn, w_mlp, vectors)
    block_out, input_grad, *updated = adam(
        *made, w_attn, w_mlp, vectors, m_attn, m_mlp, m_vec, v_attn, v_mlp, v_vec
    )
    return (block_out[None], input_grad[None], *updated[:6], *(a.transpose(0, 2, 1) for a in updated[6:]))


def solution(mesh):
    in_specs = (
        P("dp", "seq", None),
        P("dp", "seq", None),
        P("dp", "seq"),
        P(None, ("dp", "seq"), None),
        P(None, ("dp", "seq"), None),
        P(None, None, ("dp", "seq")),
        P(None, ("dp", "seq"), None),
        P(None, ("dp", "seq"), None),
        P(None, None, ("dp", "seq")),
        P(None, ("dp", "seq"), None),
        P(None, ("dp", "seq"), None),
        P(None, None, ("dp", "seq")),
    )
    out_specs = (
        P("dp", "seq", None),
        P("dp", "seq", None),
        P(None, ("dp", "seq"), None),
        P(None, ("dp", "seq"), None),
        P(None, ("dp", "seq"), None),
        P(None, ("dp", "seq"), None),
        P(None, ("dp", "seq"), None),
        P(None, ("dp", "seq"), None),
        P(None, None, ("dp", "seq")),
        P(None, None, ("dp", "seq")),
        P(None, None, ("dp", "seq")),
    )
    return jax.shard_map(local, mesh=mesh, in_specs=in_specs, out_specs=out_specs, check_vma=False)
```
